512 devices in a mesh: rp: 32 (over z, x_hi, core), re: 16 (over y, x_lo).
Axes of the slice: x: 4 (x_hi: 2, x_lo: 2; x = x_hi * 2 + x_lo), y: 8, z: 8, core: 2. Of those that a mesh axis runs over, the one named last changes fastest.
Arguments:
- wannier_coupling: bfloat16 [64, 128, 6400], P('re', 'rp'), may hold values from -0.0029296875 to 0.0029296875
- phonon_lattice: int32 [128, 3], P('rp'), may hold values from -6 to 6
- phonon_degeneracy: int32 [128], P('rp'), may hold values from 1 to 4
- electron_lattice: int32 [64, 3], replicated, may hold values from -6 to 6
- electron_degeneracy: int32 [64], replicated, may hold values from 1 to 6
- phonon_wavevectors: float32 [32, 3], replicated, may hold values from -0.5 to 0.5
- electron_wavevectors: float32 [256, 3], P('re'), may hold values from -0.5 to 0.5
- phonon_energies: float32 [32, 2], P('rp'), may hold values from 0.02 to 0.2
- bloch_rotations: float32 [256, 3200], P('re'), may hold values from -0.625 to 0.625
- band_energies: float32 [256, 40], P('re'), may hold values from -1.75 to 1.75
- shifted_points: int32 [32, 256], P('rp'), may hold values from 0 to 255, as said below
Outputs:
- linewidth: float32 [256, 40], P('re')
The draws below stay inside these ranges and needn't reach their ends.
Inputs may be any that keep to these rules, and one draw needn't show every extreme that they name: `shifted_points`: row q gives, for every fine k-point k, the index of the fine k-point k+q, and is a permutation of the 256 points. Cut the points into blocks of 16 consecutive indices: for every q, the k+q points of one block lie in exactly 8 distinct blocks, exactly 2 in each.
All inputs are finite; a program needn't handle non-finite values.
Results may differ from the reference program's by a relative error of at most 0.0011.
Values may be sent and summed in bfloat16 or wider, within the bound.
A program may use at most 64 MiB of HBM per device.

```python
import math
import jax
import jax.numpy as jnp
from jax import lax

NW = 40
MODES = 2
K_DEV = 16
NRE = 64
NRP = 128
NK = 256
NQ = 32
FLAT = 6400
UFLAT = 3200
CAP = 2


def draw_shifted_points(key, part):
    key = jax.random.fold_in(key, 7)
    blocks = NK // K_DEV

    def one_row(row_key):
        order_key, shift_key, place_key = jax.random.split(row_key, 3)
        groups = jax.random.permutation(order_key, K_DEV) // CAP
        shifts = jax.random.permutation(shift_key, blocks)
        places = jax.random.permutation(place_key, K_DEV)
        source = (jnp.arange(blocks)[:, None] + shifts[groups][None, :]) % blocks
        return (source * K_DEV + places[None, :]).reshape(NK).astype(jnp.int32)
    return jax.vmap(one_row)(jax.random.split(key, NQ))


def plant(array, stream_key, smallest, high):
    dims = array.shape
    spot = [jax.random.randint(jax.random.fold_in(stream_key, axis), (), 0, dims[axis]) for axis in range(len(dims))]
    array = array.at[tuple(spot)].set(smallest)
    longest = dims.index(max(dims))
    spot[longest] = (spot[longest] + 1) % dims[longest]
    return array.at[tuple(spot)].set(high)


def block_levels(rng, dims, pieces, low, largest):
    gain = 1.0
    for position, parts in pieces:
        heights = jax.random.uniform(jax.random.fold_in(jax.random.fold_in(rng, 6), position), (parts,), jnp.float32, low / len(pieces), largest / len(pieces))
        gain = gain * jnp.repeat(jnp.exp(heights), dims[position] // parts).reshape((-1,) + (1,) * (len(dims) - 1 - position))
    return gain


def normal_values(rng, dims, deviation, reach, cuts=(), dtype=jnp.bfloat16):
    entries = deviation * jax.random.normal(rng, dims, jnp.float32)
    if cuts:
        entries = entries * block_levels(rng, dims, cuts, -0.22, 0.18)
    return jnp.clip(entries, -reach, reach).astype(dtype)


def setup_inputs(seed: int = 0) -> dict:
    streams_of = jax.random.split(jax.random.key(seed), 12)
    return {
        "wannier_coupling": normal_values(streams_of[0], (NRE, NRP, FLAT), (600 * NRE * NRP) ** -0.5, 0.0029296875, ((0, 16), (1, 32))),
        "phonon_lattice": plant(jax.random.randint(streams_of[1], (NRP, 3), -6, 7), jax.random.fold_in(streams_of[1], 1), -6, 6).astype(jnp.int32),
        "phonon_degeneracy": plant(jax.random.randint(streams_of[2], (NRP,), 1, 5), jax.random.fold_in(streams_of[2], 1), 1, 4).astype(jnp.int32),
        "electron_lattice": plant(jax.random.randint(streams_of[3], (NRE, 3), -6, 7), jax.random.fold_in(streams_of[3], 1), -6, 6).astype(jnp.int32),
        "electron_degeneracy": plant(jax.random.randint(streams_of[4], (NRE,), 1, 7), jax.random.fold_in(streams_of[4], 1), 1, 6).astype(jnp.int32),
        "phonon_wavevectors": jnp.clip(jax.random.uniform(streams_of[5], (NQ, 3), jnp.float32, -0.5, 0.5), -0.5, 0.5),
        "electron_wavevectors": jnp.clip(jax.random.uniform(streams_of[6], (NK, 3), jnp.float32, -0.5, 0.5) * block_levels(streams_of[6], (NK, 3), ((0, 16),), -0.4, 0.0), -0.5, 0.5),
        "phonon_energies": jnp.clip(jnp.exp(math.log(0.2) - 2.3025851 * jax.random.uniform(streams_of[7], (NQ, MODES), jnp.float32) ** block_levels(streams_of[7], (NQ, MODES), ((0, 32),), -0.2, 0.2)), 0.02, 0.2),
        "bloch_rotations": normal_values(streams_of[8], (NK, UFLAT), (2 * NW) ** -0.5, 0.625, ((0, 16),), jnp.float32),
        "band_energies": normal_values(streams_of[9], (NK, NW), 0.3, 1.75, ((0, 16),), jnp.float32),
        "shifted_points": draw_shifted_points(jax.random.fold_in(streams_of[11], 71), 0),
    }


full_turn = 2.0 * math.pi
thermal = 0.025
broadening = 0.05
highest = lax.Precision.HIGHEST


def phase_tables(points, lattice, degeneracy):
    angles = full_turn * jnp.dot(points, lattice.astype(jnp.float32).T, precision=highest)
    weights = 1.0 / degeneracy.astype(jnp.float32)
    return (jnp.cos(angles) * weights).astype(jnp.bfloat16), (jnp.sin(angles) * weights).astype(jnp.bfloat16)


def quarter_turn(flat_data):
    shaped = flat_data.reshape(flat_data.shape[:-1] + (MODES, 2, -1))
    turned = jnp.stack([-shaped[..., 1, :], shaped[..., 0, :]], axis=-2)
    return turned.reshape(flat_data.shape)


def lorentzian(offset):
    return (broadening / math.pi) / (offset * offset + broadening * broadening)


def coupling_strength(coupling, here_rotation, there_rotation):
    points = coupling.shape[0]
    shaped = coupling.reshape(points, MODES, 2, NW, NW)
    here_matrix = here_rotation.reshape(points, 2, NW, NW)
    there_matrix = there_rotation.reshape(points, 2, NW, NW)
    matrix_real = shaped[:, :, 0]
    matrix_imag = shaped[:, :, 1]
    right_real = here_matrix[:, 0]
    right_imag = here_matrix[:, 1]
    left_real = there_matrix[:, 0]
    left_imag = there_matrix[:, 1]
    mixed_real = jnp.einsum('kmab,kbn->kman', matrix_real, right_real, precision=highest) - jnp.einsum('kmab,kbn->kman', matrix_imag, right_imag, precision=highest)
    mixed_imag = jnp.einsum('kmab,kbn->kman', matrix_real, right_imag, precision=highest) + jnp.einsum('kmab,kbn->kman', matrix_imag, right_real, precision=highest)
    final_real = jnp.einsum('kap,kman->kmpn', left_real, mixed_real, precision=highest) + jnp.einsum('kap,kman->kmpn', left_imag, mixed_imag, precision=highest)
    final_imag = jnp.einsum('kap,kman->kmpn', left_real, mixed_imag, precision=highest) - jnp.einsum('kap,kman->kmpn', left_imag, mixed_real, precision=highest)
    return final_real * final_real + final_imag * final_imag


def scattering(strength, mode_energy, here_energy, there_energy):
    bose_factor = 1.0 / jnp.expm1(mode_energy / thermal)
    fermi_factor = jax.nn.sigmoid(-there_energy / thermal)
    phonon = mode_energy[None, :, None, None]
    occupied = bose_factor[None, :, None, None]
    filling = fermi_factor[:, None, :, None]
    spacing = here_energy[:, None, None, :] - there_energy[:, None, :, None]
    absorbed = (occupied + filling) * lorentzian(spacing + phonon)
    emitted = (occupied + 1.0 - filling) * lorentzian(spacing - phonon)
    return jnp.sum(strength / (2.0 * phonon) * (absorbed + emitted), axis=(1, 2))


def reference(wannier_coupling, phonon_lattice, phonon_degeneracy, electron_lattice, electron_degeneracy, phonon_wavevectors, electron_wavevectors, phonon_energies, bloch_rotations, band_energies, shifted_points):
    cosine_waves, sine_waves = phase_tables(phonon_wavevectors, phonon_lattice, phonon_degeneracy)

    def per_cell(cell_coupling):
        turned = quarter_turn(cell_coupling)
        summed = jnp.dot(cosine_waves, cell_coupling, preferred_element_type=jnp.float32) + jnp.dot(sine_waves, turned, preferred_element_type=jnp.float32)
        return summed.astype(jnp.bfloat16)

    coupling_waves = lax.map(per_cell, wannier_coupling)
    cosine_points, sine_points = phase_tables(electron_wavevectors, electron_lattice, electron_degeneracy)

    def per_wave(inputs):
        coupling_cells, mode_energy, targets = inputs
        turned = quarter_turn(coupling_cells)
        coupling_points = jnp.dot(cosine_points, coupling_cells, preferred_element_type=jnp.float32) + jnp.dot(sine_points, turned, preferred_element_type=jnp.float32)
        there_rotation = jnp.take(bloch_rotations, targets, axis=0)
        there_energy = jnp.take(band_energies, targets, axis=0)
        strength = coupling_strength(coupling_points, bloch_rotations, there_rotation)
        return scattering(strength, mode_energy, band_energies, there_energy)

    partial_sums = lax.map(per_wave, (jnp.swapaxes(coupling_waves, 0, 1), phonon_energies, shifted_points))
    return jnp.sum(partial_sums, axis=0) * (math.pi / NQ)
```

```python
import math

import jax
import jax.numpy as jnp
from jax import lax
from jax.experimental import pallas as pl
from jax.experimental.pallas import tpu as pltpu
from jax.sharding import PartitionSpec as P

NW = 40
MODES = 2
ROW = 1600
LANES = 1664
PACK = 512
MESH = pl.DeviceIdType.MESH
BF = jnp.bfloat16
F32 = jnp.float32

full_turn = 2.0 * math.pi
thermal = 0.025
broadening = 0.05
highest = lax.Precision.HIGHEST


def phase_tables(points, lattice, degeneracy):
    angles = full_turn * jnp.dot(points, lattice.astype(F32).T, precision=highest)
    weights = 1.0 / degeneracy.astype(F32)
    return (jnp.cos(angles) * weights).astype(BF), (jnp.sin(angles) * weights).astype(BF)


def three_parts(values):
    high = lax.reduce_precision(values, 8, 7)
    rest = values - high
    middle = lax.reduce_precision(rest, 8, 7)
    return high.astype(BF), middle.astype(BF), (rest - middle).astype(BF)


def iota(shape, axis):
    return lax.broadcasted_iota(jnp.int32, shape, axis)


def mm(left, right):
    return jnp.dot(left, right, preferred_element_type=F32)


def mm_first(left, right):
    return lax.dot_general(left, right, (((0,), (0,)), ((), ())), preferred_element_type=F32)


LANE_TILES = [(start, min(start + 256, LANES)) for start in range(0, LANES, 256)]


def kernel(
    w_ref,
    cosw_ref,
    sinw_ref,
    pack_ref,
    points_ref,
    phonon_ref,
    out_ref,
    w_sib,
    lhs_own,
    lhs_out,
    lhs_sib,
    packs,
    u_out,
    u_in,
    part,
    send_up,
    send_down,
    land_up,
    land_down,
    total,
    land_x,
    waves,
    mix,
    left_rot,
    right_rot,
    energy_col,
    energy_row,
    weight,
    coupling,
    rates,
    land_z,
    rates_z,
    land_c,
    core_s,
    core_r,
    pack_s,
    pack_r,
    u_s,
    u_r,
    up_s,
    up_r,
    down_s,
    down_r,
    x_s,
    x_r,
    yup_s,
    yup_r,
    ydown_s,
    ydown_r,
    rz_s,
    rz_r,
    rc_s,
    rc_r,
):
    rp = lax.axis_index("rp")
    re = lax.axis_index("re")
    z = rp // 4
    x_hi = (rp // 2) % 2
    core = rp % 2
    y = re // 2
    x_lo = re % 2

    def flip_rp(dx, dc):
        row = z * 4
        hi = (1 - x_hi) if dx else x_hi
        co = (1 - core) if dc else core
        return row + hi * 2 + co

    def flip_re(dl):
        return y * 2 + ((1 - x_lo) if dl else x_lo)

    def remote(src, dst, send, recv, to_rp, to_re):
        return pltpu.make_async_remote_copy(
            src_ref=src,
            dst_ref=dst,
            send_sem=send,
            recv_sem=recv,
            device_id={"rp": to_rp, "re": to_re},
            device_id_type=MESH,
        )

    partners = [(rp, (re + step) % 16) for step in range(1, 16)]
    partners += [((rp + 4 * step) % 32, re) for step in range(1, 8)]
    partners += [
        (flip_rp(dx, dc), flip_re(dl))
        for dx in (0, 1)
        for dc in (0, 1)
        for dl in (0, 1)
        if dx or dc
    ]
    barrier = pltpu.get_barrier_semaphore()
    for to_rp, to_re in partners:
        pl.semaphore_signal(
            barrier, inc=1, device_id={"rp": to_rp, "re": to_re}, device_id_type=MESH
        )

    row = iota((256, 128), 0)
    lane = iota((256, 128), 1)
    same = ((row >> 3) & 1 == (lane >> 5) & 1) & (row & 3 == (lane >> 2) & 3) & (lane < 64)
    to_imag = (row >> 2) & 1
    of_imag = (lane >> 4) & 1
    pick_cos = same & (to_imag == of_imag)
    pick_sin = same & (to_imag != of_imag)
    sign = jnp.where(to_imag == 1, 1.0, -1.0).astype(F32)
    q_row = iota((256, 32), 0)
    q_lane = iota((256, 32), 1)

    def phases_for(which_core):
        spread = jnp.where((q_row >> 4) * 2 + which_core == q_lane, 1.0, 0.0).astype(BF)
        cos_part = mm(spread, cosw_ref[...])
        sin_part = mm(spread, sinw_ref[...])
        return jnp.where(
            pick_cos, cos_part, jnp.where(pick_sin, sign * sin_part, 0.0)
        ).astype(BF)

    lhs_out[...] = phases_for(1 - core)

    points = points_ref[...]
    mine = (points >> 4) == re
    inner = points & 15
    smaller = jnp.min(jnp.where(mine, inner, 99), axis=1, keepdims=True)
    larger = jnp.max(jnp.where(mine, inner, -1), axis=1, keepdims=True)
    both = jnp.where(iota((16, 128), 1) == 0, smaller, larger).astype(F32).astype(BF)
    spread16 = jnp.where((iota((256, 16), 0) >> 4) == iota((256, 16), 1), 1.0, 0.0).astype(BF)
    both_rows = mm(spread16, both)
    slot = (iota((256, 1), 0) >> 3) & 1
    chosen = jnp.where(slot == 0, both_rows[:, 0:1], both_rows[:, 1:2])
    take = ((lane >> 3).astype(F32) == chosen) & ((lane & 7) == (row & 7))
    take = jnp.where(take, 1.0, 0.0).astype(BF)
    taken = mm(take, pack_ref[0:128, :]).astype(BF)
    u_out[...] = taken.reshape(8, 2, 16, PACK)

    pl.semaphore_wait(barrier, len(partners))

    sib = flip_rp(0, 1)
    core_copies = [
        remote(w_ref, w_sib, core_s.at[0], core_r.at[0], sib, re),
        remote(lhs_out, lhs_sib, core_s.at[1], core_r.at[1], sib, re),
    ]
    for copy in core_copies:
        copy.start()
    pack_copy = remote(pack_ref, packs.at[x_lo], pack_s, pack_r, rp, flip_re(1))
    pack_copy.start()
    u_copies = []
    for step in range(1, 16):
        to = (re + step) % 16
        copy = remote(
            u_out.at[to // 2], u_in.at[re], u_s.at[step], u_r.at[step], rp, to
        )
        copy.start()
        u_copies.append(copy)
    packs[x_lo] = pack_ref[...]
    u_in[re] = u_out[y]

    lhs_own[...] = phases_for(core)
    for start, end in LANE_TILES:
        part[:, start:end] = mm(lhs_own[:, 0:64], w_ref[:, start:end])
    for copy in core_copies:
        copy.wait_recv()
    for start, end in LANE_TILES:
        part[:, start:end] += mm(lhs_sib[:, 0:64], w_sib[:, start:end])

    above = (rp + 4) % 32
    below = (rp + 28) % 32

    def part_of(z_to, sub):
        hi = (1 - x_hi) if sub == 0 else x_hi
        block = (z_to % 8) * 2 + hi
        return part[pl.ds(pl.multiple_of(block * 16, 16), 16), :]

    sends = []

    def go_up(hop, sub):
        copy = remote(
            send_up.at[hop, sub],
            land_up.at[hop, sub],
            up_s.at[hop, sub],
            up_r.at[hop, sub],
            above,
            re,
        )
        copy.start()
        sends.append(copy)
        return copy

    def go_down(hop, sub):
        copy = remote(
            send_down.at[hop, sub],
            land_down.at[hop, sub],
            down_s.at[hop, sub],
            down_r.at[hop, sub],
            below,
            re,
        )
        copy.start()
        sends.append(copy)
        return copy

    ups = {}
    downs = {}
    for sub in (0, 1):
        send_up[0, sub] = part_of(z + 4, sub).astype(BF)
        ups[0, sub] = go_up(0, sub)
        send_down[0, sub] = part_of(z + 5, sub).astype(BF)
        downs[0, sub] = go_down(0, sub)

    def rotations_here():
        pack_copy.wait_recv()
        for b in (0, 1):
            rows = packs[b, 0:128, :].astype(F32)
            relayout(rows, right_rot, b, True)
            tail = packs[b, 128:144, :].astype(F32)
            energy_row[b * 16 : b * 16 + 16, :] = (
                tail[:, 128:256] + tail[:, 256:384] + tail[:, 384:512]
            )

    def relayout(rows, target, b, signed):
        swapped = jnp.concatenate(
            [rows.reshape(16, 8, PACK)[:, 4:8], rows.reshape(16, 8, PACK)[:, 0:4]], axis=1
        ).reshape(128, PACK)
        if signed:
            flip = jnp.where((iota((128, 1), 0) >> 2) & 1 == 1, -1.0, 1.0)
            rows = rows * flip
        for t in range(10):
            cut = slice(t * 40, t * 40 + 40)
            target[pl.ds(b * 1280 + t, 128, stride=10), :] = jnp.concatenate(
                [rows[:, cut], swapped[:, cut], jnp.zeros((128, 48), F32)], axis=1
            )

    def rotations_there():
        for copy in u_copies:
            copy.wait_recv()
        for b in (0, 1):
            block = points_ref[pl.ds(y * 2 + b, 1), :]
            spot = iota((128, 16), 0) >> 3 == iota((128, 16), 1)
            wide = jnp.broadcast_to(block, (128, 16))
            target = jnp.sum(jnp.where(spot, wide, 0), axis=1, keepdims=True)
            before = ((wide >> 4) == (target >> 4)) & (wide < target)
            second = jnp.max(jnp.where(before, 1, 0), axis=1, keepdims=True)
            source = (target >> 4) * 16 + second * 8 + (iota((128, 1), 0) & 7)
            order = jnp.where(iota((128, 256), 1) == source, 1.0, 0.0).astype(BF)
            rows = mm(order, u_in[:, b].reshape(256, PACK))
            relayout(rows, left_rot, b, False)
            for t in range(5):
                energy = (
                    rows[:, 400 + t : 401 + t]
                    + rows[:, 405 + t : 406 + t]
                    + rows[:, 410 + t : 411 + t]
                )
                energy_col[pl.ds(b * 640 + t, 128, stride=5), :] = jnp.broadcast_to(
                    energy, (128, 128)
                )

    def weights():
        omega = jnp.where(x_lo == 0, phonon_ref[0:1, 0:1], phonon_ref[0:1, 1:2])
        bose = 1.0 / (jnp.exp(omega / thermal) - 1.0)
        scale = (math.pi / 32.0) * (broadening / math.pi) / (2.0 * omega)

        def one(i, carry):
            there = energy_col[pl.ds(pl.multiple_of(i * 40, 8), 40), :]
            here = energy_row[pl.ds(i, 1), :]
            filling = 1.0 / (1.0 + jnp.exp(there / thermal))
            spacing = here - there
            plus = spacing + omega
            minus = spacing - omega
            wide = broadening * broadening
            weight[pl.ds(pl.multiple_of(i * 40, 8), 40), :] = scale * (
                (bose + filling) / (plus * plus + wide)
                + (bose + 1.0 - filling) / (minus * minus + wide)
            )
            return carry

        lax.fori_loop(0, 32, one, 0)

    def electron_phases():
        lane4 = iota((128, 128), 1)
        e_of_lane = ((lane4 >> 4) * 2 + (x_lo + ((lane4 >> 3) & 1)) % 2) * 4 + (lane4 & 3)
        row4 = iota((128, 128), 0)
        match = (row4 & 63) == e_of_lane
        sine = row4 >> 6
        imag = (lane4 >> 2) & 1
        to_real = jnp.where(match & (sine == imag), jnp.where(sine == 1, -1.0, 1.0), 0.0)
        to_im = jnp.where(match & (sine != imag), 1.0, 0.0)
        for b in (0, 1):
            table = packs[b, 128:144, 0:128]
            mix[b * 16 : b * 16 + 16, :] = mm(table, to_real.astype(BF)).astype(BF)
            mix[32 + b * 16 : 48 + b * 16, :] = mm(table, to_im.astype(BF)).astype(BF)

    rotations_here()

    for hop in (1, 2, 3):
        for sub in (0, 1):
            ups[hop - 1, sub].wait_recv()
            send_up[hop, sub] = (
                land_up[hop - 1, sub].astype(F32) + part_of(z + 4 - hop, sub)
            ).astype(BF)
            ups[hop, sub] = go_up(hop, sub)
            if hop < 3:
                downs[hop - 1, sub].wait_recv()
                send_down[hop, sub] = (
                    land_down[hop - 1, sub].astype(F32) + part_of(z + 5 + hop, sub)
                ).astype(BF)
                downs[hop, sub] = go_down(hop, sub)
        if hop == 1:
            electron_phases()
        if hop == 2:
            rotations_there()

    x_copies = {}
    for sub in (0, 1):
        ups[3, sub].wait_recv()
        downs[2, sub].wait_recv()
        done = (
            part_of(z, sub) + land_up[3, sub].astype(F32) + land_down[2, sub].astype(F32)
        )
        total[sub] = done.reshape(2, 8, LANES)
        for dl in (0, 1):
            if sub == 1 and dl == 0:
                continue
            dx = 1 - sub
            copy = remote(
                total.at[sub, (x_lo + dl) % 2],
                land_x.at[dx * 2 + dl],
                x_s.at[dx * 2 + dl],
                x_r.at[dx * 2 + dl],
                flip_rp(dx, 0),
                flip_re(dl),
            )
            copy.start()
            x_copies[dx, dl] = copy
    weights()
    for copy in x_copies.values():
        copy.wait_recv()
    near = total[1, x_lo] + land_x[2]
    far = land_x[1] + land_x[3]
    waves[y] = jnp.concatenate([near, far], axis=0).astype(BF)

    right = (re + 2) % 16
    left = (re + 14) % 16
    y_ups = []
    y_downs = []
    for hop in range(4):
        if hop > 0:
            y_ups[-1].wait_recv()
        block = (y + 8 - hop) % 8
        copy = remote(
            waves.at[block], waves.at[block], yup_s.at[hop], yup_r.at[hop], rp, right
        )
        copy.start()
        y_ups.append(copy)
        if hop < 3:
            if hop > 0:
                y_downs[-1].wait_recv()
            block = (y + hop) % 8
            copy = remote(
                waves.at[block], waves.at[block], ydown_s.at[hop], ydown_r.at[hop], rp, left
            )
            copy.start()
            y_downs.append(copy)
    y_ups[-1].wait_recv()
    y_downs[-1].wait_recv()

    everything = waves[...].reshape(128, LANES)
    points_c = mm(mix[...], everything)
    for a in range(40):
        cut = slice(a * 40, a * 40 + 40)
        coupling[pl.ds(a, 32, stride=40), :] = jnp.concatenate(
            [points_c[0:32, cut], points_c[32:64, cut], jnp.zeros((32, 48), F32)], axis=1
        )

    def one_point(i, carry):
        here = right_rot[pl.ds(pl.multiple_of(i * 80, 8), 80), 0:80].astype(BF)
        there = left_rot[pl.ds(pl.multiple_of(i * 80, 8), 40), 0:80].astype(BF)
        block = coupling[pl.ds(pl.multiple_of(i * 40, 8), 40), 0:80].astype(BF)
        mixed = mm(block, here).astype(BF)
        final = mm_first(there, mixed)
        real = final[0:40, 0:40] + final[40:80, 40:80]
        imag = final[0:40, 40:80] - final[40:80, 0:40]
        strength = real * real + imag * imag
        terms = strength * weight[pl.ds(pl.multiple_of(i * 40, 8), 40), 0:40]
        rates[pl.ds(i, 1), 0:40] = jnp.sum(terms, axis=0, keepdims=True)
        return carry

    rates[...] = jnp.zeros((32, 128), F32)
    lax.fori_loop(0, 32, one_point, 0)

    z_copies = []
    for step in range(1, 8):
        copy = remote(
            rates, land_z.at[step - 1], rz_s.at[step], rz_r.at[step], (rp + 4 * step) % 32, re
        )
        copy.start()
        z_copies.append(copy)
    summed = rates[...]
    for step in range(1, 8):
        z_copies[step - 1].wait_recv()
        summed = summed + land_z[step - 1]
    rates_z[...] = summed.reshape(2, 16, 128)
    c_copies = []
    for dx in (0, 1):
        for dc in (0, 1):
            for dl in (0, 1):
                slot_c = dx * 4 + dc * 2 + dl
                if slot_c == 0:
                    continue
                copy = remote(
                    rates_z.at[(x_lo + dl) % 2],
                    land_c.at[slot_c],
                    rc_s.at[slot_c],
                    rc_r.at[slot_c],
                    flip_rp(dx, dc),
                    flip_re(dl),
                )
                copy.start()
                c_copies.append((slot_c, copy))
    final_sum = rates_z[x_lo]
    for slot_c, copy in c_copies:
        copy.wait_recv()
        final_sum = final_sum + land_c[slot_c]
    out_ref[...] = final_sum[:, 0:40]

    for copy in core_copies + [pack_copy] + u_copies + sends + list(x_copies.values()):
        copy.wait_send()
    for copy in y_ups + y_downs + z_copies:
        copy.wait_send()
    for _, copy in c_copies:
        copy.wait_send()


def per_device(
    wannier_coupling,
    phonon_lattice,
    phonon_degeneracy,
    electron_lattice,
    electron_degeneracy,
    phonon_wavevectors,
    electron_wavevectors,
    phonon_energies,
    bloch_rotations,
    band_energies,
    shifted_points,
):
    w = wannier_coupling.reshape(16, 4, ROW).transpose(1, 0, 2).reshape(64, ROW)
    w = jnp.pad(w, ((0, 0), (0, LANES - ROW)))
    cosw, sinw = phase_tables(
        phonon_wavevectors, jnp.tile(phonon_lattice, (32, 1)), jnp.tile(phonon_degeneracy, 32)
    )
    cosk, sink = phase_tables(electron_wavevectors, electron_lattice, electron_degeneracy)
    energies = [part.reshape(128, 5) for part in three_parts(band_energies)]
    upper = jnp.concatenate(
        [bloch_rotations.reshape(128, 400).astype(BF)] + energies + [jnp.zeros((128, 97), BF)],
        axis=1,
    )
    lower = [cosk, sink]
    for part in three_parts(band_energies):
        lower += [part, jnp.zeros((16, 88), BF)]
    pack = jnp.concatenate([upper, jnp.concatenate(lower, axis=1)], axis=0)
    points = shifted_points.reshape(16, 16)

    def vm(shape, dtype):
        return pltpu.VMEM(shape, dtype)

    dma = pltpu.SemaphoreType.DMA
    return pl.pallas_call(
        kernel,
        out_shape=jax.ShapeDtypeStruct((16, 40), F32),
        in_specs=[pl.BlockSpec(memory_space=pltpu.VMEM)] * 6,
        out_specs=pl.BlockSpec(memory_space=pltpu.VMEM),
        scratch_shapes=[
            vm((64, LANES), BF),
            vm((256, 128), BF),
            vm((256, 128), BF),
            vm((256, 128), BF),
            vm((2, 144, PACK), BF),
            vm((8, 2, 16, PACK), BF),
            vm((16, 2, 16, PACK), BF),
            vm((256, LANES), F32),
            vm((4, 2, 16, LANES), BF),
            vm((3, 2, 16, LANES), BF),
            vm((4, 2, 16, LANES), BF),
            vm((3, 2, 16, LANES), BF),
            vm((2, 2, 8, LANES), F32),
            vm((4, 8, LANES), F32),
            vm((8, 16, LANES), BF),
            vm((64, 128), BF),
            vm((2560, 128), F32),
            vm((2560, 128), F32),
            vm((1280, 128), F32),
            vm((32, 128), F32),
            vm((1280, 128), F32),
            vm((1280, 128), F32),
            vm((32, 128), F32),
            vm((7, 32, 128), F32),
            vm((2, 16, 128), F32),
            vm((8, 16, 128), F32),
            dma((2,)),
            dma((2,)),
            dma,
            dma,
            dma((16,)),
            dma((16,)),
            dma((4, 2)),
            dma((4, 2)),
            dma((3, 2)),
            dma((3, 2)),
            dma((4,)),
            dma((4,)),
            dma((4,)),
            dma((4,)),
            dma((3,)),
            dma((3,)),
            dma((8,)),
            dma((8,)),
            dma((8,)),
            dma((8,)),
        ],
        compiler_params=pltpu.CompilerParams(
            collective_id=0, has_side_effects=True, vmem_limit_bytes=40 * 1024 * 1024
        ),
        cost_estimate=pl.CostEstimate(
            flops=300_000_000, bytes_accessed=2_000_000, transcendentals=200_000
        ),
    )(w, cosw, sinw, pack, points, phonon_energies)


def solution(mesh):
    in_specs = (
        P("re", "rp", None),
        P("rp", None),
        P("rp"),
        P(),
        P(),
        P(),
        P("re", None),
        P("rp", None),
        P("re", None),
        P("re", None),
        P("rp", None),
    )
    return jax.shard_map(
        per_device, mesh=mesh, in_specs=in_specs, out_specs=P("re", None), check_vma=False
    )
```

```python
import math

import jax
import jax.numpy as jnp
from jax import lax
from jax.experimental import pallas as pl
from jax.experimental.pallas import tpu as pltpu
from jax.sharding import PartitionSpec as P

NW = 40
MODES = 2
ROW = 1600
LANES = 1664
PACK = 512
MESH = pl.DeviceIdType.MESH
BF = jnp.bfloat16
F32 = jnp.float32

full_turn = 2.0 * math.pi
thermal = 0.025
broadening = 0.05
highest = lax.Precision.HIGHEST


def three_parts(values):
    high = values.astype(BF).astype(F32)
    rest = values - high
    middle = rest.astype(BF).astype(F32)
    return high, middle, rest - middle


def iota(shape, axis):
    return lax.broadcasted_iota(jnp.int32, shape, axis)


def mm(left, right):
    return jnp.dot(left, right, preferred_element_type=F32)


def outer(left, right):
    return lax.dot_general(
        left, right, (((0,), (0,)), ((), ())), precision=highest, preferred_element_type=F32
    )


LANE_TILES = [(start, min(start + 256, LANES)) for start in range(0, LANES, 256)]
HALF = 896


def kernel(
    w_ref,
    plat_ref,
    pdeg_ref,
    elat_ref,
    edeg_ref,
    qvec_ref,
    kvec_ref,
    phonon_ref,
    rot_ref,
    band_ref,
    shift_ref,
    out_ref,
    w_own,
    w_sib,
    cosw,
    sinw,
    lhs_own,
    lhs_out,
    lhs_sib,
    points_ref,
    pack_f,
    pack,
    packs,
    u_out,
    u_in,
    part,
    s_far,
    l_far,
    s_opp,
    l_opp,
    s_near,
    l_near,
    s_two,
    l_two,
    total,
    land_x,
    waves,
    mix,
    turn_a,
    turn_b,
    right_rot,
    left_rot,
    energy_col,
    energy_row,
    weight,
    coupling,
    rates,
    rates_b,
    land_c,
    rates_z,
    land_z,
    core_s,
    core_r,
    pack_s,
    pack_r,
    u_s,
    u_r,
    far_s,
    far_r,
    opp_s,
    opp_r,
    near_s,
    near_r,
    two_s,
    two_r,
    x_s,
    x_r,
    y1_s,
    y1_r,
    y2_s,
    y2_r,
    rc_s,
    rc_r,
    rz_s,
    rz_r,
):
    rp = lax.axis_index("rp")
    re = lax.axis_index("re")
    z = rp // 4
    x_hi = (rp // 2) % 2
    core = rp % 2
    y = re // 2
    x_lo = re % 2

    def flip_rp(dx, dc):
        hi = (1 - x_hi) if dx else x_hi
        co = (1 - core) if dc else core
        return z * 4 + hi * 2 + co

    def flip_re(dl):
        return y * 2 + ((1 - x_lo) if dl else x_lo)

    def along_z(step):
        return (rp + 32 + 4 * step) % 32

    def along_y(step):
        return (re + 16 + 2 * step) % 16

    started = []

    def remote(src, dst, send, recv, to_rp, to_re):
        copy = pltpu.make_async_remote_copy(
            src_ref=src,
            dst_ref=dst,
            send_sem=send,
            recv_sem=recv,
            device_id={"rp": to_rp, "re": to_re},
            device_id_type=MESH,
        )
        copy.start()
        started.append(copy)
        return copy

    partners = [(rp, (re + step) % 16) for step in range(1, 16)]
    partners += [(along_z(step), re) for step in range(1, 8)]
    partners += [
        (flip_rp(dx, dc), flip_re(dl))
        for dx in (0, 1)
        for dc in (0, 1)
        for dl in (0, 1)
        if dx or dc
    ]
    barrier = pltpu.get_barrier_semaphore()
    for to_rp, to_re in partners:
        pl.semaphore_signal(
            barrier, inc=1, device_id={"rp": to_rp, "re": to_re}, device_id_type=MESH
        )

    cells = jnp.concatenate([w_ref[e].astype(F32) for e in range(4)], axis=0)
    for mc in range(4):
        w_own[mc * 16 : mc * 16 + 16, :] = jnp.concatenate(
            [cells[:, mc * ROW : (mc + 1) * ROW], jnp.zeros((16, LANES - ROW), F32)], axis=1
        ).astype(BF)

    r_of_lane = jnp.where(iota((4, 128), 0) == (iota((4, 128), 1) & 3), 1.0, 0.0).astype(F32)
    p_angle = full_turn * outer(qvec_ref[...], outer(plat_ref[...].astype(F32), r_of_lane))
    p_weight = 1.0 / outer(pdeg_ref[...].astype(F32), r_of_lane)
    cosw[...] = (jnp.cos(p_angle) * p_weight).astype(BF)
    sinw[...] = (jnp.sin(p_angle) * p_weight).astype(BF)
    row = iota((256, 128), 0)
    lane = iota((256, 128), 1)
    same = ((row >> 3) & 1 == (lane >> 5) & 1) & (row & 3 == (lane >> 2) & 3) & (lane < 64)
    to_imag = (row >> 2) & 1
    of_imag = (lane >> 4) & 1
    pick_cos = same & (to_imag == of_imag)
    pick_sin = same & (to_imag != of_imag)
    sign = jnp.where(to_imag == 1, 1.0, -1.0).astype(F32)
    q_row = iota((256, 32), 0)
    q_lane = iota((256, 32), 1)

    def phases_for(which_core):
        spread = jnp.where((q_row >> 4) * 2 + which_core == q_lane, 1.0, 0.0).astype(BF)
        cos_part = mm(spread, cosw[...])
        sin_part = mm(spread, sinw[...])
        return jnp.where(
            pick_cos, cos_part, jnp.where(pick_sin, sign * sin_part, 0.0)
        ).astype(BF)

    lhs_out[...] = phases_for(1 - core)

    pl.semaphore_wait(barrier, len(partners))

    sib = flip_rp(0, 1)
    core_copies = [
        remote(w_own, w_sib, core_s.at[0], core_r.at[0], sib, re),
        remote(lhs_out, lhs_sib, core_s.at[1], core_r.at[1], sib, re),
    ]

    lhs_own[...] = phases_for(core)
    for start, end in LANE_TILES:
        part[:, start:end] = mm(lhs_own[:, 0:64], w_own[:, start:end])
    for copy in core_copies:
        copy.wait_recv()
    for start, end in LANE_TILES:
        part[:, start:end] += mm(lhs_sib[:, 0:64], w_sib[:, start:end])

    def part_of(z_to, sub):
        hi = (1 - x_hi) if sub == 0 else x_hi
        block = ((z_to + 8) % 8) * 2 + hi
        return part[pl.ds(pl.multiple_of(block * 16, 16), 16), :]

    far = {}
    opp = {}
    for sub in (0, 1):
        toward = 2 if sub == 0 else -2
        s_opp[sub] = part_of(z + 4, sub).astype(BF)
        opp[sub] = remote(
            s_opp.at[sub], l_opp.at[sub], opp_s.at[sub], opp_r.at[sub], along_z(toward), re
        )
        for side, step in ((0, 1), (1, -1)):
            s_far[side, sub] = part_of(z + 3 * step, sub).astype(BF)
            far[side, sub] = remote(
                s_far.at[side, sub],
                l_far.at[side, sub],
                far_s.at[side, sub],
                far_r.at[side, sub],
                along_z(step),
                re,
            )
    near = {}
    for side, step in ((0, 1), (1, -1)):
        for sub in (0, 1):
            s_near[side, sub] = part_of(z + step, sub).astype(BF)
        near[side] = remote(
            s_near.at[side], l_near.at[side], near_s.at[side], near_r.at[side], along_z(step), re
        )

    e_angle = full_turn * outer(kvec_ref[...], elat_ref[...].astype(F32))
    e_weight = 1.0 / edeg_ref[...].astype(F32)
    high, middle, low = three_parts(band_ref[...])
    gap = jnp.zeros((16, 48), F32)
    pack[128:144, :] = jnp.concatenate(
        [jnp.cos(e_angle) * e_weight, jnp.sin(e_angle) * e_weight]
        + [high, high, gap, middle, middle, gap, low, low, gap],
        axis=1,
    ).astype(BF)
    rest = jnp.zeros((16, PACK - 415), F32)
    for j in range(8):
        five = slice(j * 5, j * 5 + 5)
        eighth = jnp.concatenate(
            [rot_ref[:, j * 400 : j * 400 + 400], high[:, five], middle[:, five], low[:, five], rest],
            axis=1,
        )
        for v in range(4):
            pack_f[v, pl.ds(j, 16, stride=8), :] = eighth[:, v * 128 : v * 128 + 128]
    for v in range(4):
        pack[0:128, v * 128 : v * 128 + 128] = pack_f[v].astype(BF)
    pack_copy = remote(pack, packs.at[x_lo], pack_s, pack_r, rp, flip_re(1))

    for d in range(16):
        points_ref[d : d + 1, :] = shift_ref[:, d * 16 : d * 16 + 16]
    points = points_ref[...]
    mine = (points >> 4) == re
    inner = points & 15
    smaller = jnp.min(jnp.where(mine, inner, 99), axis=1, keepdims=True)
    larger = jnp.max(jnp.where(mine, inner, -1), axis=1, keepdims=True)
    both = jnp.where(iota((16, 128), 1) == 0, smaller, larger).astype(F32).astype(BF)
    spread16 = jnp.where((iota((256, 16), 0) >> 4) == iota((256, 16), 1), 1.0, 0.0).astype(BF)
    both_rows = mm(spread16, both)
    slot = (iota((256, 1), 0) >> 3) & 1
    chosen = jnp.where(slot == 0, both_rows[:, 0:1], both_rows[:, 1:2])
    take = ((lane >> 3).astype(F32) == chosen) & ((lane & 7) == (row & 7))
    take = jnp.where(take, 1.0, 0.0).astype(BF)
    u_out[...] = mm(take, pack[0:128, :]).astype(BF).reshape(8, 2, 16, PACK)
    u_copies = []
    for step in range(1, 16):
        to = (re + step) % 16
        u_copies.append(
            remote(u_out.at[to // 2], u_in.at[re], u_s.at[step], u_r.at[step], rp, to)
        )
    packs[x_lo] = pack[...]
    u_in[re] = u_out[y]

    two = {}
    for sub in (0, 1):
        for side, step in ((0, 1), (1, -1)):
            far[side, sub].wait_recv()
            done = part_of(z + 2 * step, sub) + l_far[side, sub].astype(F32)
            if side == sub:
                opp[sub].wait_recv()
                done = done + l_opp[sub].astype(F32)
            s_two[side, sub] = done.astype(BF)
            two[side, sub] = remote(
                s_two.at[side, sub],
                l_two.at[side, sub],
                two_s.at[side, sub],
                two_r.at[side, sub],
                along_z(2 * step),
                re,
            )

    def swap_halves(rows):
        cut = rows.reshape(16, 8, PACK)
        return jnp.concatenate([cut[:, 4:8], cut[:, 0:4]], axis=1).reshape(128, PACK)

    def rotations_here():
        pack_copy.wait_recv()
        blank = jnp.zeros((128, 48), F32)
        for b in (0, 1):
            rows = packs[b, 0:128, :].astype(F32)
            swapped = swap_halves(rows)
            rows = rows * jnp.where((iota((128, 1), 0) >> 2) & 1 == 1, -1.0, 1.0)
            for t in range(10):
                cut = slice(t * 40, t * 40 + 40)
                spot = pl.ds(b * 1280 + t, 128, stride=10)
                turn_a[spot, :] = jnp.concatenate([rows[:, cut], swapped[:, cut], blank], axis=1)
                turn_b[spot, :] = jnp.concatenate([swapped[:, cut], -rows[:, cut], blank], axis=1)
            tail = packs[b, 128:144, :].astype(F32)
            energy_row[b * 16 : b * 16 + 16, :] = (
                tail[:, 128:256] + tail[:, 256:384] + tail[:, 384:512]
            )

        def one(i, carry):
            spot = pl.ds(pl.multiple_of(i * 80, 8), 80)
            right_rot[i] = jnp.concatenate([turn_a[spot, :], turn_b[spot, :]], axis=1).astype(BF)
            return carry

        lax.fori_loop(0, 32, one, 0)

    def rotations_there():
        for copy in u_copies:
            copy.wait_recv()
        blank = jnp.zeros((128, 88), F32)
        for b in (0, 1):
            block = points_ref[pl.ds(y * 2 + b, 1), :]
            spot = iota((128, 16), 0) >> 3 == iota((128, 16), 1)
            wide = jnp.broadcast_to(block, (128, 16))
            target = jnp.sum(jnp.where(spot, wide, 0), axis=1, keepdims=True)
            before = ((wide >> 4) == (target >> 4)) & (wide < target)
            second = jnp.max(jnp.where(before, 1, 0), axis=1, keepdims=True)
            source = (target >> 4) * 16 + second * 8 + (iota((128, 1), 0) & 7)
            order = jnp.where(iota((128, 256), 1) == source, 1.0, 0.0).astype(BF)
            rows = mm(order, u_in[:, b].reshape(256, PACK))
            for t in range(10):
                turn_a[pl.ds(b * 1280 + t, 128, stride=10), :] = jnp.concatenate(
                    [rows[:, t * 40 : t * 40 + 40], blank], axis=1
                )
            for t in range(5):
                energy = (
                    rows[:, 400 + t : 401 + t]
                    + rows[:, 405 + t : 406 + t]
                    + rows[:, 410 + t : 411 + t]
                )
                energy_col[pl.ds(b * 640 + t, 128, stride=5), :] = jnp.broadcast_to(
                    energy, (128, 128)
                )

        def one(i, carry):
            spot = pl.ds(pl.multiple_of(i * 80, 8), 80)
            left_rot[i, :, 0:80] = jnp.transpose(turn_a[spot, :])[0:48, :].astype(BF)
            return carry

        lax.fori_loop(0, 32, one, 0)

    def weights():
        omega = jnp.where(x_lo == 0, phonon_ref[0:1, 0:1], phonon_ref[0:1, 1:2])
        bose = 1.0 / (jnp.exp(omega / thermal) - 1.0)
        scale = (math.pi / 32.0) * (broadening / math.pi) / (2.0 * omega)

        def one(i, carry):
            there = energy_col[pl.ds(pl.multiple_of(i * 40, 8), 40), :]
            here = energy_row[pl.ds(i, 1), :]
            filling = 1.0 / (1.0 + jnp.exp(there / thermal))
            spacing = here - there
            plus = spacing + omega
            minus = spacing - omega
            wide = broadening * broadening
            weight[pl.ds(pl.multiple_of(i * 40, 8), 40), :] = scale * (
                (bose + filling) / (plus * plus + wide)
                + (bose + 1.0 - filling) / (minus * minus + wide)
            )
            return carry

        lax.fori_loop(0, 32, one, 0)

    def electron_phases():
        lane4 = iota((128, 128), 1)
        place = lane4 >> 4
        ahead = (place + 1) >> 1
        source = (y + 8 + jnp.where(place & 1 == 1, ahead, -ahead)) & 7
        e_of_lane = (source * 2 + ((x_lo + (lane4 >> 3)) & 1)) * 4 + (lane4 & 3)
        row4 = iota((128, 128), 0)
        match = (row4 & 63) == e_of_lane
        sine = row4 >> 6
        imag = (lane4 >> 2) & 1
        to_real = jnp.where(match & (sine == imag), jnp.where(sine == 1, -1.0, 1.0), 0.0)
        to_im = jnp.where(match & (sine != imag), 1.0, 0.0)
        for b in (0, 1):
            table = packs[b, 128:144, 0:128]
            mix[b * 16 : b * 16 + 16, :] = mm(table, to_real.astype(BF)).astype(BF)
            mix[32 + b * 16 : 48 + b * 16, :] = mm(table, to_im.astype(BF)).astype(BF)

    rotations_here()
    electron_phases()

    x_copies = {}
    for side in (0, 1):
        near[side].wait_recv()
    for sub in (0, 1):
        done = part_of(z, sub) + l_near[0, sub].astype(F32) + l_near[1, sub].astype(F32)
        for side in (0, 1):
            two[side, sub].wait_recv()
            done = done + l_two[side, sub].astype(F32)
        total[sub] = done.reshape(2, 8, LANES)
        for dl in (0, 1):
            if sub == 1 and dl == 0:
                continue
            dx = 1 - sub
            spot = dx * 2 + dl
            x_copies[spot] = remote(
                total.at[sub, (x_lo + dl) % 2],
                land_x.at[spot],
                x_s.at[spot],
                x_r.at[spot],
                flip_rp(dx, 0),
                flip_re(dl),
            )
    rotations_there()
    for copy in x_copies.values():
        copy.wait_recv()
    waves[0] = jnp.concatenate(
        [total[1, x_lo] + land_x[2], land_x[1] + land_x[3]], axis=0
    ).astype(BF)

    first = {}
    for place, step in ((4, 2), (3, -2), (2, 1), (1, -1)):
        first[place] = remote(
            waves.at[0], waves.at[place], y1_s.at[place], y1_r.at[place], rp, along_y(step)
        )
    weights()
    first[2].wait_recv()
    later = [remote(waves.at[2], waves.at[6], y2_s.at[0], y2_r.at[0], rp, along_y(2))]
    first[1].wait_recv()
    later.append(remote(waves.at[1], waves.at[5], y2_s.at[1], y2_r.at[1], rp, along_y(-2)))
    lower = pl.ds(0, HALF)
    upper = pl.ds(HALF, LANES - HALF)
    first[4].wait_recv()
    later.append(
        remote(
            waves.at[4, :, lower],
            waves.at[7, :, lower],
            y2_s.at[2],
            y2_r.at[2],
            rp,
            along_y(2),
        )
    )
    first[3].wait_recv()
    later.append(
        remote(
            waves.at[3, :, upper],
            waves.at[7, :, upper],
            y2_s.at[3],
            y2_r.at[3],
            rp,
            along_y(-2),
        )
    )
    points_c = mm(mix[:, 0:80], waves[0:5].reshape(80, LANES))
    for copy in later:
        copy.wait_recv()
    points_c = points_c + mm(mix[:, 80:128], waves[5:8].reshape(48, LANES))

    for a in range(40):
        cut = slice(a * 40, a * 40 + 40)
        coupling[pl.ds(a, 32, stride=40), :] = jnp.concatenate(
            [points_c[0:32, cut], points_c[32:64, cut], jnp.zeros((32, 48), F32)], axis=1
        )

    def some_points(group, carry):
        indices = [group * 8 + i for i in range(8)]
        spots = [pl.ds(pl.multiple_of(i * 40, 8), 40) for i in indices]
        turned = [
            mm(coupling[spot, 0:80].astype(BF), right_rot[i])
            for i, spot in zip(indices, spots, strict=True)
        ]
        stacked = [
            jnp.concatenate([t[:, 0:80], t[:, 128:208]], axis=0).astype(BF) for t in turned
        ]
        final = [
            mm(left_rot[i, 0:40, 0:80], s) for i, s in zip(indices, stacked, strict=True)
        ]
        sums = [
            jnp.sum(f * f * weight[spot, 0:80], axis=0, keepdims=True)
            for f, spot in zip(final, spots, strict=True)
        ]
        rates[pl.ds(pl.multiple_of(group * 8, 8), 8), 0:80] = jnp.concatenate(sums, axis=0)
        return carry

    lax.fori_loop(0, 4, some_points, 0)

    for b in (0, 1):
        rows = rates[b * 16 : b * 16 + 16, 0:40] + rates[b * 16 : b * 16 + 16, 40:80]
        rates_b[b] = jnp.concatenate([rows[0:8], rows[8:16], jnp.zeros((8, 48), F32)], axis=1)
    c_copies = []
    for dx in (1, 0):
        for dl in (1, 0):
            for dc in (1, 0):
                spot = dx * 4 + dc * 2 + dl
                if spot == 0:
                    continue
                copy = remote(
                    rates_b.at[(x_lo + dl) % 2],
                    land_c.at[spot],
                    rc_s.at[spot],
                    rc_r.at[spot],
                    flip_rp(dx, dc),
                    flip_re(dl),
                )
                c_copies.append((spot, copy))
    summed = rates_b[x_lo]
    for spot, copy in reversed(c_copies):
        copy.wait_recv()
        summed = summed + land_c[spot]
    rates_z[...] = summed
    z_copies = []
    for step in (4, 3, 5, 2, 6, 1, 7):
        copy = remote(
            rates_z, land_z.at[step], rz_s.at[step], rz_r.at[step], along_z(step), re
        )
        z_copies.append((step, copy))
    for step, copy in reversed(z_copies):
        copy.wait_recv()
        summed = summed + land_z[step]
    out_ref[0:8, :] = summed[:, 0:40]
    out_ref[8:16, :] = summed[:, 40:80]

    for copy in started:
        copy.wait_send()


def per_device(
    wannier_coupling,
    phonon_lattice,
    phonon_degeneracy,
    electron_lattice,
    electron_degeneracy,
    phonon_wavevectors,
    electron_wavevectors,
    phonon_energies,
    bloch_rotations,
    band_energies,
    shifted_points,
):
    def vm(shape, dtype):
        return pltpu.VMEM(shape, dtype)

    def dma(*shape):
        return pltpu.SemaphoreType.DMA(shape)

    return pl.pallas_call(
        kernel,
        out_shape=jax.ShapeDtypeStruct((16, 40), F32),
        in_specs=[pl.BlockSpec(memory_space=pltpu.VMEM)] * 11,
        out_specs=pl.BlockSpec(memory_space=pltpu.VMEM),
        scratch_shapes=[
            vm((64, LANES), BF),
            vm((64, LANES), BF),
            vm((32, 128), BF),
            vm((32, 128), BF),
            vm((256, 128), BF),
            vm((256, 128), BF),
            vm((256, 128), BF),
            vm((16, 16), jnp.int32),
            vm((4, 128, 128), F32),
            vm((144, PACK), BF),
            vm((2, 144, PACK), BF),
            vm((8, 2, 16, PACK), BF),
            vm((16, 2, 16, PACK), BF),
            vm((256, LANES), F32),
            vm((2, 2, 16, LANES), BF),
            vm((2, 2, 16, LANES), BF),
            vm((2, 16, LANES), BF),
            vm((2, 16, LANES), BF),
            vm((2, 2, 16, LANES), BF),
            vm((2, 2, 16, LANES), BF),
            vm((2, 2, 16, LANES), BF),
            vm((2, 2, 16, LANES), BF),
            vm((2, 2, 8, LANES), F32),
            vm((4, 8, LANES), F32),
            vm((8, 16, LANES), BF),
            vm((64, 128), BF),
            vm((2560, 128), F32),
            vm((2560, 128), F32),
            vm((32, 80, 256), BF),
            vm((32, 48, 128), BF),
            vm((1280, 128), F32),
            vm((32, 128), F32),
            vm((1280, 128), F32),
            vm((1280, 128), F32),
            vm((32, 128), F32),
            vm((2, 8, 128), F32),
            vm((8, 8, 128), F32),
            vm((8, 128), F32),
            vm((8, 8, 128), F32),
            dma(2),
            dma(2),
            pltpu.SemaphoreType.DMA,
            pltpu.SemaphoreType.DMA,
            dma(16),
            dma(16),
            dma(2, 2),
            dma(2, 2),
            dma(2),
            dma(2),
            dma(2),
            dma(2),
            dma(2, 2),
            dma(2, 2),
            dma(4),
            dma(4),
            dma(5),
            dma(5),
            dma(4),
            dma(4),
            dma(8),
            dma(8),
            dma(8),
            dma(8),
        ],
        compiler_params=pltpu.CompilerParams(
            collective_id=0, has_side_effects=True, vmem_limit_bytes=40 * 1024 * 1024
        ),
        cost_estimate=pl.CostEstimate(
            flops=300_000_000, bytes_accessed=2_000_000, transcendentals=200_000
        ),
    )(
        wannier_coupling,
        phonon_lattice,
        phonon_degeneracy.reshape(4, 1),
        electron_lattice.T,
        electron_degeneracy.reshape(1, 64),
        phonon_wavevectors.T,
        electron_wavevectors.T,
        phonon_energies,
        bloch_rotations,
        band_energies,
        shifted_points,
    )


def solution(mesh):
    in_specs = (
        P("re", "rp", None),
        P("rp", None),
        P("rp"),
        P(),
        P(),
        P(),
        P("re", None),
        P("rp", None),
        P("re", None),
        P("re", None),
        P("rp", None),
    )
    return jax.shard_map(
        per_device, mesh=mesh, in_specs=in_specs, out_specs=P("re", None), check_vma=False
    )
```

```python
import math

import jax
import jax.numpy as jnp
from jax import lax
from jax.experimental import pallas as pl
from jax.experimental.pallas import tpu as pltpu
from jax.sharding import PartitionSpec as P

NW = 40
MODES = 2
ROW = 1600
LANES = 1664
PACK = 512
MESH = pl.DeviceIdType.MESH
BF = jnp.bfloat16
F32 = jnp.float32

full_turn = 2.0 * math.pi
thermal = 0.025
broadening = 0.05
highest = lax.Precision.HIGHEST


def three_parts(values):
    high = values.astype(BF).astype(F32)
    rest = values - high
    middle = rest.astype(BF).astype(F32)
    return high, middle, rest - middle


def iota(shape, axis):
    return lax.broadcasted_iota(jnp.int32, shape, axis)


def mm(left, right):
    return jnp.dot(left, right, preferred_element_type=F32)


def outer(left, right):
    return lax.dot_general(
        left, right, (((0,), (0,)), ((), ())), precision=highest, preferred_element_type=F32
    )


LANE_TILES = [(start, min(start + 256, LANES)) for start in range(0, LANES, 256)]
HALF = 896


def kernel(
    w_hbm,
    plat_hbm,
    pdeg_hbm,
    elat_hbm,
    edeg_hbm,
    qvec_hbm,
    kvec_hbm,
    phonon_hbm,
    rot_hbm,
    band_hbm,
    shift_hbm,
    out_ref,
    w_ref,
    plat_ref,
    pdeg_ref,
    elat_ref,
    edeg_ref,
    qvec_ref,
    kvec_ref,
    phonon_ref,
    rot_ref,
    band_ref,
    shift_ref,
    w_own,
    w_sib,
    cosw,
    sinw,
    lhs_own,
    lhs_out,
    lhs_sib,
    points_ref,
    pack_f,
    pack,
    packs,
    u_out,
    u_in,
    part,
    s_far,
    l_far,
    s_opp,
    l_opp,
    s_piece,
    l_piece,
    waves,
    mix,
    turn_a,
    turn_b,
    right_rot,
    left_rot,
    energy_col,
    energy_row,
    weight,
    coupling,
    rates,
    rates_b,
    land_c,
    rates_z,
    land_z,
    in_s,
    core_s,
    core_r,
    pack_s,
    pack_r,
    u_s,
    u_r,
    far_s,
    far_r,
    opp_s,
    opp_r,
    piece_s,
    piece_r,
    swap_s,
    swap_r,
    y1_s,
    y1_r,
    y2_s,
    y2_r,
    rc_s,
    rc_r,
    rz_s,
    rz_r,
):
    rp = lax.axis_index("rp")
    re = lax.axis_index("re")
    z = rp // 4
    x_hi = (rp // 2) % 2
    core = rp % 2
    y = re // 2
    x_lo = re % 2

    def flip_rp(dx, dc, step=0):
        hi = (1 - x_hi) if dx else x_hi
        co = (1 - core) if dc else core
        return ((z + 8 + step) % 8) * 4 + hi * 2 + co

    def flip_re(dl):
        return y * 2 + ((1 - x_lo) if dl else x_lo)

    def along_z(step):
        return (rp + 32 + 4 * step) % 32

    def along_y(step):
        return (re + 16 + 2 * step) % 16

    loads = {}
    for number, (name, src, dst) in enumerate(
        (
            ("w", w_hbm, w_ref),
            ("plat", plat_hbm, plat_ref),
            ("pdeg", pdeg_hbm, pdeg_ref),
            ("qvec", qvec_hbm, qvec_ref),
            ("elat", elat_hbm, elat_ref),
            ("edeg", edeg_hbm, edeg_ref),
            ("kvec", kvec_hbm, kvec_ref),
            ("phonon", phonon_hbm, phonon_ref),
            ("rot", rot_hbm, rot_ref),
            ("band", band_hbm, band_ref),
            ("shift", shift_hbm, shift_ref),
        )
    ):
        loads[name] = pltpu.make_async_copy(src, dst, in_s.at[number])
        loads[name].start()

    def loaded(*names):
        for name in names:
            loads[name].wait()

    started = []

    def remote(src, dst, send, recv, to_rp, to_re):
        copy = pltpu.make_async_remote_copy(
            src_ref=src,
            dst_ref=dst,
            send_sem=send,
            recv_sem=recv,
            device_id={"rp": to_rp, "re": to_re},
            device_id_type=MESH,
        )
        copy.start()
        started.append(copy)
        return copy

    partners = [
        (flip_rp(dx, dc), flip_re(dl))
        for dc in (1, 0)
        for dx in (0, 1)
        for dl in (0, 1)
        if dx or dc or dl
    ]
    partners += [(along_z(step), re) for step in range(1, 8)]
    partners += [
        (flip_rp(dx, 0, step), flip_re(dl))
        for step in (1, -1, 2, -2)
        for dx, dl in ((0, 1), (1, 0), (1, 1))
    ]
    partners += [(rp, along_y(step)) for step in range(1, 8)]
    barrier = pltpu.get_barrier_semaphore()
    for to_rp, to_re in partners:
        pl.semaphore_signal(
            barrier, inc=1, device_id={"rp": to_rp, "re": to_re}, device_id_type=MESH
        )

    loaded("w")
    cells = jnp.concatenate([w_ref[e].astype(F32) for e in range(4)], axis=0)
    for mc in range(4):
        w_own[mc * 16 : mc * 16 + 16, :] = jnp.concatenate(
            [cells[:, mc * ROW : (mc + 1) * ROW], jnp.zeros((16, LANES - ROW), F32)], axis=1
        ).astype(BF)

    pl.semaphore_wait(barrier, len(partners))

    sib = flip_rp(0, 1)
    core_copies = [remote(w_own, w_sib, core_s.at[0], core_r.at[0], sib, re)]

    loaded("plat", "pdeg", "qvec")
    r_of_lane = jnp.where(iota((4, 128), 0) == (iota((4, 128), 1) & 3), 1.0, 0.0).astype(F32)
    p_angle = full_turn * outer(qvec_ref[...], outer(plat_ref[...].astype(F32), r_of_lane))
    p_weight = 1.0 / jnp.dot(
        pdeg_ref[...].astype(F32), r_of_lane, precision=highest, preferred_element_type=F32
    )
    cosw[...] = (jnp.cos(p_angle) * p_weight).astype(BF)
    sinw[...] = (jnp.sin(p_angle) * p_weight).astype(BF)
    row = iota((256, 128), 0)
    lane = iota((256, 128), 1)
    same = ((row >> 3) & 1 == (lane >> 5) & 1) & (row & 3 == (lane >> 2) & 3) & (lane < 64)
    to_imag = (row >> 2) & 1
    of_imag = (lane >> 4) & 1
    pick_cos = same & (to_imag == of_imag)
    pick_sin = same & (to_imag != of_imag)
    sign = jnp.where(to_imag == 1, 1.0, -1.0).astype(F32)
    q_row = iota((256, 32), 0)
    q_lane = iota((256, 32), 1)

    def phases_for(which_core):
        spread = jnp.where((q_row >> 4) * 2 + which_core == q_lane, 1.0, 0.0).astype(BF)
        cos_part = mm(spread, cosw[...])
        sin_part = mm(spread, sinw[...])
        return jnp.where(
            pick_cos, cos_part, jnp.where(pick_sin, sign * sin_part, 0.0)
        ).astype(BF)

    lhs_out[...] = phases_for(1 - core)

    core_copies.append(remote(lhs_out, lhs_sib, core_s.at[1], core_r.at[1], sib, re))
    lhs_own[...] = phases_for(core)
    for start, end in LANE_TILES:
        part[:, start:end] = mm(lhs_own[:, 0:64], w_own[:, start:end])
    for copy in core_copies:
        copy.wait_recv()
    for start, end in LANE_TILES:
        part[:, start:end] += mm(lhs_sib[:, 0:64], w_sib[:, start:end])

    def part_of(z_to, sub):
        hi = (1 - x_hi) if sub == 0 else x_hi
        block = ((z_to + 8) % 8) * 2 + hi
        return part[pl.ds(pl.multiple_of(block * 16, 16), 16), :]

    far = {}
    opp = {}
    for sub in (0, 1):
        toward = 2 if sub == 0 else -2
        s_opp[sub] = part_of(z + 4, sub).astype(BF)
        opp[sub] = remote(
            s_opp.at[sub], l_opp.at[sub], opp_s.at[sub], opp_r.at[sub], along_z(toward), re
        )
        for side, step in ((0, 1), (1, -1)):
            s_far[side, sub] = part_of(z + 3 * step, sub).astype(BF)
            far[side, sub] = remote(
                s_far.at[side, sub],
                l_far.at[side, sub],
                far_s.at[side, sub],
                far_r.at[side, sub],
                along_z(step),
                re,
            )

    def piece_of(z_to, dx, dl):
        hi = (1 - x_hi) if dx else x_hi
        mode = (x_lo + dl) % 2
        first_row = (((z_to + 8) % 8) * 2 + hi) * 16 + mode * 8
        rows = part[pl.ds(pl.multiple_of(first_row, 8), 8), :]
        end = jnp.concatenate([rows[:, HALF:], jnp.zeros((8, 2 * HALF - LANES), F32)], axis=1)
        return jnp.concatenate([rows[:, 0:HALF], end], axis=0).astype(BF)

    pieces = {}

    def send_piece(place, step, dx, dl):
        s_piece[dl, dx, place] = piece_of(z + step, dx, dl)
        pieces[dl, dx, place] = remote(
            s_piece.at[dl, dx, place],
            l_piece.at[dl, dx, place],
            piece_s.at[dl, dx, place],
            piece_r.at[dl, dx, place],
            flip_rp(dx, 0, step),
            flip_re(dl),
        )

    for dx, dl in ((1, 1), (1, 0), (0, 1), (0, 0)):
        for place, step in ((1, 1), (2, -1)):
            send_piece(place, step, dx, dl)
    for dx, dl in ((1, 1), (1, 0), (0, 1)):
        send_piece(0, 0, dx, dl)

    loaded("elat", "edeg", "kvec", "phonon", "rot", "band", "shift")
    e_angle = full_turn * outer(kvec_ref[...], elat_ref[...].astype(F32))
    e_weight = 1.0 / edeg_ref[...].astype(F32)
    high, middle, low = three_parts(band_ref[...])
    gap = jnp.zeros((16, 48), F32)
    pack[128:144, :] = jnp.concatenate(
        [jnp.cos(e_angle) * e_weight, jnp.sin(e_angle) * e_weight]
        + [high, high, gap, middle, middle, gap, low, low, gap],
        axis=1,
    ).astype(BF)
    rest = jnp.zeros((16, PACK - 415), F32)
    for j in range(8):
        five = slice(j * 5, j * 5 + 5)
        eighth = jnp.concatenate(
            [rot_ref[:, j * 400 : j * 400 + 400], high[:, five], middle[:, five], low[:, five], rest],
            axis=1,
        )
        for v in range(4):
            pack_f[v, pl.ds(j, 16, stride=8), :] = eighth[:, v * 128 : v * 128 + 128]
    for v in range(4):
        pack[0:128, v * 128 : v * 128 + 128] = pack_f[v].astype(BF)
    pack_copy = remote(pack, packs.at[x_lo], pack_s, pack_r, rp, flip_re(1))

    for d in range(16):
        points_ref[d : d + 1, :] = shift_ref[:, d * 16 : d * 16 + 16]
    points = points_ref[...]
    mine = (points >> 4) == re
    inner = points & 15
    smaller = jnp.min(jnp.where(mine, inner, 99), axis=1, keepdims=True)
    larger = jnp.max(jnp.where(mine, inner, -1), axis=1, keepdims=True)
    both = jnp.where(iota((16, 128), 1) == 0, smaller, larger).astype(F32).astype(BF)
    spread16 = jnp.where((iota((256, 16), 0) >> 4) == iota((256, 16), 1), 1.0, 0.0).astype(BF)
    both_rows = mm(spread16, both)
    slot = (iota((256, 1), 0) >> 3) & 1
    chosen = jnp.where(slot == 0, both_rows[:, 0:1], both_rows[:, 1:2])
    take = ((lane >> 3).astype(F32) == chosen) & ((lane & 7) == (row & 7))
    take = jnp.where(take, 1.0, 0.0).astype(BF)
    u_out[...] = mm(take, pack[0:128, :]).astype(BF).reshape(8, 2, 16, PACK)
    u_copies = []
    for step in (4, 3, 5, 2, 6, 1, 7):
        u_copies.append(
            remote(
                u_out.at[(y + step) % 8],
                u_in.at[x_lo, y],
                u_s.at[step],
                u_r.at[step],
                rp,
                along_y(step),
            )
        )
    packs[x_lo] = pack[...]
    u_in[x_lo, y] = u_out[y]

    for sub in (0, 1):
        for side, step in ((0, 1), (1, -1)):
            far[side, sub].wait_recv()
            more = l_far[side, sub].astype(F32)
            if side == sub:
                opp[sub].wait_recv()
                more = more + l_opp[sub].astype(F32)
            hi = (1 - x_hi) if sub == 0 else x_hi
            block = ((z + 8 + 2 * step) % 8) * 2 + hi
            part[pl.ds(pl.multiple_of(block * 16, 16), 16), :] += more
            for dl in (1, 0):
                send_piece(3 + side, 2 * step, 1 - sub, dl)

    def swap_halves(rows):
        cut = rows.reshape(16, 8, PACK)
        return jnp.concatenate([cut[:, 4:8], cut[:, 0:4]], axis=1).reshape(128, PACK)

    def rotations_here():
        pack_copy.wait_recv()
        blank = jnp.zeros((128, 48), F32)
        for b in (0, 1):
            rows = packs[b, 0:128, :].astype(F32)
            swapped = swap_halves(rows)
            rows = rows * jnp.where((iota((128, 1), 0) >> 2) & 1 == 1, -1.0, 1.0)
            for t in range(10):
                cut = slice(t * 40, t * 40 + 40)
                spot = pl.ds(b * 1280 + t, 128, stride=10)
                turn_a[spot, :] = jnp.concatenate([rows[:, cut], swapped[:, cut], blank], axis=1)
                turn_b[spot, :] = jnp.concatenate([swapped[:, cut], -rows[:, cut], blank], axis=1)
            tail = packs[b, 128:144, :].astype(F32)
            energy_row[b * 16 : b * 16 + 16, :] = (
                tail[:, 128:256] + tail[:, 256:384] + tail[:, 384:512]
            )

        def one(i, carry):
            spot = pl.ds(pl.multiple_of(i * 80, 8), 80)
            right_rot[i] = jnp.concatenate([turn_a[spot, :], turn_b[spot, :]], axis=1).astype(BF)
            return carry

        lax.fori_loop(0, 32, one, 0)

    def rotations_there():
        u_swap.wait_recv()
        blank = jnp.zeros((128, 88), F32)
        for b in (0, 1):
            block = points_ref[pl.ds(y * 2 + b, 1), :]
            spot = iota((128, 16), 0) >> 3 == iota((128, 16), 1)
            wide = jnp.broadcast_to(block, (128, 16))
            target = jnp.sum(jnp.where(spot, wide, 0), axis=1, keepdims=True)
            before = ((wide >> 4) == (target >> 4)) & (wide < target)
            second = jnp.max(jnp.where(before, 1, 0), axis=1, keepdims=True)
            source = ((target >> 4) & 1) * 128 + (target >> 5) * 16 + second * 8
            source = source + (iota((128, 1), 0) & 7)
            order = jnp.where(iota((128, 256), 1) == source, 1.0, 0.0).astype(BF)
            rows = mm(order, u_in[:, :, b].reshape(256, PACK))
            for t in range(10):
                turn_a[pl.ds(b * 1280 + t, 128, stride=10), :] = jnp.concatenate(
                    [rows[:, t * 40 : t * 40 + 40], blank], axis=1
                )
            for t in range(5):
                energy = (
                    rows[:, 400 + t : 401 + t]
                    + rows[:, 405 + t : 406 + t]
                    + rows[:, 410 + t : 411 + t]
                )
                energy_col[pl.ds(b * 640 + t, 128, stride=5), :] = jnp.broadcast_to(
                    energy, (128, 128)
                )

        def one(i, carry):
            spot = pl.ds(pl.multiple_of(i * 80, 8), 80)
            left_rot[i, :, 0:80] = jnp.transpose(turn_a[spot, :])[0:48, :].astype(BF)
            return carry

        lax.fori_loop(0, 32, one, 0)

    def weights():
        omega = jnp.where(x_lo == 0, phonon_ref[0:1, 0:1], phonon_ref[0:1, 1:2])
        bose = 1.0 / (jnp.exp(omega / thermal) - 1.0)
        scale = (math.pi / 32.0) * (broadening / math.pi) / (2.0 * omega)

        def one(i, carry):
            there = energy_col[pl.ds(pl.multiple_of(i * 40, 8), 40), :]
            here = energy_row[pl.ds(i, 1), :]
            filling = 1.0 / (1.0 + jnp.exp(there / thermal))
            spacing = here - there
            plus = spacing + omega
            minus = spacing - omega
            wide = broadening * broadening
            weight[pl.ds(pl.multiple_of(i * 40, 8), 40), :] = scale * (
                (bose + filling) / (plus * plus + wide)
                + (bose + 1.0 - filling) / (minus * minus + wide)
            )
            return carry

        lax.fori_loop(0, 32, one, 0)

    def electron_phases():
        lane4 = iota((128, 128), 1)
        place = lane4 >> 4
        ahead = (place + 1) >> 1
        source = (y + 8 + jnp.where(place & 1 == 1, ahead, -ahead)) & 7
        e_of_lane = (source * 2 + ((x_lo + (lane4 >> 3)) & 1)) * 4 + (lane4 & 3)
        row4 = iota((128, 128), 0)
        match = (row4 & 63) == e_of_lane
        sine = row4 >> 6
        imag = (lane4 >> 2) & 1
        to_real = jnp.where(match & (sine == imag), jnp.where(sine == 1, -1.0, 1.0), 0.0)
        to_im = jnp.where(match & (sine != imag), 1.0, 0.0)
        for b in (0, 1):
            table = packs[b, 128:144, 0:128]
            mix[b * 16 : b * 16 + 16, :] = mm(table, to_real.astype(BF)).astype(BF)
            mix[32 + b * 16 : 48 + b * 16, :] = mm(table, to_im.astype(BF)).astype(BF)

    rotations_here()
    electron_phases()

    for copy in u_copies:
        copy.wait_recv()
    u_swap = remote(u_in.at[x_lo], u_in.at[x_lo], swap_s, swap_r, rp, flip_re(1))
    for copy in pieces.values():
        copy.wait_recv()
    own_row = (z * 2 + x_hi) * 16 + x_lo * 8
    blocks = []
    for dl in (0, 1):
        added = None
        for dx in (0, 1):
            for place in range(5):
                if dl == 0 and dx == 0 and place == 0:
                    continue
                piece = l_piece[dl, dx, place].astype(F32)
                added = piece if added is None else added + piece
        block = jnp.concatenate([added[0:8], added[8:16, 0 : LANES - HALF]], axis=1)
        if dl == 0:
            block = block + part[pl.ds(pl.multiple_of(own_row, 8), 8), :]
        blocks.append(block)
    waves[0] = jnp.concatenate(blocks, axis=0).astype(BF)

    first = {}
    for place, step in ((2, 1), (1, -1), (4, 2), (3, -2)):
        first[place] = remote(
            waves.at[0], waves.at[place], y1_s.at[place], y1_r.at[place], rp, along_y(step)
        )
    first[2].wait_recv()
    later = [remote(waves.at[2], waves.at[6], y2_s.at[0], y2_r.at[0], rp, along_y(2))]
    first[1].wait_recv()
    later.append(remote(waves.at[1], waves.at[5], y2_s.at[1], y2_r.at[1], rp, along_y(-2)))
    lower = pl.ds(0, HALF)
    upper = pl.ds(HALF, LANES - HALF)
    first[4].wait_recv()
    later.append(
        remote(
            waves.at[4, :, lower],
            waves.at[7, :, lower],
            y2_s.at[2],
            y2_r.at[2],
            rp,
            along_y(2),
        )
    )
    first[3].wait_recv()
    later.append(
        remote(
            waves.at[3, :, upper],
            waves.at[7, :, upper],
            y2_s.at[3],
            y2_r.at[3],
            rp,
            along_y(-2),
        )
    )
    rotations_there()
    weights()
    points_c = mm(mix[:, 0:80], waves[0:5].reshape(80, LANES))
    for copy in later:
        copy.wait_recv()
    points_c = points_c + mm(mix[:, 80:128], waves[5:8].reshape(48, LANES))

    for a in range(40):
        cut = slice(a * 40, a * 40 + 40)
        coupling[pl.ds(a, 32, stride=40), :] = jnp.concatenate(
            [points_c[0:32, cut], points_c[32:64, cut], jnp.zeros((32, 48), F32)], axis=1
        )

    def some_points(group, carry):
        indices = [group * 8 + i for i in range(8)]
        spots = [pl.ds(pl.multiple_of(i * 40, 8), 40) for i in indices]
        turned = [
            mm(coupling[spot, 0:80].astype(BF), right_rot[i])
            for i, spot in zip(indices, spots, strict=True)
        ]
        stacked = [
            jnp.concatenate([t[:, 0:80], t[:, 128:208]], axis=0).astype(BF) for t in turned
        ]
        final = [
            mm(left_rot[i, 0:40, 0:80], s) for i, s in zip(indices, stacked, strict=True)
        ]
        sums = [
            jnp.sum(f * f * weight[spot, 0:80], axis=0, keepdims=True)
            for f, spot in zip(final, spots, strict=True)
        ]
        rates[pl.ds(pl.multiple_of(group * 8, 8), 8), 0:80] = jnp.concatenate(sums, axis=0)
        return carry

    lax.fori_loop(0, 4, some_points, 0)

    for b in (0, 1):
        rows = rates[b * 16 : b * 16 + 16, 0:40] + rates[b * 16 : b * 16 + 16, 40:80]
        rates_b[b] = jnp.concatenate([rows[0:8], rows[8:16], jnp.zeros((8, 48), F32)], axis=1)
    c_copies = []
    for dx in (1, 0):
        for dl in (1, 0):
            for dc in (1, 0):
                spot = dx * 4 + dc * 2 + dl
                if spot == 0:
                    continue
                copy = remote(
                    rates_b.at[(x_lo + dl) % 2],
                    land_c.at[spot],
                    rc_s.at[spot],
                    rc_r.at[spot],
                    flip_rp(dx, dc),
                    flip_re(dl),
                )
                c_copies.append((spot, copy))
    summed = rates_b[x_lo]
    for spot, copy in reversed(c_copies):
        copy.wait_recv()
        summed = summed + land_c[spot]
    rates_z[...] = summed
    z_copies = []
    for step in (4, 3, 5, 2, 6, 1, 7):
        copy = remote(
            rates_z, land_z.at[step], rz_s.at[step], rz_r.at[step], along_z(step), re
        )
        z_copies.append((step, copy))
    for step, copy in reversed(z_copies):
        copy.wait_recv()
        summed = summed + land_z[step]
    out_ref[0:8, :] = summed[:, 0:40]
    out_ref[8:16, :] = summed[:, 40:80]

    for copy in started:
        copy.wait_send()


def per_device(
    wannier_coupling,
    phonon_lattice,
    phonon_degeneracy,
    electron_lattice,
    electron_degeneracy,
    phonon_wavevectors,
    electron_wavevectors,
    phonon_energies,
    bloch_rotations,
    band_energies,
    shifted_points,
):
    def vm(shape, dtype):
        return pltpu.VMEM(shape, dtype)

    def dma(*shape):
        return pltpu.SemaphoreType.DMA(shape)

    return pl.pallas_call(
        kernel,
        out_shape=jax.ShapeDtypeStruct((16, 40), F32),
        in_specs=[pl.BlockSpec(memory_space=pl.ANY)] * 11,
        out_specs=pl.BlockSpec(memory_space=pltpu.VMEM),
        scratch_shapes=[
            vm((4, 4, 6400), BF),
            vm((4, 3), jnp.int32),
            vm((1, 4), jnp.int32),
            vm((3, 64), jnp.int32),
            vm((1, 64), jnp.int32),
            vm((3, 32), F32),
            vm((3, 16), F32),
            vm((1, 2), F32),
            vm((16, 3200), F32),
            vm((16, 40), F32),
            vm((1, 256), jnp.int32),
            vm((64, LANES), BF),
            vm((64, LANES), BF),
            vm((32, 128), BF),
            vm((32, 128), BF),
            vm((256, 128), BF),
            vm((256, 128), BF),
            vm((256, 128), BF),
            vm((16, 16), jnp.int32),
            vm((4, 128, 128), F32),
            vm((144, PACK), BF),
            vm((2, 144, PACK), BF),
            vm((8, 2, 16, PACK), BF),
            vm((2, 8, 2, 16, PACK), BF),
            vm((256, LANES), F32),
            vm((2, 2, 16, LANES), BF),
            vm((2, 2, 16, LANES), BF),
            vm((2, 16, LANES), BF),
            vm((2, 16, LANES), BF),
            vm((2, 2, 5, 16, HALF), BF),
            vm((2, 2, 5, 16, HALF), BF),
            vm((8, 16, LANES), BF),
            vm((64, 128), BF),
            vm((2560, 128), F32),
            vm((2560, 128), F32),
            vm((32, 80, 256), BF),
            vm((32, 48, 128), BF),
            vm((1280, 128), F32),
            vm((32, 128), F32),
            vm((1280, 128), F32),
            vm((1280, 128), F32),
            vm((32, 128), F32),
            vm((2, 8, 128), F32),
            vm((8, 8, 128), F32),
            vm((8, 128), F32),
            vm((8, 8, 128), F32),
            dma(11),
            dma(2),
            dma(2),
            pltpu.SemaphoreType.DMA,
            pltpu.SemaphoreType.DMA,
            dma(8),
            dma(8),
            dma(2, 2),
            dma(2, 2),
            dma(2),
            dma(2),
            dma(2, 2, 5),
            dma(2, 2, 5),
            pltpu.SemaphoreType.DMA,
            pltpu.SemaphoreType.DMA,
            dma(5),
            dma(5),
            dma(4),
            dma(4),
            dma(8),
            dma(8),
            dma(8),
            dma(8),
        ],
        compiler_params=pltpu.CompilerParams(
            collective_id=0, has_side_effects=True, vmem_limit_bytes=60 * 1024 * 1024
        ),
        cost_estimate=pl.CostEstimate(
            flops=300_000_000, bytes_accessed=2_000_000, transcendentals=200_000
        ),
    )(
        wannier_coupling,
        phonon_lattice,
        phonon_degeneracy.reshape(1, 4),
        electron_lattice.T,
        electron_degeneracy.reshape(1, 64),
        phonon_wavevectors.T,
        electron_wavevectors.T,
        phonon_energies,
        bloch_rotations,
        band_energies,
        shifted_points,
    )


def solution(mesh):
    in_specs = (
        P("re", "rp", None),
        P("rp", None),
        P("rp"),
        P(),
        P(),
        P(),
        P("re", None),
        P("rp", None),
        P("re", None),
        P("re", None),
        P("rp", None),
    )
    return jax.shard_map(
        per_device, mesh=mesh, in_specs=in_specs, out_specs=P("re", None), check_vma=False
    )
```

```python
import math

import jax
import jax.numpy as jnp
from jax import lax
from jax.experimental import pallas as pl
from jax.experimental.pallas import tpu as pltpu
from jax.sharding import PartitionSpec as P

NW = 40
MODES = 2
ROW = 1600
LANES = 1664
PACK = 512
MESH = pl.DeviceIdType.MESH
BF = jnp.bfloat16
F32 = jnp.float32

full_turn = 2.0 * math.pi
thermal = 0.025
broadening = 0.05
highest = lax.Precision.HIGHEST


def three_parts(values):
    high = values.astype(BF).astype(F32)
    rest = values - high
    middle = rest.astype(BF).astype(F32)
    return high, middle, rest - middle


def iota(shape, axis):
    return lax.broadcasted_iota(jnp.int32, shape, axis)


def mm(left, right):
    return jnp.dot(left, right, preferred_element_type=F32)


def outer(left, right):
    return lax.dot_general(
        left, right, (((0,), (0,)), ((), ())), precision=highest, preferred_element_type=F32
    )


LANE_TILES = [(start, min(start + 256, LANES)) for start in range(0, LANES, 256)]
HALF = 896


def kernel(
    w_hbm,
    plat_hbm,
    pdeg_hbm,
    elat_hbm,
    edeg_hbm,
    qvec_hbm,
    kvec_hbm,
    phonon_hbm,
    rot_hbm,
    band_hbm,
    shift_hbm,
    out_ref,
    w_ref,
    plat_ref,
    pdeg_ref,
    elat_ref,
    edeg_ref,
    qvec_ref,
    kvec_ref,
    phonon_ref,
    rot_ref,
    band_ref,
    shift_ref,
    w_own,
    w_sib,
    cosw,
    sinw,
    lhs_own,
    lhs_out,
    lhs_sib,
    points_ref,
    pack_f,
    pack,
    packs,
    u_out,
    u_in,
    part,
    s_far,
    l_far,
    s_opp,
    l_opp,
    s_piece,
    l_piece,
    waves,
    mix,
    turn_a,
    turn_b,
    right_rot,
    left_rot,
    energy_col,
    energy_row,
    length_row,
    weight,
    coupling,
    rates,
    rates_b,
    land_c,
    rates_z,
    land_z,
    in_s,
    core_s,
    core_r,
    pack_s,
    pack_r,
    u_s,
    u_r,
    far_s,
    far_r,
    opp_s,
    opp_r,
    piece_s,
    piece_r,
    swap_s,
    swap_r,
    y1_s,
    y1_r,
    y2_s,
    y2_r,
    rc_s,
    rc_r,
    rz_s,
    rz_r,
):
    rp = lax.axis_index("rp")
    re = lax.axis_index("re")
    z = rp // 4
    x_hi = (rp // 2) % 2
    core = rp % 2
    y = re // 2
    x_lo = re % 2

    def flip_rp(dx, dc, step=0):
        hi = (1 - x_hi) if dx else x_hi
        co = (1 - core) if dc else core
        return ((z + 8 + step) % 8) * 4 + hi * 2 + co

    def flip_re(dl):
        return y * 2 + ((1 - x_lo) if dl else x_lo)

    def along_z(step):
        return (rp + 32 + 4 * step) % 32

    def along_y(step):
        return (re + 16 + 2 * step) % 16

    loads = {}

    def load(name, src, dst, number):
        loads[name] = pltpu.make_async_copy(src, dst, in_s.at[number])
        loads[name].start()

    for e in range(4):
        load(f"w{e}", w_hbm.at[e], w_ref.at[e], e)

    def loaded(*names):
        for name in names:
            loads[name].wait()

    started = []

    def remote(src, dst, send, recv, to_rp, to_re):
        copy = pltpu.make_async_remote_copy(
            src_ref=src,
            dst_ref=dst,
            send_sem=send,
            recv_sem=recv,
            device_id={"rp": to_rp, "re": to_re},
            device_id_type=MESH,
        )
        copy.start()
        started.append(copy)
        return copy

    partners = []
    for step in (4, 3, -3, 2, -2, 1, -1):
        partners += [(rp, along_y(step)), (along_z(step), re)]
        if abs(step) < 3:
            partners += [
                (flip_rp(dx, 0, step), flip_re(dl)) for dx, dl in ((1, 1), (1, 0), (0, 1))
            ]
    partners += [
        (flip_rp(dx, dc), flip_re(dl))
        for dc in (0, 1)
        for dx in (1, 0)
        for dl in (1, 0)
        if dx or dc or dl
    ]
    barrier = pltpu.get_barrier_semaphore()
    for to_rp, to_re in partners:
        pl.semaphore_signal(
            barrier, inc=1, device_id={"rp": to_rp, "re": to_re}, device_id_type=MESH
        )

    for number, (name, src, dst) in enumerate(
        (
            ("plat", plat_hbm, plat_ref),
            ("pdeg", pdeg_hbm, pdeg_ref),
            ("qvec", qvec_hbm, qvec_ref),
            ("elat", elat_hbm, elat_ref),
            ("edeg", edeg_hbm, edeg_ref),
            ("kvec", kvec_hbm, kvec_ref),
            ("phonon", phonon_hbm, phonon_ref),
            ("rot", rot_hbm, rot_ref),
            ("band", band_hbm, band_ref),
            ("shift", shift_hbm, shift_ref),
        )
    ):
        load(name, src, dst, 4 + number)

    loaded("w0", "w1", "w2", "w3")
    cells = jnp.concatenate([w_ref[e].astype(F32) for e in range(4)], axis=0)
    for mc in range(4):
        w_own[mc * 16 : mc * 16 + 16, :] = jnp.concatenate(
            [cells[:, mc * ROW : (mc + 1) * ROW], jnp.zeros((16, LANES - ROW), F32)], axis=1
        ).astype(BF)

    pl.semaphore_wait(barrier, len(partners))

    sib = flip_rp(0, 1)
    core_copies = [remote(w_own, w_sib, core_s.at[0], core_r.at[0], sib, re)]

    loaded("plat", "pdeg", "qvec")
    r_of_lane = jnp.where(iota((4, 128), 0) == (iota((4, 128), 1) & 3), 1.0, 0.0).astype(F32)
    p_angle = full_turn * outer(qvec_ref[...], outer(plat_ref[...].astype(F32), r_of_lane))
    p_weight = 1.0 / jnp.dot(
        pdeg_ref[...].astype(F32), r_of_lane, precision=highest, preferred_element_type=F32
    )
    cosw[...] = (jnp.cos(p_angle) * p_weight).astype(BF)
    sinw[...] = (jnp.sin(p_angle) * p_weight).astype(BF)
    row = iota((256, 128), 0)
    lane = iota((256, 128), 1)
    same = ((row >> 3) & 1 == (lane >> 5) & 1) & (row & 3 == (lane >> 2) & 3) & (lane < 64)
    to_imag = (row >> 2) & 1
    of_imag = (lane >> 4) & 1
    pick_cos = same & (to_imag == of_imag)
    pick_sin = same & (to_imag != of_imag)
    sign = jnp.where(to_imag == 1, 1.0, -1.0).astype(F32)
    q_row = iota((256, 32), 0)
    q_lane = iota((256, 32), 1)

    def phases_for(which_core):
        spread = jnp.where((q_row >> 4) * 2 + which_core == q_lane, 1.0, 0.0).astype(BF)
        cos_part = mm(spread, cosw[...])
        sin_part = mm(spread, sinw[...])
        return jnp.where(
            pick_cos, cos_part, jnp.where(pick_sin, sign * sin_part, 0.0)
        ).astype(BF)

    lhs_out[...] = phases_for(1 - core)

    core_copies.append(remote(lhs_out, lhs_sib, core_s.at[1], core_r.at[1], sib, re))
    lhs_own[...] = phases_for(core)
    for start, end in LANE_TILES:
        part[:, start:end] = mm(lhs_own[:, 0:64], w_own[:, start:end])
    for copy in core_copies:
        copy.wait_recv()
    for start, end in LANE_TILES:
        part[:, start:end] += mm(lhs_sib[:, 0:64], w_sib[:, start:end])

    def part_of(z_to, sub):
        hi = (1 - x_hi) if sub == 0 else x_hi
        block = ((z_to + 8) % 8) * 2 + hi
        return part[pl.ds(pl.multiple_of(block * 16, 16), 16), :]

    far = {}
    opp = {}
    for sub in (0, 1):
        toward = 2 if sub == 0 else -2
        s_opp[sub] = part_of(z + 4, sub).astype(BF)
        opp[sub] = remote(
            s_opp.at[sub], l_opp.at[sub], opp_s.at[sub], opp_r.at[sub], along_z(toward), re
        )
        for side, step in ((0, 1), (1, -1)):
            s_far[side, sub] = part_of(z + 3 * step, sub).astype(BF)
            far[side, sub] = remote(
                s_far.at[side, sub],
                l_far.at[side, sub],
                far_s.at[side, sub],
                far_r.at[side, sub],
                along_z(step),
                re,
            )

    def piece_of(z_to, dx, dl):
        hi = (1 - x_hi) if dx else x_hi
        mode = (x_lo + dl) % 2
        first_row = (((z_to + 8) % 8) * 2 + hi) * 16 + mode * 8
        rows = part[pl.ds(pl.multiple_of(first_row, 8), 8), :]
        end = jnp.concatenate([rows[:, HALF:], jnp.zeros((8, 2 * HALF - LANES), F32)], axis=1)
        return jnp.concatenate([rows[:, 0:HALF], end], axis=0).astype(BF)

    pieces = {}

    def send_piece(place, step, dx, dl):
        s_piece[dl, dx, place] = piece_of(z + step, dx, dl)
        pieces[dl, dx, place] = remote(
            s_piece.at[dl, dx, place],
            l_piece.at[dl, dx, place],
            piece_s.at[dl, dx, place],
            piece_r.at[dl, dx, place],
            flip_rp(dx, 0, step),
            flip_re(dl),
        )

    for dx, dl in ((1, 1), (1, 0), (0, 1), (0, 0)):
        for place, step in ((1, 1), (2, -1)):
            send_piece(place, step, dx, dl)
    for dx, dl in ((1, 1), (1, 0), (0, 1)):
        send_piece(0, 0, dx, dl)

    loaded("elat", "edeg", "kvec", "phonon", "rot", "band", "shift")
    e_angle = full_turn * outer(kvec_ref[...], elat_ref[...].astype(F32))
    e_weight = 1.0 / edeg_ref[...].astype(F32)
    high, middle, low = three_parts(band_ref[...])
    rest = jnp.zeros((16, PACK - 415), F32)
    for j in range(8):
        five = slice(j * 5, j * 5 + 5)
        eighth = jnp.concatenate(
            [rot_ref[:, j * 400 : j * 400 + 400], high[:, five], middle[:, five], low[:, five], rest],
            axis=1,
        )
        for v in range(4):
            pack_f[v, pl.ds(j, 16, stride=8), :] = eighth[:, v * 128 : v * 128 + 128]
    for v in range(4):
        pack[0:128, v * 128 : v * 128 + 128] = pack_f[v].astype(BF)
    exact = jnp.concatenate([pack_f[v] for v in range(4)], axis=1)
    kept = pack[0:128, :].astype(F32)
    took = (exact - kept) * (exact + kept)
    left = kept * kept
    took = sum(took[:, t * 40 : t * 40 + 40] for t in range(10)).reshape(16, 8, 40)
    left = sum(left[:, t * 40 : t * 40 + 40] for t in range(10)).reshape(16, 8, 40)
    took, left = jnp.sum(took, axis=1), jnp.sum(left, axis=1)
    short = jnp.where(left > 0.0, took / jnp.where(left > 0.0, left, 1.0), 0.0)
    gap = jnp.zeros((16, 48), F32)
    pack[128:144, :] = jnp.concatenate(
        [jnp.cos(e_angle) * e_weight, jnp.sin(e_angle) * e_weight]
        + [high, high, short, gap[:, 0:8], middle, middle, gap, low, low, gap],
        axis=1,
    ).astype(BF)
    pack_copy = remote(pack, packs.at[x_lo], pack_s, pack_r, rp, flip_re(1))

    for d in range(16):
        points_ref[d : d + 1, :] = shift_ref[:, d * 16 : d * 16 + 16]
    points = points_ref[...]
    mine = (points >> 4) == re
    inner = points & 15
    smaller = jnp.min(jnp.where(mine, inner, 99), axis=1, keepdims=True)
    larger = jnp.max(jnp.where(mine, inner, -1), axis=1, keepdims=True)
    both = jnp.where(iota((16, 128), 1) == 0, smaller, larger).astype(F32).astype(BF)
    spread16 = jnp.where((iota((256, 16), 0) >> 4) == iota((256, 16), 1), 1.0, 0.0).astype(BF)
    both_rows = mm(spread16, both)
    slot = (iota((256, 1), 0) >> 3) & 1
    chosen = jnp.where(slot == 0, both_rows[:, 0:1], both_rows[:, 1:2])
    take = ((lane >> 3).astype(F32) == chosen) & ((lane & 7) == (row & 7))
    take = jnp.where(take, 1.0, 0.0).astype(BF)
    u_out[...] = mm(take, pack[0:128, :]).astype(BF).reshape(8, 2, 16, PACK)
    u_copies = []
    for step in (4, 3, 5, 2, 6, 1, 7):
        u_copies.append(
            remote(
                u_out.at[(y + step) % 8],
                u_in.at[x_lo, y],
                u_s.at[step],
                u_r.at[step],
                rp,
                along_y(step),
            )
        )
    packs[x_lo] = pack[...]
    u_in[x_lo, y] = u_out[y]

    for sub in (0, 1):
        for side, step in ((0, 1), (1, -1)):
            far[side, sub].wait_recv()
            more = l_far[side, sub].astype(F32)
            if side == sub:
                opp[sub].wait_recv()
                more = more + l_opp[sub].astype(F32)
            hi = (1 - x_hi) if sub == 0 else x_hi
            block = ((z + 8 + 2 * step) % 8) * 2 + hi
            part[pl.ds(pl.multiple_of(block * 16, 16), 16), :] += more
            for dl in (1, 0):
                send_piece(3 + side, 2 * step, 1 - sub, dl)

    def swap_halves(rows):
        cut = rows.reshape(16, 8, PACK)
        return jnp.concatenate([cut[:, 4:8], cut[:, 0:4]], axis=1).reshape(128, PACK)

    def rotations_here():
        pack_copy.wait_recv()
        blank = jnp.zeros((128, 48), F32)
        for b in (0, 1):
            rows = packs[b, 0:128, :].astype(F32)
            swapped = swap_halves(rows)
            rows = rows * jnp.where((iota((128, 1), 0) >> 2) & 1 == 1, -1.0, 1.0)
            for t in range(10):
                cut = slice(t * 40, t * 40 + 40)
                spot = pl.ds(b * 1280 + t, 128, stride=10)
                turn_a[spot, :] = jnp.concatenate([rows[:, cut], swapped[:, cut], blank], axis=1)
                turn_b[spot, :] = jnp.concatenate([swapped[:, cut], -rows[:, cut], blank], axis=1)
            tail = packs[b, 128:144, :].astype(F32)
            energy_row[b * 16 : b * 16 + 16, :] = (
                tail[:, 128:256] + tail[:, 256:384] + tail[:, 384:512]
            )
            gain = 1.0 + tail[:, 208:248]
            length_row[b * 16 : b * 16 + 16, :] = jnp.concatenate(
                [gain, gain, jnp.zeros((16, 48), F32)], axis=1
            )

        def some(group, carry):
            for i in [group * 8 + member for member in range(8)]:
                spot = pl.ds(pl.multiple_of(i * 80, 8), 80)
                both = [turn_a[spot, :], turn_b[spot, :]]
                right_rot[i] = jnp.concatenate(both, axis=1).astype(BF)
            return carry

        lax.fori_loop(0, 4, some, 0)

    def rotations_there():
        u_swap.wait_recv()
        blank = jnp.zeros((128, 88), F32)
        for b in (0, 1):
            block = points_ref[pl.ds(y * 2 + b, 1), :]
            spot = iota((128, 16), 0) >> 3 == iota((128, 16), 1)
            wide = jnp.broadcast_to(block, (128, 16))
            target = jnp.sum(jnp.where(spot, wide, 0), axis=1, keepdims=True)
            before = ((wide >> 4) == (target >> 4)) & (wide < target)
            second = jnp.max(jnp.where(before, 1, 0), axis=1, keepdims=True)
            source = ((target >> 4) & 1) * 128 + (target >> 5) * 16 + second * 8
            source = source + (iota((128, 1), 0) & 7)
            order = jnp.where(iota((128, 256), 1) == source, 1.0, 0.0).astype(BF)
            rows = mm(order, u_in[:, :, b].reshape(256, PACK))
            for t in range(10):
                turn_a[pl.ds(b * 1280 + t, 128, stride=10), :] = jnp.concatenate(
                    [rows[:, t * 40 : t * 40 + 40], blank], axis=1
                )
            for t in range(5):
                energy = (
                    rows[:, 400 + t : 401 + t]
                    + rows[:, 405 + t : 406 + t]
                    + rows[:, 410 + t : 411 + t]
                )
                energy_col[pl.ds(b * 640 + t, 128, stride=5), :] = jnp.broadcast_to(
                    energy, (128, 128)
                )

        def some(group, carry):
            indices = [group * 8 + member for member in range(8)]
            spots = [pl.ds(pl.multiple_of(i * 80, 8), 80) for i in indices]
            turned = [jnp.transpose(turn_a[spot, :])[0:48, :].astype(BF) for spot in spots]
            for i, block in zip(indices, turned, strict=True):
                left_rot[i, :, 0:80] = block
            return carry

        lax.fori_loop(0, 4, some, 0)

    def weights():
        omega = jnp.where(x_lo == 0, phonon_ref[0:1, 0:1], phonon_ref[0:1, 1:2])
        bose = 1.0 / (jnp.exp(omega / thermal) - 1.0)
        scale = (math.pi / 32.0) * (broadening / math.pi) / (2.0 * omega)

        wide = broadening * broadening

        def some(group, carry):
            spots = [pl.ds(pl.multiple_of((group * 8 + i) * 40, 8), 40) for i in range(8)]
            rows = energy_row[pl.ds(pl.multiple_of(group * 8, 8), 8), :]
            gains = scale * length_row[pl.ds(pl.multiple_of(group * 8, 8), 8), :]
            found = []
            for i, spot in enumerate(spots):
                there = energy_col[spot, :]
                filling = 1.0 / (1.0 + jnp.exp(there / thermal))
                spacing = rows[i : i + 1, :] - there
                plus = spacing + omega
                minus = spacing - omega
                found.append(
                    gains[i : i + 1, :]
                    * (
                        (bose + filling) / (plus * plus + wide)
                        + (bose + 1.0 - filling) / (minus * minus + wide)
                    )
                )
            for spot, value in zip(spots, found, strict=True):
                weight[spot, :] = value
            return carry

        lax.fori_loop(0, 4, some, 0)

    def electron_phases():
        lane4 = iota((128, 128), 1)
        place = lane4 >> 4
        ahead = (place + 1) >> 1
        source = (y + 8 + jnp.where(place & 1 == 1, ahead, -ahead)) & 7
        e_of_lane = (source * 2 + ((x_lo + (lane4 >> 3)) & 1)) * 4 + (lane4 & 3)
        row4 = iota((128, 128), 0)
        match = (row4 & 63) == e_of_lane
        sine = row4 >> 6
        imag = (lane4 >> 2) & 1
        to_real = jnp.where(match & (sine == imag), jnp.where(sine == 1, -1.0, 1.0), 0.0)
        to_im = jnp.where(match & (sine != imag), 1.0, 0.0)
        for b in (0, 1):
            table = packs[b, 128:144, 0:128]
            mix[b * 16 : b * 16 + 16, :] = mm(table, to_real.astype(BF)).astype(BF)
            mix[32 + b * 16 : 48 + b * 16, :] = mm(table, to_im.astype(BF)).astype(BF)

    rotations_here()
    electron_phases()

    for copy in u_copies:
        copy.wait_recv()
    u_swap = remote(u_in.at[x_lo], u_in.at[x_lo], swap_s, swap_r, rp, flip_re(1))
    for copy in pieces.values():
        copy.wait_recv()
    own_row = (z * 2 + x_hi) * 16 + x_lo * 8
    blocks = []
    for dl in (0, 1):
        added = None
        for dx in (0, 1):
            for place in range(5):
                if dl == 0 and dx == 0 and place == 0:
                    continue
                piece = l_piece[dl, dx, place].astype(F32)
                added = piece if added is None else added + piece
        block = jnp.concatenate([added[0:8], added[8:16, 0 : LANES - HALF]], axis=1)
        if dl == 0:
            block = block + part[pl.ds(pl.multiple_of(own_row, 8), 8), :]
        blocks.append(block)
    waves[0] = jnp.concatenate(blocks, axis=0).astype(BF)

    first = {}
    for place, step in ((2, 1), (1, -1), (4, 2), (3, -2)):
        first[place] = remote(
            waves.at[0], waves.at[place], y1_s.at[place], y1_r.at[place], rp, along_y(step)
        )
    first[2].wait_recv()
    later = [remote(waves.at[2], waves.at[6], y2_s.at[0], y2_r.at[0], rp, along_y(2))]
    first[1].wait_recv()
    later.append(remote(waves.at[1], waves.at[5], y2_s.at[1], y2_r.at[1], rp, along_y(-2)))
    lower = pl.ds(0, HALF)
    upper = pl.ds(HALF, LANES - HALF)
    first[4].wait_recv()
    later.append(
        remote(
            waves.at[4, :, lower],
            waves.at[7, :, lower],
            y2_s.at[2],
            y2_r.at[2],
            rp,
            along_y(2),
        )
    )
    first[3].wait_recv()
    later.append(
        remote(
            waves.at[3, :, upper],
            waves.at[7, :, upper],
            y2_s.at[3],
            y2_r.at[3],
            rp,
            along_y(-2),
        )
    )
    rotations_there()
    weights()
    points_c = mm(mix[:, 0:80], waves[0:5].reshape(80, LANES))
    for copy in later:
        copy.wait_recv()
    points_c = points_c + mm(mix[:, 80:128], waves[5:8].reshape(48, LANES))

    for a in range(40):
        cut = slice(a * 40, a * 40 + 40)
        coupling[pl.ds(a, 32, stride=40), :] = jnp.concatenate(
            [points_c[0:32, cut], points_c[32:64, cut], jnp.zeros((32, 48), F32)], axis=1
        )

    def some_points(group, carry):
        indices = [group * 16 + i for i in range(16)]
        spots = [pl.ds(pl.multiple_of(i * 40, 8), 40) for i in indices]
        turned = [
            mm(coupling[spot, 0:80].astype(BF), right_rot[i])
            for i, spot in zip(indices, spots, strict=True)
        ]
        stacked = [
            jnp.concatenate([t[:, 0:80], t[:, 128:208]], axis=0).astype(BF) for t in turned
        ]
        final = [
            mm(left_rot[i, 0:40, 0:80], s) for i, s in zip(indices, stacked, strict=True)
        ]
        sums = [
            jnp.sum(f * f * weight[spot, 0:80], axis=0, keepdims=True)
            for f, spot in zip(final, spots, strict=True)
        ]
        rates[pl.ds(pl.multiple_of(group * 16, 8), 16), 0:80] = jnp.concatenate(sums, axis=0)
        return carry

    rates[...] = jnp.zeros((32, 128), F32)
    c_copies = []
    for dl in (0, 1):
        b = (x_lo + dl) % 2
        some_points(b, 0)
        rows = rates[pl.ds(pl.multiple_of(b * 16, 16), 16), :]
        rows = rows[:, 0:40] + rows[:, 40:80]
        rates_b[b] = jnp.concatenate([rows[0:8], rows[8:16], jnp.zeros((8, 48), F32)], axis=1)
        for dx in (1, 0):
            for dc in (1, 0):
                spot = dx * 4 + dc * 2 + dl
                if spot == 0:
                    continue
                copy = remote(
                    rates_b.at[b],
                    land_c.at[spot],
                    rc_s.at[spot],
                    rc_r.at[spot],
                    flip_rp(dx, dc),
                    flip_re(dl),
                )
                c_copies.append((spot, copy))
    summed = rates_b[x_lo]
    for spot, copy in reversed(c_copies):
        copy.wait_recv()
        summed = summed + land_c[spot]
    rates_z[...] = summed
    z_copies = []
    for step in (4, 3, 5, 2, 6, 1, 7):
        copy = remote(
            rates_z, land_z.at[step], rz_s.at[step], rz_r.at[step], along_z(step), re
        )
        z_copies.append((step, copy))
    for step, copy in reversed(z_copies):
        copy.wait_recv()
        summed = summed + land_z[step]
    out_ref[0:8, :] = summed[:, 0:40]
    out_ref[8:16, :] = summed[:, 40:80]

    for copy in started:
        copy.wait_send()


def per_device(
    wannier_coupling,
    phonon_lattice,
    phonon_degeneracy,
    electron_lattice,
    electron_degeneracy,
    phonon_wavevectors,
    electron_wavevectors,
    phonon_energies,
    bloch_rotations,
    band_energies,
    shifted_points,
):
    def vm(shape, dtype):
        return pltpu.VMEM(shape, dtype)

    def dma(*shape):
        return pltpu.SemaphoreType.DMA(shape)

    return pl.pallas_call(
        kernel,
        out_shape=jax.ShapeDtypeStruct((16, 40), F32),
        in_specs=[pl.BlockSpec(memory_space=pl.ANY)] * 11,
        out_specs=pl.BlockSpec(memory_space=pltpu.VMEM),
        scratch_shapes=[
            vm((4, 4, 6400), BF),
            vm((4, 3), jnp.int32),
            vm((1, 4), jnp.int32),
            vm((3, 64), jnp.int32),
            vm((1, 64), jnp.int32),
            vm((3, 32), F32),
            vm((3, 16), F32),
            vm((1, 2), F32),
            vm((16, 3200), F32),
            vm((16, 40), F32),
            vm((1, 256), jnp.int32),
            vm((64, LANES), BF),
            vm((64, LANES), BF),
            vm((32, 128), BF),
            vm((32, 128), BF),
            vm((256, 128), BF),
            vm((256, 128), BF),
            vm((256, 128), BF),
            vm((16, 16), jnp.int32),
            vm((4, 128, 128), F32),
            vm((144, PACK), BF),
            vm((2, 144, PACK), BF),
            vm((8, 2, 16, PACK), BF),
            vm((2, 8, 2, 16, PACK), BF),
            vm((256, LANES), F32),
            vm((2, 2, 16, LANES), BF),
            vm((2, 2, 16, LANES), BF),
            vm((2, 16, LANES), BF),
            vm((2, 16, LANES), BF),
            vm((2, 2, 5, 16, HALF), BF),
            vm((2, 2, 5, 16, HALF), BF),
            vm((8, 16, LANES), BF),
            vm((64, 128), BF),
            vm((2560, 128), F32),
            vm((2560, 128), F32),
            vm((32, 80, 256), BF),
            vm((32, 48, 128), BF),
            vm((1280, 128), F32),
            vm((32, 128), F32),
            vm((32, 128), F32),
            vm((1280, 128), F32),
            vm((1280, 128), F32),
            vm((32, 128), F32),
            vm((2, 8, 128), F32),
            vm((8, 8, 128), F32),
            vm((8, 128), F32),
            vm((8, 8, 128), F32),
            dma(14),
            dma(2),
            dma(2),
            pltpu.SemaphoreType.DMA,
            pltpu.SemaphoreType.DMA,
            dma(8),
            dma(8),
            dma(2, 2),
            dma(2, 2),
            dma(2),
            dma(2),
            dma(2, 2, 5),
            dma(2, 2, 5),
            pltpu.SemaphoreType.DMA,
            pltpu.SemaphoreType.DMA,
            dma(5),
            dma(5),
            dma(4),
            dma(4),
            dma(8),
            dma(8),
            dma(8),
            dma(8),
        ],
        compiler_params=pltpu.CompilerParams(
            collective_id=0, has_side_effects=True, vmem_limit_bytes=60 * 1024 * 1024
        ),
        cost_estimate=pl.CostEstimate(
            flops=300_000_000, bytes_accessed=2_000_000, transcendentals=200_000
        ),
    )(
        wannier_coupling,
        phonon_lattice,
        phonon_degeneracy.reshape(1, 4),
        electron_lattice.T,
        electron_degeneracy.reshape(1, 64),
        phonon_wavevectors.T,
        electron_wavevectors.T,
        phonon_energies,
        bloch_rotations,
        band_energies,
        shifted_points,
    )


def solution(mesh):
    in_specs = (
        P("re", "rp", None),
        P("rp", None),
        P("rp"),
        P(),
        P(),
        P(),
        P("re", None),
        P("rp", None),
        P("re", None),
        P("re", None),
        P("rp", None),
    )
    return jax.shard_map(
        per_device, mesh=mesh, in_specs=in_specs, out_specs=P("re", None), check_vma=False
    )
```

```python
import math

import jax
import jax.numpy as jnp
from jax import lax
from jax.experimental import pallas as pl
from jax.experimental.pallas import tpu as pltpu
from jax.sharding import PartitionSpec as P

NW = 40
MODES = 2
ROW = 1600
LANES = 1664
PACK = 512
MESH = pl.DeviceIdType.MESH
BF = jnp.bfloat16
F32 = jnp.float32

full_turn = 2.0 * math.pi
thermal = 0.025
broadening = 0.05
highest = lax.Precision.HIGHEST


def three_parts(values):
    high = values.astype(BF).astype(F32)
    rest = values - high
    middle = rest.astype(BF).astype(F32)
    return high, middle, rest - middle


def iota(shape, axis):
    return lax.broadcasted_iota(jnp.int32, shape, axis)


def mm(left, right):
    return jnp.dot(left, right, preferred_element_type=F32)


def outer(left, right):
    return lax.dot_general(
        left, right, (((0,), (0,)), ((), ())), precision=highest, preferred_element_type=F32
    )


LANE_TILES = [(start, min(start + 256, LANES)) for start in range(0, LANES, 256)]
HALF = 896


def kernel(
    w_hbm,
    plat_hbm,
    pdeg_hbm,
    elat_hbm,
    edeg_hbm,
    qvec_hbm,
    kvec_hbm,
    phonon_hbm,
    rot_hbm,
    band_hbm,
    shift_hbm,
    out_ref,
    w_ref,
    plat_ref,
    pdeg_ref,
    elat_ref,
    edeg_ref,
    qvec_ref,
    kvec_ref,
    phonon_ref,
    rot_ref,
    band_ref,
    shift_ref,
    w_both,
    cosw,
    sinw,
    lhs_own,
    lhs_out,
    lhs_sib,
    points_ref,
    pack_f,
    pack,
    packs,
    u_out,
    u_in,
    part,
    s_far,
    l_far,
    s_opp,
    l_opp,
    s_piece,
    l_piece,
    waves,
    mix,
    turn_a,
    turn_b,
    right_rot,
    left_rot,
    energy_col,
    energy_row,
    length_row,
    weight,
    coupling,
    rates,
    rates_b,
    land_c,
    rates_z,
    land_z,
    in_s,
    core_s,
    core_r,
    pack_s,
    pack_r,
    u_s,
    u_r,
    far_s,
    far_r,
    opp_s,
    opp_r,
    piece_s,
    piece_r,
    swap_s,
    swap_r,
    y1_s,
    y1_r,
    y2_s,
    y2_r,
    rc_s,
    rc_r,
    rz_s,
    rz_r,
):
    rp = lax.axis_index("rp")
    re = lax.axis_index("re")
    z = rp // 4
    x_hi = (rp // 2) % 2
    core = rp % 2
    y = re // 2
    x_lo = re % 2

    def flip_rp(dx, dc, step=0):
        hi = (1 - x_hi) if dx else x_hi
        co = (1 - core) if dc else core
        return ((z + 8 + step) % 8) * 4 + hi * 2 + co

    def flip_re(dl):
        return y * 2 + ((1 - x_lo) if dl else x_lo)

    def along_z(step):
        return (rp + 32 + 4 * step) % 32

    def along_y(step):
        return (re + 16 + 2 * step) % 16

    loads = {}

    def load(name, src, dst, number):
        loads[name] = pltpu.make_async_copy(src, dst, in_s.at[number])
        loads[name].start()

    for e in range(4):
        load(f"w{e}", w_hbm.at[e], w_ref.at[e], e)

    def loaded(*names):
        for name in names:
            loads[name].wait()

    started = []

    def remote(src, dst, send, recv, to_rp, to_re):
        copy = pltpu.make_async_remote_copy(
            src_ref=src,
            dst_ref=dst,
            send_sem=send,
            recv_sem=recv,
            device_id={"rp": to_rp, "re": to_re},
            device_id_type=MESH,
        )
        copy.start()
        started.append(copy)
        return copy

    partners = []
    for step in (4, 3, -3, 2, -2, 1, -1):
        partners += [(rp, along_y(step)), (along_z(step), re)]
        if abs(step) < 3:
            partners += [
                (flip_rp(dx, 0, step), flip_re(dl)) for dx, dl in ((1, 1), (1, 0), (0, 1))
            ]
    partners += [
        (flip_rp(dx, dc), flip_re(dl))
        for dc in (0, 1)
        for dx in (1, 0)
        for dl in (1, 0)
        if dx or dc or dl
    ]
    barrier = pltpu.get_barrier_semaphore()
    for to_rp, to_re in partners:
        pl.semaphore_signal(
            barrier, inc=1, device_id={"rp": to_rp, "re": to_re}, device_id_type=MESH
        )

    for number, (name, src, dst) in enumerate(
        (
            ("plat", plat_hbm, plat_ref),
            ("pdeg", pdeg_hbm, pdeg_ref),
            ("qvec", qvec_hbm, qvec_ref),
            ("elat", elat_hbm, elat_ref),
            ("edeg", edeg_hbm, edeg_ref),
            ("kvec", kvec_hbm, kvec_ref),
            ("phonon", phonon_hbm, phonon_ref),
            ("rot", rot_hbm, rot_ref),
            ("band", band_hbm, band_ref),
            ("shift", shift_hbm, shift_ref),
        )
    ):
        load(name, src, dst, 4 + number)

    loaded("w0", "w1", "w2", "w3")
    cells = jnp.concatenate([w_ref[e].astype(F32) for e in range(4)], axis=0)
    for mc in range(4):
        w_both[mc * 16 : mc * 16 + 16, :] = jnp.concatenate(
            [cells[:, mc * ROW : (mc + 1) * ROW], jnp.zeros((16, LANES - ROW), F32)], axis=1
        ).astype(BF)

    pl.semaphore_wait(barrier, len(partners))

    sib = flip_rp(0, 1)
    core_copies = [
        remote(
            w_both.at[0:64], w_both.at[64:128], core_s.at[0], core_r.at[0], sib, re
        )
    ]

    loaded("plat", "pdeg", "qvec")
    r_of_lane = jnp.where(iota((4, 128), 0) == (iota((4, 128), 1) & 3), 1.0, 0.0).astype(F32)
    p_angle = full_turn * outer(qvec_ref[...], outer(plat_ref[...].astype(F32), r_of_lane))
    p_weight = 1.0 / jnp.dot(
        pdeg_ref[...].astype(F32), r_of_lane, precision=highest, preferred_element_type=F32
    )
    cosw[...] = (jnp.cos(p_angle) * p_weight).astype(BF)
    sinw[...] = (jnp.sin(p_angle) * p_weight).astype(BF)
    row = iota((256, 128), 0)
    lane = iota((256, 128), 1)
    same = ((row >> 3) & 1 == (lane >> 5) & 1) & (row & 3 == (lane >> 2) & 3)
    to_imag = (row >> 2) & 1
    of_imag = (lane >> 4) & 1
    pick_cos = same & (to_imag == of_imag)
    pick_sin = same & (to_imag != of_imag)
    sign = jnp.where(to_imag == 1, 1.0, -1.0).astype(F32)
    q_row = iota((256, 32), 0)
    q_lane = iota((256, 32), 1)

    def phases_for(which_core, lanes):
        spread = jnp.where((q_row >> 4) * 2 + which_core == q_lane, 1.0, 0.0).astype(BF)
        cos_part = mm(spread, cosw[...])
        sin_part = mm(spread, sinw[...])
        return jnp.where(
            pick_cos & lanes, cos_part, jnp.where(pick_sin & lanes, sign * sin_part, 0.0)
        ).astype(BF)

    lhs_out[...] = phases_for(1 - core, lane >= 64)

    core_copies.append(remote(lhs_out, lhs_sib, core_s.at[1], core_r.at[1], sib, re))
    lhs_own[...] = phases_for(core, lane < 64)
    for copy in core_copies:
        copy.wait_recv()
    lhs_own[...] += lhs_sib[...]

    def lhs_of(z_to, sub):
        hi = (1 - x_hi) if sub == 0 else x_hi
        block = ((z_to + 8) % 8) * 2 + hi
        return lhs_own[pl.ds(pl.multiple_of(block * 16, 16), 16), :]

    outer_lhs = jnp.concatenate([lhs_of(z + s, sub) for s in (4, 3, -3) for sub in (0, 1)], axis=0)
    for start, end in LANE_TILES:
        block = mm(outer_lhs, w_both[:, start:end]).astype(BF)
        for sub in (0, 1):
            s_opp[sub, :, start:end] = block[sub * 16 : sub * 16 + 16]
            s_far[0, sub, :, start:end] = block[32 + sub * 16 : 48 + sub * 16]
            s_far[1, sub, :, start:end] = block[64 + sub * 16 : 80 + sub * 16]
    far = {}
    opp = {}
    for sub in (0, 1):
        toward = 2 if sub == 0 else -2
        opp[sub] = remote(
            s_opp.at[sub], l_opp.at[sub], opp_s.at[sub], opp_r.at[sub], along_z(toward), re
        )
        for side, step in ((0, 1), (1, -1)):
            far[side, sub] = remote(
                s_far.at[side, sub],
                l_far.at[side, sub],
                far_s.at[side, sub],
                far_r.at[side, sub],
                along_z(step),
                re,
            )
    inner_lhs = jnp.concatenate(
        [lhs_of(z + s, sub) for s in (0, 1, -1, 2, -2) for sub in (0, 1)], axis=0
    )
    for start, end in LANE_TILES:
        part[:, start:end] = mm(inner_lhs, w_both[:, start:end])

    def piece_of(place, dx, dl):
        first_row = place * 32 + (1 - dx) * 16 + ((x_lo + dl) % 2) * 8
        rows = part[pl.ds(pl.multiple_of(first_row, 8), 8), :]
        end = jnp.concatenate([rows[:, HALF:], jnp.zeros((8, 2 * HALF - LANES), F32)], axis=1)
        return jnp.concatenate([rows[:, 0:HALF], end], axis=0).astype(BF)

    pieces = {}

    def send_piece(place, step, dx, dl):
        s_piece[dl, dx, place] = piece_of(place, dx, dl)
        pieces[dl, dx, place] = remote(
            s_piece.at[dl, dx, place],
            l_piece.at[dl, dx, place],
            piece_s.at[dl, dx, place],
            piece_r.at[dl, dx, place],
            flip_rp(dx, 0, step),
            flip_re(dl),
        )

    for dx, dl in ((1, 1), (1, 0), (0, 1), (0, 0)):
        for place, step in ((1, 1), (2, -1)):
            send_piece(place, step, dx, dl)
    for dx, dl in ((1, 1), (1, 0), (0, 1)):
        send_piece(0, 0, dx, dl)

    loaded("elat", "edeg", "kvec", "phonon", "rot", "band", "shift")
    e_angle = full_turn * outer(kvec_ref[...], elat_ref[...].astype(F32))
    e_weight = 1.0 / edeg_ref[...].astype(F32)
    high, middle, low = three_parts(band_ref[...])
    rest = jnp.zeros((16, PACK - 415), F32)
    for j in range(8):
        five = slice(j * 5, j * 5 + 5)
        eighth = jnp.concatenate(
            [rot_ref[:, j * 400 : j * 400 + 400], high[:, five], middle[:, five], low[:, five], rest],
            axis=1,
        )
        for v in range(4):
            pack_f[v, pl.ds(j, 16, stride=8), :] = eighth[:, v * 128 : v * 128 + 128]
    for v in range(4):
        pack[0:128, v * 128 : v * 128 + 128] = pack_f[v].astype(BF)
    exact = jnp.concatenate([pack_f[v] for v in range(4)], axis=1)
    kept = pack[0:128, :].astype(F32)
    took = (exact - kept) * (exact + kept)
    left = kept * kept
    took = sum(took[:, t * 40 : t * 40 + 40] for t in range(10)).reshape(16, 8, 40)
    left = sum(left[:, t * 40 : t * 40 + 40] for t in range(10)).reshape(16, 8, 40)
    took, left = jnp.sum(took, axis=1), jnp.sum(left, axis=1)
    short = jnp.where(left > 0.0, took / jnp.where(left > 0.0, left, 1.0), 0.0)
    gap = jnp.zeros((16, 48), F32)
    pack[128:144, :] = jnp.concatenate(
        [jnp.cos(e_angle) * e_weight, jnp.sin(e_angle) * e_weight]
        + [high, high, short, gap[:, 0:8], middle, middle, gap, low, low, gap],
        axis=1,
    ).astype(BF)
    pack_copy = remote(pack, packs.at[x_lo], pack_s, pack_r, rp, flip_re(1))

    for d in range(16):
        points_ref[d : d + 1, :] = shift_ref[:, d * 16 : d * 16 + 16]
    points = points_ref[...]
    mine = (points >> 4) == re
    inner = points & 15
    smaller = jnp.min(jnp.where(mine, inner, 99), axis=1, keepdims=True)
    larger = jnp.max(jnp.where(mine, inner, -1), axis=1, keepdims=True)
    both = jnp.where(iota((16, 128), 1) == 0, smaller, larger).astype(F32).astype(BF)
    spread16 = jnp.where((iota((256, 16), 0) >> 4) == iota((256, 16), 1), 1.0, 0.0).astype(BF)
    both_rows = mm(spread16, both)
    slot = (iota((256, 1), 0) >> 3) & 1
    chosen = jnp.where(slot == 0, both_rows[:, 0:1], both_rows[:, 1:2])
    take = ((lane >> 3).astype(F32) == chosen) & ((lane & 7) == (row & 7))
    take = jnp.where(take, 1.0, 0.0).astype(BF)
    u_out[...] = mm(take, pack[0:128, :]).astype(BF).reshape(8, 2, 16, PACK)
    u_copies = []
    for step in (4, 3, 5, 2, 6, 1, 7):
        u_copies.append(
            remote(
                u_out.at[(y + step) % 8],
                u_in.at[x_lo, y],
                u_s.at[step],
                u_r.at[step],
                rp,
                along_y(step),
            )
        )
    packs[x_lo] = pack[...]
    u_in[x_lo, y] = u_out[y]

    for sub in (0, 1):
        for side, step in ((0, 1), (1, -1)):
            far[side, sub].wait_recv()
            more = l_far[side, sub].astype(F32)
            if side == sub:
                opp[sub].wait_recv()
                more = more + l_opp[sub].astype(F32)
            first_row = (3 + side) * 32 + sub * 16
            part[first_row : first_row + 16, :] += more
            for dl in (1, 0):
                send_piece(3 + side, 2 * step, 1 - sub, dl)

    def swap_halves(rows):
        cut = rows.reshape(16, 8, PACK)
        return jnp.concatenate([cut[:, 4:8], cut[:, 0:4]], axis=1).reshape(128, PACK)

    def rotations_here():
        pack_copy.wait_recv()
        blank = jnp.zeros((128, 48), F32)
        for b in (0, 1):
            rows = packs[b, 0:128, :].astype(F32)
            swapped = swap_halves(rows)
            rows = rows * jnp.where((iota((128, 1), 0) >> 2) & 1 == 1, -1.0, 1.0)
            for t in range(10):
                cut = slice(t * 40, t * 40 + 40)
                spot = pl.ds(b * 1280 + t, 128, stride=10)
                turn_a[spot, :] = jnp.concatenate([rows[:, cut], swapped[:, cut], blank], axis=1)
                turn_b[spot, :] = jnp.concatenate([swapped[:, cut], -rows[:, cut], blank], axis=1)
            tail = packs[b, 128:144, :].astype(F32)
            energy_row[b * 16 : b * 16 + 16, :] = (
                tail[:, 128:256] + tail[:, 256:384] + tail[:, 384:512]
            )
            gain = 1.0 + tail[:, 208:248]
            length_row[b * 16 : b * 16 + 16, :] = jnp.concatenate(
                [gain, gain, jnp.zeros((16, 48), F32)], axis=1
            )

        def some(group, carry):
            for i in [group * 8 + member for member in range(8)]:
                spot = pl.ds(pl.multiple_of(i * 80, 8), 80)
                both = [turn_a[spot, :], turn_b[spot, :]]
                right_rot[i] = jnp.concatenate(both, axis=1).astype(BF)
            return carry

        lax.fori_loop(0, 4, some, 0)

    def rotations_there():
        u_swap.wait_recv()
        blank = jnp.zeros((128, 88), F32)
        for b in (0, 1):
            block = points_ref[pl.ds(y * 2 + b, 1), :]
            spot = iota((128, 16), 0) >> 3 == iota((128, 16), 1)
            wide = jnp.broadcast_to(block, (128, 16))
            target = jnp.sum(jnp.where(spot, wide, 0), axis=1, keepdims=True)
            before = ((wide >> 4) == (target >> 4)) & (wide < target)
            second = jnp.max(jnp.where(before, 1, 0), axis=1, keepdims=True)
            source = ((target >> 4) & 1) * 128 + (target >> 5) * 16 + second * 8
            source = source + (iota((128, 1), 0) & 7)
            order = jnp.where(iota((128, 256), 1) == source, 1.0, 0.0).astype(BF)
            rows = mm(order, u_in[:, :, b].reshape(256, PACK))
            for t in range(10):
                turn_a[pl.ds(b * 1280 + t, 128, stride=10), :] = jnp.concatenate(
                    [rows[:, t * 40 : t * 40 + 40], blank], axis=1
                )
            for t in range(5):
                energy = (
                    rows[:, 400 + t : 401 + t]
                    + rows[:, 405 + t : 406 + t]
                    + rows[:, 410 + t : 411 + t]
                )
                energy_col[pl.ds(b * 640 + t, 128, stride=5), :] = jnp.broadcast_to(
                    energy, (128, 128)
                )

        def some(group, carry):
            indices = [group * 8 + member for member in range(8)]
            spots = [pl.ds(pl.multiple_of(i * 80, 8), 80) for i in indices]
            turned = [jnp.transpose(turn_a[spot, :])[0:48, :].astype(BF) for spot in spots]
            for i, block in zip(indices, turned, strict=True):
                left_rot[i, :, 0:80] = block
            return carry

        lax.fori_loop(0, 4, some, 0)

    def weights():
        omega = jnp.where(x_lo == 0, phonon_ref[0:1, 0:1], phonon_ref[0:1, 1:2])
        bose = 1.0 / (jnp.exp(omega / thermal) - 1.0)
        scale = (math.pi / 32.0) * (broadening / math.pi) / (2.0 * omega)

        wide = broadening * broadening

        def some(group, carry):
            spots = [pl.ds(pl.multiple_of((group * 8 + i) * 40, 8), 40) for i in range(8)]
            rows = energy_row[pl.ds(pl.multiple_of(group * 8, 8), 8), :]
            gains = scale * length_row[pl.ds(pl.multiple_of(group * 8, 8), 8), :]
            found = []
            for i, spot in enumerate(spots):
                there = energy_col[spot, :]
                filling = 1.0 / (1.0 + jnp.exp(there / thermal))
                spacing = rows[i : i + 1, :] - there
                plus = spacing + omega
                minus = spacing - omega
                found.append(
                    gains[i : i + 1, :]
                    * (
                        (bose + filling) / (plus * plus + wide)
                        + (bose + 1.0 - filling) / (minus * minus + wide)
                    )
                )
            for spot, value in zip(spots, found, strict=True):
                weight[spot, :] = value
            return carry

        lax.fori_loop(0, 4, some, 0)

    def electron_phases():
        lane4 = iota((128, 128), 1)
        place = lane4 >> 4
        ahead = (place + 1) >> 1
        source = (y + 8 + jnp.where(place & 1 == 1, ahead, -ahead)) & 7
        e_of_lane = (source * 2 + ((x_lo + (lane4 >> 3)) & 1)) * 4 + (lane4 & 3)
        row4 = iota((128, 128), 0)
        match = (row4 & 63) == e_of_lane
        sine = row4 >> 6
        imag = (lane4 >> 2) & 1
        to_real = jnp.where(match & (sine == imag), jnp.where(sine == 1, -1.0, 1.0), 0.0)
        to_im = jnp.where(match & (sine != imag), 1.0, 0.0)
        for b in (0, 1):
            table = packs[b, 128:144, 0:128]
            mix[b * 16 : b * 16 + 16, :] = mm(table, to_real.astype(BF)).astype(BF)
            mix[32 + b * 16 : 48 + b * 16, :] = mm(table, to_im.astype(BF)).astype(BF)

    rotations_here()
    electron_phases()

    for copy in u_copies:
        copy.wait_recv()
    u_swap = remote(u_in.at[x_lo], u_in.at[x_lo], swap_s, swap_r, rp, flip_re(1))
    for copy in pieces.values():
        copy.wait_recv()
    own_row = 16 + x_lo * 8
    blocks = []
    for dl in (0, 1):
        added = None
        for dx in (0, 1):
            for place in range(5):
                if dl == 0 and dx == 0 and place == 0:
                    continue
                piece = l_piece[dl, dx, place].astype(F32)
                added = piece if added is None else added + piece
        block = jnp.concatenate([added[0:8], added[8:16, 0 : LANES - HALF]], axis=1)
        if dl == 0:
            block = block + part[pl.ds(pl.multiple_of(own_row, 8), 8), :]
        blocks.append(block)
    waves[0] = jnp.concatenate(blocks, axis=0).astype(BF)

    first = {}
    for place, step in ((4, 2), (3, -2), (2, 1), (1, -1)):
        first[place] = remote(
            waves.at[0], waves.at[place], y1_s.at[place], y1_r.at[place], rp, along_y(step)
        )
    lower = pl.ds(0, HALF)
    upper = pl.ds(HALF, LANES - HALF)
    later = []
    for number, (place, lanes, step) in enumerate(((4, lower, 1), (3, upper, -1))):
        first[place].wait_recv()
        later.append(
            remote(
                waves.at[place, :, lanes],
                waves.at[7, :, lanes],
                y2_s.at[number],
                y2_r.at[number],
                rp,
                along_y(2 * step),
            )
        )
    for number, (place, to, step) in enumerate(((4, 6, 1), (3, 5, -1))):
        later.append(
            remote(
                waves.at[place],
                waves.at[to],
                y2_s.at[2 + number],
                y2_r.at[2 + number],
                rp,
                along_y(step),
            )
        )
    rotations_there()
    weights()
    first[2].wait_recv()
    first[1].wait_recv()
    points_c = mm(mix[:, 0:80], waves[0:5].reshape(80, LANES))
    for copy in later:
        copy.wait_recv()
    points_c = points_c + mm(mix[:, 80:128], waves[5:8].reshape(48, LANES))

    for a in range(40):
        cut = slice(a * 40, a * 40 + 40)
        coupling[pl.ds(a, 32, stride=40), :] = jnp.concatenate(
            [points_c[0:32, cut], points_c[32:64, cut], jnp.zeros((32, 48), F32)], axis=1
        )

    def some_points(group, carry):
        indices = [group * 16 + i for i in range(16)]
        spots = [pl.ds(pl.multiple_of(i * 40, 8), 40) for i in indices]
        turned = [
            mm(coupling[spot, 0:80].astype(BF), right_rot[i])
            for i, spot in zip(indices, spots, strict=True)
        ]
        stacked = [
            jnp.concatenate([t[:, 0:80], t[:, 128:208]], axis=0).astype(BF) for t in turned
        ]
        final = [
            mm(left_rot[i, 0:40, 0:80], s) for i, s in zip(indices, stacked, strict=True)
        ]
        sums = [
            jnp.sum(f * f * weight[spot, 0:80], axis=0, keepdims=True)
            for f, spot in zip(final, spots, strict=True)
        ]
        rates[pl.ds(pl.multiple_of(group * 16, 8), 16), 0:80] = jnp.concatenate(sums, axis=0)
        return carry

    rates[...] = jnp.zeros((32, 128), F32)
    c_copies = []
    for dl in (0, 1):
        b = (x_lo + dl) % 2
        some_points(b, 0)
        rows = rates[pl.ds(pl.multiple_of(b * 16, 16), 16), :]
        rows = rows[:, 0:40] + rows[:, 40:80]
        rates_b[b] = jnp.concatenate([rows[0:8], rows[8:16], jnp.zeros((8, 48), F32)], axis=1)
        for dx in (1, 0):
            for dc in (1, 0):
                spot = dx * 4 + dc * 2 + dl
                if spot == 0:
                    continue
                copy = remote(
                    rates_b.at[b],
                    land_c.at[spot],
                    rc_s.at[spot],
                    rc_r.at[spot],
                    flip_rp(dx, dc),
                    flip_re(dl),
                )
                c_copies.append((spot, copy))
    summed = rates_b[x_lo]
    for spot, copy in reversed(c_copies):
        copy.wait_recv()
        summed = summed + land_c[spot]
    rates_z[...] = summed
    z_copies = []
    for step in (4, 3, 5, 2, 6, 1, 7):
        copy = remote(
            rates_z, land_z.at[step], rz_s.at[step], rz_r.at[step], along_z(step), re
        )
        z_copies.append((step, copy))
    for step, copy in reversed(z_copies):
        copy.wait_recv()
        summed = summed + land_z[step]
    out_ref[0:8, :] = summed[:, 0:40]
    out_ref[8:16, :] = summed[:, 40:80]

    for copy in started:
        copy.wait_send()


def per_device(
    wannier_coupling,
    phonon_lattice,
    phonon_degeneracy,
    electron_lattice,
    electron_degeneracy,
    phonon_wavevectors,
    electron_wavevectors,
    phonon_energies,
    bloch_rotations,
    band_energies,
    shifted_points,
):
    def vm(shape, dtype):
        return pltpu.VMEM(shape, dtype)

    def dma(*shape):
        return pltpu.SemaphoreType.DMA(shape)

    return pl.pallas_call(
        kernel,
        out_shape=jax.ShapeDtypeStruct((16, 40), F32),
        in_specs=[pl.BlockSpec(memory_space=pl.ANY)] * 11,
        out_specs=pl.BlockSpec(memory_space=pltpu.VMEM),
        scratch_shapes=[
            vm((4, 4, 6400), BF),
            vm((4, 3), jnp.int32),
            vm((1, 4), jnp.int32),
            vm((3, 64), jnp.int32),
            vm((1, 64), jnp.int32),
            vm((3, 32), F32),
            vm((3, 16), F32),
            vm((1, 2), F32),
            vm((16, 3200), F32),
            vm((16, 40), F32),
            vm((1, 256), jnp.int32),
            vm((128, LANES), BF),
            vm((32, 128), BF),
            vm((32, 128), BF),
            vm((256, 128), BF),
            vm((256, 128), BF),
            vm((256, 128), BF),
            vm((16, 16), jnp.int32),
            vm((4, 128, 128), F32),
            vm((144, PACK), BF),
            vm((2, 144, PACK), BF),
            vm((8, 2, 16, PACK), BF),
            vm((2, 8, 2, 16, PACK), BF),
            vm((160, LANES), F32),
            vm((2, 2, 16, LANES), BF),
            vm((2, 2, 16, LANES), BF),
            vm((2, 16, LANES), BF),
            vm((2, 16, LANES), BF),
            vm((2, 2, 5, 16, HALF), BF),
            vm((2, 2, 5, 16, HALF), BF),
            vm((8, 16, LANES), BF),
            vm((64, 128), BF),
            vm((2560, 128), F32),
            vm((2560, 128), F32),
            vm((32, 80, 256), BF),
            vm((32, 48, 128), BF),
            vm((1280, 128), F32),
            vm((32, 128), F32),
            vm((32, 128), F32),
            vm((1280, 128), F32),
            vm((1280, 128), F32),
            vm((32, 128), F32),
            vm((2, 8, 128), F32),
            vm((8, 8, 128), F32),
            vm((8, 128), F32),
            vm((8, 8, 128), F32),
            dma(14),
            dma(2),
            dma(2),
            pltpu.SemaphoreType.DMA,
            pltpu.SemaphoreType.DMA,
            dma(8),
            dma(8),
            dma(2, 2),
            dma(2, 2),
            dma(2),
            dma(2),
            dma(2, 2, 5),
            dma(2, 2, 5),
            pltpu.SemaphoreType.DMA,
            pltpu.SemaphoreType.DMA,
            dma(5),
            dma(5),
            dma(4),
            dma(4),
            dma(8),
            dma(8),
            dma(8),
            dma(8),
        ],
        compiler_params=pltpu.CompilerParams(
            collective_id=0, has_side_effects=True, vmem_limit_bytes=60 * 1024 * 1024
        ),
        cost_estimate=pl.CostEstimate(
            flops=300_000_000, bytes_accessed=2_000_000, transcendentals=200_000
        ),
    )(
        wannier_coupling,
        phonon_lattice,
        phonon_degeneracy.reshape(1, 4),
        electron_lattice.T,
        electron_degeneracy.reshape(1, 64),
        phonon_wavevectors.T,
        electron_wavevectors.T,
        phonon_energies,
        bloch_rotations,
        band_energies,
        shifted_points,
    )


def solution(mesh):
    in_specs = (
        P("re", "rp", None),
        P("rp", None),
        P("rp"),
        P(),
        P(),
        P(),
        P("re", None),
        P("rp", None),
        P("re", None),
        P("re", None),
        P("rp", None),
    )
    return jax.shard_map(
        per_device, mesh=mesh, in_specs=in_specs, out_specs=P("re", None), check_vma=False
    )
```

```python
import math

import jax
import jax.numpy as jnp
from jax import lax
from jax.experimental import pallas as pl
from jax.experimental.pallas import tpu as pltpu
from jax.sharding import PartitionSpec as P

NW = 40
MODES = 2
ROW = 1600
LANES = 1664
PACK = 512
MESH = pl.DeviceIdType.MESH
BF = jnp.bfloat16
F32 = jnp.float32

full_turn = 2.0 * math.pi
thermal = 0.025
broadening = 0.05
highest = lax.Precision.HIGHEST


def three_parts(values):
    high = values.astype(BF).astype(F32)
    rest = values - high
    middle = rest.astype(BF).astype(F32)
    return high, middle, rest - middle


def iota(shape, axis):
    return lax.broadcasted_iota(jnp.int32, shape, axis)


def mm(left, right):
    return jnp.dot(left, right, preferred_element_type=F32)


def outer(left, right):
    return lax.dot_general(
        left, right, (((0,), (0,)), ((), ())), precision=highest, preferred_element_type=F32
    )


LANE_TILES = [(start, min(start + 256, LANES)) for start in range(0, LANES, 256)]
HALF = 896


def kernel(
    w_hbm,
    plat_hbm,
    pdeg_hbm,
    elat_hbm,
    edeg_hbm,
    qvec_hbm,
    kvec_hbm,
    phonon_hbm,
    rot_hbm,
    band_hbm,
    shift_hbm,
    out_ref,
    w_ref,
    plat_ref,
    pdeg_ref,
    elat_ref,
    edeg_ref,
    qvec_ref,
    kvec_ref,
    phonon_ref,
    rot_ref,
    band_ref,
    shift_ref,
    w_both,
    cosw,
    sinw,
    lhs_own,
    lhs_out,
    lhs_sib,
    points_ref,
    pack_f,
    pack,
    packs,
    u_out,
    u_in,
    part,
    s_far,
    l_far,
    s_opp,
    l_opp,
    s_piece,
    l_piece,
    waves,
    mix,
    turn_a,
    turn_b,
    right_rot,
    left_rot,
    energy_col,
    energy_row,
    length_row,
    weight,
    coupling,
    rates,
    rates_b,
    land_c,
    rates_z,
    land_z,
    in_s,
    core_s,
    core_r,
    pack_s,
    pack_r,
    u_s,
    u_r,
    far_s,
    far_r,
    opp_s,
    opp_r,
    piece_s,
    piece_r,
    swap_s,
    swap_r,
    y1_s,
    y1_r,
    y2_s,
    y2_r,
    rc_s,
    rc_r,
    rz_s,
    rz_r,
):
    rp = lax.axis_index("rp")
    re = lax.axis_index("re")
    z = rp // 4
    x_hi = (rp // 2) % 2
    core = rp % 2
    y = re // 2
    x_lo = re % 2

    def flip_rp(dx, dc, step=0):
        hi = (1 - x_hi) if dx else x_hi
        co = (1 - core) if dc else core
        return ((z + 8 + step) % 8) * 4 + hi * 2 + co

    def flip_re(dl):
        return y * 2 + ((1 - x_lo) if dl else x_lo)

    def along_z(step):
        return (rp + 32 + 4 * step) % 32

    def along_y(step):
        return (re + 16 + 2 * step) % 16

    loads = {}

    def load(name, src, dst, number):
        loads[name] = pltpu.make_async_copy(src, dst, in_s.at[number])
        loads[name].start()

    for e in range(4):
        load(f"w{e}", w_hbm.at[e], w_ref.at[e], e)

    def loaded(*names):
        for name in names:
            loads[name].wait()

    started = []

    def remote(src, dst, send, recv, to_rp, to_re):
        copy = pltpu.make_async_remote_copy(
            src_ref=src,
            dst_ref=dst,
            send_sem=send,
            recv_sem=recv,
            device_id={"rp": to_rp, "re": to_re},
            device_id_type=MESH,
        )
        copy.start()
        started.append(copy)
        return copy

    partners = []
    for step in (4, 3, -3, 2, -2, 1, -1):
        partners += [(rp, along_y(step)), (along_z(step), re)]
        if abs(step) < 3:
            partners += [
                (flip_rp(dx, 0, step), flip_re(dl)) for dx, dl in ((1, 1), (1, 0), (0, 1))
            ]
    partners += [
        (flip_rp(dx, dc), flip_re(dl))
        for dc in (0, 1)
        for dx in (1, 0)
        for dl in (1, 0)
        if dx or dc or dl
    ]
    barrier = pltpu.get_barrier_semaphore()
    for to_rp, to_re in partners:
        pl.semaphore_signal(
            barrier, inc=1, device_id={"rp": to_rp, "re": to_re}, device_id_type=MESH
        )

    for number, (name, src, dst) in enumerate(
        (
            ("plat", plat_hbm, plat_ref),
            ("pdeg", pdeg_hbm, pdeg_ref),
            ("qvec", qvec_hbm, qvec_ref),
            ("elat", elat_hbm, elat_ref),
            ("edeg", edeg_hbm, edeg_ref),
            ("kvec", kvec_hbm, kvec_ref),
            ("phonon", phonon_hbm, phonon_ref),
            ("rot", rot_hbm, rot_ref),
            ("band", band_hbm, band_ref),
            ("shift", shift_hbm, shift_ref),
        )
    ):
        load(name, src, dst, 4 + number)

    loaded("w0", "w1", "w2", "w3")
    cells = jnp.concatenate([w_ref[e].astype(F32) for e in range(4)], axis=0)
    for mc in range(4):
        w_both[mc * 16 : mc * 16 + 16, :] = jnp.concatenate(
            [cells[:, mc * ROW : (mc + 1) * ROW], jnp.zeros((16, LANES - ROW), F32)], axis=1
        ).astype(BF)

    loaded("plat", "pdeg", "qvec")
    r_of_lane = jnp.where(iota((4, 128), 0) == (iota((4, 128), 1) & 3), 1.0, 0.0).astype(F32)
    p_angle = full_turn * outer(qvec_ref[...], outer(plat_ref[...].astype(F32), r_of_lane))
    p_weight = 1.0 / jnp.dot(
        pdeg_ref[...].astype(F32), r_of_lane, precision=highest, preferred_element_type=F32
    )
    cosw[...] = (jnp.cos(p_angle) * p_weight).astype(BF)
    sinw[...] = (jnp.sin(p_angle) * p_weight).astype(BF)
    row = iota((256, 128), 0)
    lane = iota((256, 128), 1)
    same = ((row >> 3) & 1 == (lane >> 5) & 1) & (row & 3 == (lane >> 2) & 3)
    to_imag = (row >> 2) & 1
    of_imag = (lane >> 4) & 1
    pick_cos = same & (to_imag == of_imag)
    pick_sin = same & (to_imag != of_imag)
    sign = jnp.where(to_imag == 1, 1.0, -1.0).astype(F32)
    q_row = iota((256, 32), 0)
    q_lane = iota((256, 32), 1)

    def phases_for(which_core, lanes):
        spread = jnp.where((q_row >> 4) * 2 + which_core == q_lane, 1.0, 0.0).astype(BF)
        cos_part = mm(spread, cosw[...])
        sin_part = mm(spread, sinw[...])
        return jnp.where(
            pick_cos & lanes, cos_part, jnp.where(pick_sin & lanes, sign * sin_part, 0.0)
        ).astype(BF)

    lhs_out[...] = phases_for(1 - core, lane >= 64)

    pl.semaphore_wait(barrier, len(partners))

    sib = flip_rp(0, 1)
    core_copies = [
        remote(
            w_both.at[0:64], w_both.at[64:128], core_s.at[0], core_r.at[0], sib, re
        )
    ]

    core_copies.append(remote(lhs_out, lhs_sib, core_s.at[1], core_r.at[1], sib, re))
    lhs_own[...] = phases_for(core, lane < 64)
    for copy in core_copies:
        copy.wait_recv()
    lhs_own[...] += lhs_sib[...]

    def lhs_of(z_to, sub):
        hi = (1 - x_hi) if sub == 0 else x_hi
        block = ((z_to + 8) % 8) * 2 + hi
        return lhs_own[pl.ds(pl.multiple_of(block * 16, 16), 16), :]

    outer_lhs = jnp.concatenate([lhs_of(z + s, sub) for s in (4, 3, -3) for sub in (0, 1)], axis=0)
    for start, end in LANE_TILES:
        block = mm(outer_lhs, w_both[:, start:end]).astype(BF)
        for sub in (0, 1):
            s_opp[sub, :, start:end] = block[sub * 16 : sub * 16 + 16]
            s_far[0, sub, :, start:end] = block[32 + sub * 16 : 48 + sub * 16]
            s_far[1, sub, :, start:end] = block[64 + sub * 16 : 80 + sub * 16]
    far = {}
    opp = {}
    for sub in (0, 1):
        toward = 2 if sub == 0 else -2
        opp[sub] = remote(
            s_opp.at[sub], l_opp.at[sub], opp_s.at[sub], opp_r.at[sub], along_z(toward), re
        )
        for side, step in ((0, 1), (1, -1)):
            far[side, sub] = remote(
                s_far.at[side, sub],
                l_far.at[side, sub],
                far_s.at[side, sub],
                far_r.at[side, sub],
                along_z(step),
                re,
            )
    inner_lhs = jnp.concatenate(
        [lhs_of(z + s, sub) for s in (0, 1, -1, 2, -2) for sub in (0, 1)], axis=0
    )
    for start, end in LANE_TILES:
        part[:, start:end] = mm(inner_lhs, w_both[:, start:end])

    def piece_of(place, dx, dl):
        first_row = place * 32 + (1 - dx) * 16 + ((x_lo + dl) % 2) * 8
        rows = part[pl.ds(pl.multiple_of(first_row, 8), 8), :]
        end = jnp.concatenate([rows[:, HALF:], jnp.zeros((8, 2 * HALF - LANES), F32)], axis=1)
        return jnp.concatenate([rows[:, 0:HALF], end], axis=0).astype(BF)

    pieces = {}

    def send_piece(place, step, dx, dl):
        s_piece[dl, dx, place] = piece_of(place, dx, dl)
        pieces[dl, dx, place] = remote(
            s_piece.at[dl, dx, place],
            l_piece.at[dl, dx, place],
            piece_s.at[dl, dx, place],
            piece_r.at[dl, dx, place],
            flip_rp(dx, 0, step),
            flip_re(dl),
        )

    for dx, dl in ((1, 1), (1, 0), (0, 1), (0, 0)):
        for place, step in ((1, 1), (2, -1)):
            send_piece(place, step, dx, dl)
    for dx, dl in ((1, 1), (1, 0), (0, 1)):
        send_piece(0, 0, dx, dl)

    loaded("elat", "edeg", "kvec", "phonon", "rot", "band", "shift")
    e_angle = full_turn * outer(kvec_ref[...], elat_ref[...].astype(F32))
    e_weight = 1.0 / edeg_ref[...].astype(F32)
    high, middle, low = three_parts(band_ref[...])
    rest = jnp.zeros((16, PACK - 415), F32)
    for j in range(8):
        five = slice(j * 5, j * 5 + 5)
        eighth = jnp.concatenate(
            [rot_ref[:, j * 400 : j * 400 + 400], high[:, five], middle[:, five], low[:, five], rest],
            axis=1,
        )
        for v in range(4):
            pack_f[v, pl.ds(j, 16, stride=8), :] = eighth[:, v * 128 : v * 128 + 128]
    for v in range(4):
        pack[0:128, v * 128 : v * 128 + 128] = pack_f[v].astype(BF)
    exact = jnp.concatenate([pack_f[v] for v in range(4)], axis=1)
    kept = pack[0:128, :].astype(F32)
    took = (exact - kept) * (exact + kept)
    left = kept * kept
    took = sum(took[:, t * 40 : t * 40 + 40] for t in range(10)).reshape(16, 8, 40)
    left = sum(left[:, t * 40 : t * 40 + 40] for t in range(10)).reshape(16, 8, 40)
    took, left = jnp.sum(took, axis=1), jnp.sum(left, axis=1)
    short = jnp.where(left > 0.0, took / jnp.where(left > 0.0, left, 1.0), 0.0)
    gap = jnp.zeros((16, 48), F32)
    pack[128:144, :] = jnp.concatenate(
        [jnp.cos(e_angle) * e_weight, jnp.sin(e_angle) * e_weight]
        + [high, high, short, gap[:, 0:8], middle, middle, gap, low, low, gap],
        axis=1,
    ).astype(BF)
    pack_copy = remote(pack, packs.at[x_lo], pack_s, pack_r, rp, flip_re(1))

    for d in range(16):
        points_ref[d : d + 1, :] = shift_ref[:, d * 16 : d * 16 + 16]
    points = points_ref[...]
    mine = (points >> 4) == re
    inner = points & 15
    smaller = jnp.min(jnp.where(mine, inner, 99), axis=1, keepdims=True)
    larger = jnp.max(jnp.where(mine, inner, -1), axis=1, keepdims=True)
    both = jnp.where(iota((16, 128), 1) == 0, smaller, larger).astype(F32).astype(BF)
    spread16 = jnp.where((iota((256, 16), 0) >> 4) == iota((256, 16), 1), 1.0, 0.0).astype(BF)
    both_rows = mm(spread16, both)
    slot = (iota((256, 1), 0) >> 3) & 1
    chosen = jnp.where(slot == 0, both_rows[:, 0:1], both_rows[:, 1:2])
    take = ((lane >> 3).astype(F32) == chosen) & ((lane & 7) == (row & 7))
    take = jnp.where(take, 1.0, 0.0).astype(BF)
    u_out[...] = mm(take, pack[0:128, :]).astype(BF).reshape(8, 2, 16, PACK)
    u_copies = []
    for step in (4, 3, 5, 2, 6, 1, 7):
        u_copies.append(
            remote(
                u_out.at[(y + step) % 8],
                u_in.at[x_lo, y],
                u_s.at[step],
                u_r.at[step],
                rp,
                along_y(step),
            )
        )
    packs[x_lo] = pack[...]
    u_in[x_lo, y] = u_out[y]

    for sub in (0, 1):
        for side, step in ((0, 1), (1, -1)):
            far[side, sub].wait_recv()
            more = l_far[side, sub].astype(F32)
            if side == sub:
                opp[sub].wait_recv()
                more = more + l_opp[sub].astype(F32)
            first_row = (3 + side) * 32 + sub * 16
            part[first_row : first_row + 16, :] += more
            for dl in (1, 0):
                send_piece(3 + side, 2 * step, 1 - sub, dl)

    def swap_halves(rows):
        cut = rows.reshape(16, 8, PACK)
        return jnp.concatenate([cut[:, 4:8], cut[:, 0:4]], axis=1).reshape(128, PACK)

    def rotations_here():
        pack_copy.wait_recv()
        blank = jnp.zeros((128, 48), F32)
        for b in (0, 1):
            rows = packs[b, 0:128, :].astype(F32)
            swapped = swap_halves(rows)
            rows = rows * jnp.where((iota((128, 1), 0) >> 2) & 1 == 1, -1.0, 1.0)
            for t in range(10):
                cut = slice(t * 40, t * 40 + 40)
                spot = pl.ds(b * 1280 + t, 128, stride=10)
                turn_a[spot, :] = jnp.concatenate([rows[:, cut], swapped[:, cut], blank], axis=1)
                turn_b[spot, :] = jnp.concatenate([swapped[:, cut], -rows[:, cut], blank], axis=1)
            tail = packs[b, 128:144, :].astype(F32)
            energy_row[b * 16 : b * 16 + 16, :] = (
                tail[:, 128:256] + tail[:, 256:384] + tail[:, 384:512]
            )
            gain = 1.0 + tail[:, 208:248]
            length_row[b * 16 : b * 16 + 16, :] = jnp.concatenate(
                [gain, gain, jnp.zeros((16, 48), F32)], axis=1
            )

        def some(group, carry):
            for i in [group * 8 + member for member in range(8)]:
                spot = pl.ds(pl.multiple_of(i * 80, 8), 80)
                both = [turn_a[spot, :], turn_b[spot, :]]
                right_rot[i] = jnp.concatenate(both, axis=1).astype(BF)
            return carry

        lax.fori_loop(0, 4, some, 0)

    def rotations_there():
        u_swap.wait_recv()
        blank = jnp.zeros((128, 88), F32)
        for b in (0, 1):
            block = points_ref[pl.ds(y * 2 + b, 1), :]
            spot = iota((128, 16), 0) >> 3 == iota((128, 16), 1)
            wide = jnp.broadcast_to(block, (128, 16))
            target = jnp.sum(jnp.where(spot, wide, 0), axis=1, keepdims=True)
            before = ((wide >> 4) == (target >> 4)) & (wide < target)
            second = jnp.max(jnp.where(before, 1, 0), axis=1, keepdims=True)
            source = ((target >> 4) & 1) * 128 + (target >> 5) * 16 + second * 8
            source = source + (iota((128, 1), 0) & 7)
            order = jnp.where(iota((128, 256), 1) == source, 1.0, 0.0).astype(BF)
            rows = mm(order, u_in[:, :, b].reshape(256, PACK))
            for t in range(10):
                turn_a[pl.ds(b * 1280 + t, 128, stride=10), :] = jnp.concatenate(
                    [rows[:, t * 40 : t * 40 + 40], blank], axis=1
                )
            for t in range(5):
                energy = (
                    rows[:, 400 + t : 401 + t]
                    + rows[:, 405 + t : 406 + t]
                    + rows[:, 410 + t : 411 + t]
                )
                energy_col[pl.ds(b * 640 + t, 128, stride=5), :] = jnp.broadcast_to(
                    energy, (128, 128)
                )

        def some(group, carry):
            indices = [group * 8 + member for member in range(8)]
            spots = [pl.ds(pl.multiple_of(i * 80, 8), 80) for i in indices]
            turned = [jnp.transpose(turn_a[spot, :])[0:48, :].astype(BF) for spot in spots]
            for i, block in zip(indices, turned, strict=True):
                left_rot[i, :, 0:80] = block
            return carry

        lax.fori_loop(0, 4, some, 0)

    def weights():
        omega = jnp.where(x_lo == 0, phonon_ref[0:1, 0:1], phonon_ref[0:1, 1:2])
        bose = 1.0 / (jnp.exp(omega / thermal) - 1.0)
        scale = (math.pi / 32.0) * (broadening / math.pi) / (2.0 * omega)

        wide = broadening * broadening

        def some(group, carry):
            spots = [pl.ds(pl.multiple_of((group * 8 + i) * 40, 8), 40) for i in range(8)]
            rows = energy_row[pl.ds(pl.multiple_of(group * 8, 8), 8), :]
            gains = scale * length_row[pl.ds(pl.multiple_of(group * 8, 8), 8), :]
            found = []
            for i, spot in enumerate(spots):
                there = energy_col[spot, :]
                filling = 1.0 / (1.0 + jnp.exp(there / thermal))
                spacing = rows[i : i + 1, :] - there
                plus = spacing + omega
                minus = spacing - omega
                found.append(
                    gains[i : i + 1, :]
                    * (
                        (bose + filling) / (plus * plus + wide)
                        + (bose + 1.0 - filling) / (minus * minus + wide)
                    )
                )
            for spot, value in zip(spots, found, strict=True):
                weight[spot, :] = value
            return carry

        lax.fori_loop(0, 4, some, 0)

    def electron_phases():
        lane4 = iota((128, 128), 1)
        place = lane4 >> 4
        ahead = (place + 1) >> 1
        source = (y + 8 + jnp.where(place & 1 == 1, ahead, -ahead)) & 7
        e_of_lane = (source * 2 + ((x_lo + (lane4 >> 3)) & 1)) * 4 + (lane4 & 3)
        row4 = iota((128, 128), 0)
        match = (row4 & 63) == e_of_lane
        sine = row4 >> 6
        imag = (lane4 >> 2) & 1
        to_real = jnp.where(match & (sine == imag), jnp.where(sine == 1, -1.0, 1.0), 0.0)
        to_im = jnp.where(match & (sine != imag), 1.0, 0.0)
        for b in (0, 1):
            table = packs[b, 128:144, 0:128]
            mix[b * 16 : b * 16 + 16, :] = mm(table, to_real.astype(BF)).astype(BF)
            mix[32 + b * 16 : 48 + b * 16, :] = mm(table, to_im.astype(BF)).astype(BF)

    rotations_here()
    electron_phases()

    for copy in u_copies:
        copy.wait_recv()
    u_swap = remote(u_in.at[x_lo], u_in.at[x_lo], swap_s, swap_r, rp, flip_re(1))
    for copy in pieces.values():
        copy.wait_recv()
    own_row = 16 + x_lo * 8
    blocks = []
    for dl in (0, 1):
        added = None
        for dx in (0, 1):
            for place in range(5):
                if dl == 0 and dx == 0 and place == 0:
                    continue
                piece = l_piece[dl, dx, place].astype(F32)
                added = piece if added is None else added + piece
        block = jnp.concatenate([added[0:8], added[8:16, 0 : LANES - HALF]], axis=1)
        if dl == 0:
            block = block + part[pl.ds(pl.multiple_of(own_row, 8), 8), :]
        blocks.append(block)
    waves[0] = jnp.concatenate(blocks, axis=0).astype(BF)

    first = {}
    for place, step in ((4, 2), (3, -2), (2, 1), (1, -1)):
        first[place] = remote(
            waves.at[0], waves.at[place], y1_s.at[place], y1_r.at[place], rp, along_y(step)
        )
    lower = pl.ds(0, HALF)
    upper = pl.ds(HALF, LANES - HALF)
    later = []
    for number, (place, lanes, step) in enumerate(((4, lower, 1), (3, upper, -1))):
        first[place].wait_recv()
        later.append(
            remote(
                waves.at[place, :, lanes],
                waves.at[7, :, lanes],
                y2_s.at[number],
                y2_r.at[number],
                rp,
                along_y(2 * step),
            )
        )
    for number, (place, to, step) in enumerate(((4, 6, 1), (3, 5, -1))):
        later.append(
            remote(
                waves.at[place],
                waves.at[to],
                y2_s.at[2 + number],
                y2_r.at[2 + number],
                rp,
                along_y(step),
            )
        )
    rotations_there()
    weights()
    first[2].wait_recv()
    first[1].wait_recv()
    points_c = mm(mix[:, 0:80], waves[0:5].reshape(80, LANES))
    for copy in later:
        copy.wait_recv()
    points_c = points_c + mm(mix[:, 80:128], waves[5:8].reshape(48, LANES))

    for a in range(40):
        cut = slice(a * 40, a * 40 + 40)
        coupling[pl.ds(a, 32, stride=40), :] = jnp.concatenate(
            [points_c[0:32, cut], points_c[32:64, cut], jnp.zeros((32, 48), F32)], axis=1
        )

    def some_points(group, carry):
        indices = [group * 16 + i for i in range(16)]
        spots = [pl.ds(pl.multiple_of(i * 40, 8), 40) for i in indices]
        turned = [
            mm(coupling[spot, 0:80].astype(BF), right_rot[i])
            for i, spot in zip(indices, spots, strict=True)
        ]
        stacked = [
            jnp.concatenate([t[:, 0:80], t[:, 128:208]], axis=0).astype(BF) for t in turned
        ]
        final = [
            mm(left_rot[i, 0:40, 0:80], s) for i, s in zip(indices, stacked, strict=True)
        ]
        sums = [
            jnp.sum(f * f * weight[spot, 0:80], axis=0, keepdims=True)
            for f, spot in zip(final, spots, strict=True)
        ]
        rates[pl.ds(pl.multiple_of(group * 16, 8), 16), 0:80] = jnp.concatenate(sums, axis=0)
        return carry

    rates[...] = jnp.zeros((32, 128), F32)
    c_copies = []
    for dl in (0, 1):
        b = (x_lo + dl) % 2
        some_points(b, 0)
        rows = rates[pl.ds(pl.multiple_of(b * 16, 16), 16), :]
        rows = rows[:, 0:40] + rows[:, 40:80]
        rates_b[b] = jnp.concatenate([rows[0:8], rows[8:16], jnp.zeros((8, 48), F32)], axis=1)
        for dx in (1, 0):
            for dc in (1, 0):
                spot = dx * 4 + dc * 2 + dl
                if spot == 0:
                    continue
                copy = remote(
                    rates_b.at[b],
                    land_c.at[spot],
                    rc_s.at[spot],
                    rc_r.at[spot],
                    flip_rp(dx, dc),
                    flip_re(dl),
                )
                c_copies.append((spot, copy))
    summed = rates_b[x_lo]
    for spot, copy in reversed(c_copies):
        copy.wait_recv()
        summed = summed + land_c[spot]
    rates_z[...] = summed
    z_copies = []
    for step in (4, 3, 5, 2, 6, 1, 7):
        copy = remote(
            rates_z, land_z.at[step], rz_s.at[step], rz_r.at[step], along_z(step), re
        )
        z_copies.append((step, copy))
    for step, copy in reversed(z_copies):
        copy.wait_recv()
        summed = summed + land_z[step]
    out_ref[0:8, :] = summed[:, 0:40]
    out_ref[8:16, :] = summed[:, 40:80]

    for copy in started:
        copy.wait_send()


def per_device(
    wannier_coupling,
    phonon_lattice,
    phonon_degeneracy,
    electron_lattice,
    electron_degeneracy,
    phonon_wavevectors,
    electron_wavevectors,
    phonon_energies,
    bloch_rotations,
    band_energies,
    shifted_points,
):
    def vm(shape, dtype):
        return pltpu.VMEM(shape, dtype)

    def dma(*shape):
        return pltpu.SemaphoreType.DMA(shape)

    return pl.pallas_call(
        kernel,
        out_shape=pltpu.VMEM((16, 40), F32),
        in_specs=[pl.BlockSpec(memory_space=pl.ANY)] * 11,
        out_specs=pl.BlockSpec(memory_space=pltpu.VMEM),
        scratch_shapes=[
            vm((4, 4, 6400), BF),
            vm((4, 3), jnp.int32),
            vm((1, 4), jnp.int32),
            vm((3, 64), jnp.int32),
            vm((1, 64), jnp.int32),
            vm((3, 32), F32),
            vm((3, 16), F32),
            vm((1, 2), F32),
            vm((16, 3200), F32),
            vm((16, 40), F32),
            vm((1, 256), jnp.int32),
            vm((128, LANES), BF),
            vm((32, 128), BF),
            vm((32, 128), BF),
            vm((256, 128), BF),
            vm((256, 128), BF),
            vm((256, 128), BF),
            vm((16, 16), jnp.int32),
            vm((4, 128, 128), F32),
            vm((144, PACK), BF),
            vm((2, 144, PACK), BF),
            vm((8, 2, 16, PACK), BF),
            vm((2, 8, 2, 16, PACK), BF),
            vm((160, LANES), F32),
            vm((2, 2, 16, LANES), BF),
            vm((2, 2, 16, LANES), BF),
            vm((2, 16, LANES), BF),
            vm((2, 16, LANES), BF),
            vm((2, 2, 5, 16, HALF), BF),
            vm((2, 2, 5, 16, HALF), BF),
            vm((8, 16, LANES), BF),
            vm((64, 128), BF),
            vm((2560, 128), F32),
            vm((2560, 128), F32),
            vm((32, 80, 256), BF),
            vm((32, 48, 128), BF),
            vm((1280, 128), F32),
            vm((32, 128), F32),
            vm((32, 128), F32),
            vm((1280, 128), F32),
            vm((1280, 128), F32),
            vm((32, 128), F32),
            vm((2, 8, 128), F32),
            vm((8, 8, 128), F32),
            vm((8, 128), F32),
            vm((8, 8, 128), F32),
            dma(14),
            dma(2),
            dma(2),
            pltpu.SemaphoreType.DMA,
            pltpu.SemaphoreType.DMA,
            dma(8),
            dma(8),
            dma(2, 2),
            dma(2, 2),
            dma(2),
            dma(2),
            dma(2, 2, 5),
            dma(2, 2, 5),
            pltpu.SemaphoreType.DMA,
            pltpu.SemaphoreType.DMA,
            dma(5),
            dma(5),
            dma(4),
            dma(4),
            dma(8),
            dma(8),
            dma(8),
            dma(8),
        ],
        compiler_params=pltpu.CompilerParams(
            collective_id=0, has_side_effects=True, vmem_limit_bytes=60 * 1024 * 1024
        ),
        cost_estimate=pl.CostEstimate(
            flops=300_000_000, bytes_accessed=2_000_000, transcendentals=200_000
        ),
    )(
        wannier_coupling,
        phonon_lattice,
        phonon_degeneracy.reshape(1, 4),
        electron_lattice.T,
        electron_degeneracy.reshape(1, 64),
        phonon_wavevectors.T,
        electron_wavevectors.T,
        phonon_energies,
        bloch_rotations,
        band_energies,
        shifted_points,
    )


def solution(mesh):
    in_specs = (
        P("re", "rp", None),
        P("rp", None),
        P("rp"),
        P(),
        P(),
        P(),
        P("re", None),
        P("rp", None),
        P("re", None),
        P("re", None),
        P("rp", None),
    )
    return jax.shard_map(
        per_device, mesh=mesh, in_specs=in_specs, out_specs=P("re", None), check_vma=False
    )
```

```python
import math

import jax
import jax.numpy as jnp
from jax import lax
from jax.experimental import pallas as pl
from jax.experimental.pallas import tpu as pltpu
from jax.sharding import PartitionSpec as P

NW = 40
MODES = 2
ROW = 1600
LANES = 1664
PACK = 512
MESH = pl.DeviceIdType.MESH
BF = jnp.bfloat16
F32 = jnp.float32

full_turn = 2.0 * math.pi
thermal = 0.025
broadening = 0.05
highest = lax.Precision.HIGHEST


def three_parts(values):
    high = values.astype(BF).astype(F32)
    rest = values - high
    middle = rest.astype(BF).astype(F32)
    return high, middle, rest - middle


def iota(shape, axis):
    return lax.broadcasted_iota(jnp.int32, shape, axis)


def mm(left, right):
    return jnp.dot(left, right, preferred_element_type=F32)


def outer(left, right):
    return lax.dot_general(
        left, right, (((0,), (0,)), ((), ())), precision=highest, preferred_element_type=F32
    )


LANE_TILES = [(start, min(start + 256, LANES)) for start in range(0, LANES, 256)]
HALF = 896


def kernel(
    w_hbm,
    plat_hbm,
    pdeg_hbm,
    elat_hbm,
    edeg_hbm,
    qvec_hbm,
    kvec_hbm,
    phonon_hbm,
    rot_hbm,
    band_hbm,
    shift_hbm,
    out_ref,
    w_ref,
    plat_ref,
    pdeg_ref,
    elat_ref,
    edeg_ref,
    qvec_ref,
    kvec_ref,
    phonon_ref,
    rot_ref,
    band_ref,
    shift_ref,
    w_both,
    cosw,
    sinw,
    lhs_own,
    lhs_out,
    lhs_sib,
    points_ref,
    pack_f,
    pack,
    packs,
    u_out,
    u_in,
    part,
    s_far,
    l_far,
    s_opp,
    l_opp,
    s_piece,
    l_piece,
    waves,
    mix,
    turn_a,
    turn_b,
    right_rot,
    left_rot,
    energy_col,
    energy_row,
    length_row,
    weight,
    coupling,
    rates,
    rates_b,
    land_c,
    rates_z,
    land_z,
    in_s,
    core_s,
    core_r,
    pack_s,
    pack_r,
    u_s,
    u_r,
    far_s,
    far_r,
    opp_s,
    opp_r,
    piece_s,
    piece_r,
    swap_s,
    swap_r,
    y1_s,
    y1_r,
    y2_s,
    y2_r,
    rc_s,
    rc_r,
    rz_s,
    rz_r,
):
    rp = lax.axis_index("rp")
    re = lax.axis_index("re")
    z = rp // 4
    x_hi = (rp // 2) % 2
    core = rp % 2
    y = re // 2
    x_lo = re % 2

    def flip_rp(dx, dc, step=0):
        hi = (1 - x_hi) if dx else x_hi
        co = (1 - core) if dc else core
        return ((z + 8 + step) % 8) * 4 + hi * 2 + co

    def flip_re(dl):
        return y * 2 + ((1 - x_lo) if dl else x_lo)

    def along_z(step):
        return (rp + 32 + 4 * step) % 32

    def along_y(step):
        return (re + 16 + 2 * step) % 16

    loads = {}

    def load(name, src, dst, number):
        loads[name] = pltpu.make_async_copy(src, dst, in_s.at[number])
        loads[name].start()

    for e in range(4):
        load(f"w{e}", w_hbm.at[e], w_ref.at[e], e)

    def loaded(*names):
        for name in names:
            loads[name].wait()

    started = []

    def remote(src, dst, send, recv, to_rp, to_re):
        copy = pltpu.make_async_remote_copy(
            src_ref=src,
            dst_ref=dst,
            send_sem=send,
            recv_sem=recv,
            device_id={"rp": to_rp, "re": to_re},
            device_id_type=MESH,
        )
        copy.start()
        started.append(copy)
        return copy

    partners = []
    for step in (4, 3, -3, 2, -2, 1, -1):
        partners += [(rp, along_y(step)), (along_z(step), re)]
        if abs(step) < 3:
            partners += [
                (flip_rp(dx, 0, step), flip_re(dl)) for dx, dl in ((1, 1), (1, 0), (0, 1))
            ]
    partners += [
        (flip_rp(dx, dc), flip_re(dl))
        for dc in (0, 1)
        for dx in (1, 0)
        for dl in (1, 0)
        if dx or dc or dl
    ]
    barrier = pltpu.get_barrier_semaphore()
    for to_rp, to_re in partners:
        pl.semaphore_signal(
            barrier, inc=1, device_id={"rp": to_rp, "re": to_re}, device_id_type=MESH
        )

    for number, (name, src, dst) in enumerate(
        (
            ("plat", plat_hbm, plat_ref),
            ("pdeg", pdeg_hbm, pdeg_ref),
            ("qvec", qvec_hbm, qvec_ref),
            ("elat", elat_hbm, elat_ref),
            ("edeg", edeg_hbm, edeg_ref),
            ("kvec", kvec_hbm, kvec_ref),
            ("phonon", phonon_hbm, phonon_ref),
            ("rot", rot_hbm, rot_ref),
            ("band", band_hbm, band_ref),
            ("shift", shift_hbm, shift_ref),
        )
    ):
        load(name, src, dst, 4 + number)

    loaded("w0", "w1", "w2", "w3")
    cells = jnp.concatenate([w_ref[e].astype(F32) for e in range(4)], axis=0)
    for mc in range(4):
        w_both[mc * 16 : mc * 16 + 16, :] = jnp.concatenate(
            [cells[:, mc * ROW : (mc + 1) * ROW], jnp.zeros((16, LANES - ROW), F32)], axis=1
        ).astype(BF)

    loaded("plat", "pdeg", "qvec")
    r_of_lane = jnp.where(iota((4, 128), 0) == (iota((4, 128), 1) & 3), 1.0, 0.0).astype(F32)
    p_angle = full_turn * outer(qvec_ref[...], outer(plat_ref[...].astype(F32), r_of_lane))
    p_weight = 1.0 / jnp.dot(
        pdeg_ref[...].astype(F32), r_of_lane, precision=highest, preferred_element_type=F32
    )
    cosw[...] = (jnp.cos(p_angle) * p_weight).astype(BF)
    sinw[...] = (jnp.sin(p_angle) * p_weight).astype(BF)
    row = iota((256, 128), 0)
    lane = iota((256, 128), 1)
    same = ((row >> 3) & 1 == (lane >> 5) & 1) & (row & 3 == (lane >> 2) & 3)
    to_imag = (row >> 2) & 1
    of_imag = (lane >> 4) & 1
    pick_cos = same & (to_imag == of_imag)
    pick_sin = same & (to_imag != of_imag)
    sign = jnp.where(to_imag == 1, 1.0, -1.0).astype(F32)
    q_row = iota((256, 32), 0)
    q_lane = iota((256, 32), 1)

    def phases_for(which_core, lanes):
        spread = jnp.where((q_row >> 4) * 2 + which_core == q_lane, 1.0, 0.0).astype(BF)
        cos_part = mm(spread, cosw[...])
        sin_part = mm(spread, sinw[...])
        return jnp.where(
            pick_cos & lanes, cos_part, jnp.where(pick_sin & lanes, sign * sin_part, 0.0)
        ).astype(BF)

    lhs_out[...] = phases_for(1 - core, lane >= 64)

    pl.semaphore_wait(barrier, len(partners))

    sib = flip_rp(0, 1)
    core_copies = [
        remote(
            w_both.at[0:64], w_both.at[64:128], core_s.at[0], core_r.at[0], sib, re
        )
    ]

    core_copies.append(remote(lhs_out, lhs_sib, core_s.at[1], core_r.at[1], sib, re))
    lhs_own[...] = phases_for(core, lane < 64)
    for copy in core_copies:
        copy.wait_recv()
    lhs_own[...] += lhs_sib[...]

    def lhs_of(z_to, sub):
        hi = (1 - x_hi) if sub == 0 else x_hi
        block = ((z_to + 8) % 8) * 2 + hi
        return lhs_own[pl.ds(pl.multiple_of(block * 16, 16), 16), :]

    outer_lhs = jnp.concatenate([lhs_of(z + s, sub) for s in (4, 3, -3) for sub in (0, 1)], axis=0)
    for start, end in LANE_TILES:
        block = mm(outer_lhs, w_both[:, start:end]).astype(BF)
        for sub in (0, 1):
            s_opp[sub, :, start:end] = block[sub * 16 : sub * 16 + 16]
            s_far[0, sub, :, start:end] = block[32 + sub * 16 : 48 + sub * 16]
            s_far[1, sub, :, start:end] = block[64 + sub * 16 : 80 + sub * 16]
    far = {}
    opp = {}
    for sub in (0, 1):
        toward = 2 if sub == 0 else -2
        opp[sub] = remote(
            s_opp.at[sub], l_opp.at[sub], opp_s.at[sub], opp_r.at[sub], along_z(toward), re
        )
        for side, step in ((0, 1), (1, -1)):
            far[side, sub] = remote(
                s_far.at[side, sub],
                l_far.at[side, sub],
                far_s.at[side, sub],
                far_r.at[side, sub],
                along_z(step),
                re,
            )
    inner_lhs = jnp.concatenate(
        [lhs_of(z + s, sub) for s in (0, 1, -1, 2, -2) for sub in (0, 1)], axis=0
    )
    for start, end in LANE_TILES:
        part[:, start:end] = mm(inner_lhs, w_both[:, start:end])

    def piece_of(place, dx, dl):
        first_row = place * 32 + (1 - dx) * 16 + ((x_lo + dl) % 2) * 8
        rows = part[pl.ds(pl.multiple_of(first_row, 8), 8), :]
        end = jnp.concatenate([rows[:, HALF:], jnp.zeros((8, 2 * HALF - LANES), F32)], axis=1)
        return jnp.concatenate([rows[:, 0:HALF], end], axis=0).astype(BF)

    pieces = {}

    def send_piece(place, step, dx, dl):
        s_piece[dl, dx, place] = piece_of(place, dx, dl)
        pieces[dl, dx, place] = remote(
            s_piece.at[dl, dx, place],
            l_piece.at[dl, dx, place],
            piece_s.at[dl, dx, place],
            piece_r.at[dl, dx, place],
            flip_rp(dx, 0, step),
            flip_re(dl),
        )

    for dx, dl in ((1, 1), (1, 0), (0, 1), (0, 0)):
        for place, step in ((1, 1), (2, -1)):
            send_piece(place, step, dx, dl)
    for dx, dl in ((1, 1), (1, 0), (0, 1)):
        send_piece(0, 0, dx, dl)

    loaded("elat", "edeg", "kvec", "phonon", "rot", "band", "shift")
    e_angle = full_turn * outer(kvec_ref[...], elat_ref[...].astype(F32))
    e_weight = 1.0 / edeg_ref[...].astype(F32)
    high, middle, low = three_parts(band_ref[...])
    rest = jnp.zeros((16, PACK - 415), F32)
    for j in range(8):
        five = slice(j * 5, j * 5 + 5)
        eighth = jnp.concatenate(
            [rot_ref[:, j * 400 : j * 400 + 400], high[:, five], middle[:, five], low[:, five], rest],
            axis=1,
        )
        for v in range(4):
            pack_f[v, pl.ds(j, 16, stride=8), :] = eighth[:, v * 128 : v * 128 + 128]
    for v in range(4):
        pack[0:128, v * 128 : v * 128 + 128] = pack_f[v].astype(BF)
    exact = jnp.concatenate([pack_f[v] for v in range(4)], axis=1)
    kept = pack[0:128, :].astype(F32)
    took = (exact - kept) * (exact + kept)
    left = kept * kept
    took = sum(took[:, t * 40 : t * 40 + 40] for t in range(10)).reshape(16, 8, 40)
    left = sum(left[:, t * 40 : t * 40 + 40] for t in range(10)).reshape(16, 8, 40)
    took, left = jnp.sum(took, axis=1), jnp.sum(left, axis=1)
    short = jnp.where(left > 0.0, took / jnp.where(left > 0.0, left, 1.0), 0.0)
    gap = jnp.zeros((16, 48), F32)
    pack[128:144, :] = jnp.concatenate(
        [jnp.cos(e_angle) * e_weight, jnp.sin(e_angle) * e_weight]
        + [high, high, short, gap[:, 0:8], middle, middle, gap, low, low, gap],
        axis=1,
    ).astype(BF)
    pack_copy = remote(pack, packs.at[x_lo], pack_s, pack_r, rp, flip_re(1))

    for d in range(16):
        points_ref[d : d + 1, :] = shift_ref[:, d * 16 : d * 16 + 16]
    points = points_ref[...]
    mine = (points >> 4) == re
    inner = points & 15
    smaller = jnp.min(jnp.where(mine, inner, 99), axis=1, keepdims=True)
    larger = jnp.max(jnp.where(mine, inner, -1), axis=1, keepdims=True)
    both = jnp.where(iota((16, 128), 1) == 0, smaller, larger).astype(F32).astype(BF)
    spread16 = jnp.where((iota((256, 16), 0) >> 4) == iota((256, 16), 1), 1.0, 0.0).astype(BF)
    both_rows = mm(spread16, both)
    slot = (iota((256, 1), 0) >> 3) & 1
    chosen = jnp.where(slot == 0, both_rows[:, 0:1], both_rows[:, 1:2])
    take = ((lane >> 3).astype(F32) == chosen) & ((lane & 7) == (row & 7))
    take = jnp.where(take, 1.0, 0.0).astype(BF)
    u_out[...] = mm(take, pack[0:128, :]).astype(BF).reshape(8, 2, 16, PACK)
    u_copies = []
    for step in (1, 7, 2, 6, 3, 5, 4):
        u_copies.append(
            remote(
                u_out.at[(y + step) % 8],
                u_in.at[x_lo, y],
                u_s.at[step],
                u_r.at[step],
                rp,
                along_y(step),
            )
        )
    packs[x_lo] = pack[...]
    u_in[x_lo, y] = u_out[y]

    for sub in (0, 1):
        for side, step in ((0, 1), (1, -1)):
            far[side, sub].wait_recv()
            more = l_far[side, sub].astype(F32)
            if side == sub:
                opp[sub].wait_recv()
                more = more + l_opp[sub].astype(F32)
            first_row = (3 + side) * 32 + sub * 16
            part[first_row : first_row + 16, :] += more
            for dl in (1, 0):
                send_piece(3 + side, 2 * step, 1 - sub, dl)

    def swap_halves(rows):
        cut = rows.reshape(16, 8, PACK)
        return jnp.concatenate([cut[:, 4:8], cut[:, 0:4]], axis=1).reshape(128, PACK)

    def rotations_here():
        pack_copy.wait_recv()
        blank = jnp.zeros((128, 48), F32)
        for b in (0, 1):
            rows = packs[b, 0:128, :].astype(F32)
            swapped = swap_halves(rows)
            rows = rows * jnp.where((iota((128, 1), 0) >> 2) & 1 == 1, -1.0, 1.0)
            for t in range(10):
                cut = slice(t * 40, t * 40 + 40)
                spot = pl.ds(b * 1280 + t, 128, stride=10)
                turn_a[spot, :] = jnp.concatenate([rows[:, cut], swapped[:, cut], blank], axis=1)
                turn_b[spot, :] = jnp.concatenate([swapped[:, cut], -rows[:, cut], blank], axis=1)
            tail = packs[b, 128:144, :].astype(F32)
            energy_row[b * 16 : b * 16 + 16, :] = (
                tail[:, 128:256] + tail[:, 256:384] + tail[:, 384:512]
            )
            gain = 1.0 + tail[:, 208:248]
            length_row[b * 16 : b * 16 + 16, :] = jnp.concatenate(
                [gain, gain, jnp.zeros((16, 48), F32)], axis=1
            )

        def some(group, carry):
            for i in [group * 8 + member for member in range(8)]:
                spot = pl.ds(pl.multiple_of(i * 80, 8), 80)
                both = [turn_a[spot, :], turn_b[spot, :]]
                right_rot[i] = jnp.concatenate(both, axis=1).astype(BF)
            return carry

        lax.fori_loop(0, 4, some, 0)

    def rotations_there():
        u_swap.wait_recv()
        blank = jnp.zeros((128, 88), F32)
        for b in (0, 1):
            block = points_ref[pl.ds(y * 2 + b, 1), :]
            spot = iota((128, 16), 0) >> 3 == iota((128, 16), 1)
            wide = jnp.broadcast_to(block, (128, 16))
            target = jnp.sum(jnp.where(spot, wide, 0), axis=1, keepdims=True)
            before = ((wide >> 4) == (target >> 4)) & (wide < target)
            second = jnp.max(jnp.where(before, 1, 0), axis=1, keepdims=True)
            source = ((target >> 4) & 1) * 128 + (target >> 5) * 16 + second * 8
            source = source + (iota((128, 1), 0) & 7)
            order = jnp.where(iota((128, 256), 1) == source, 1.0, 0.0).astype(BF)
            rows = mm(order, u_in[:, :, b].reshape(256, PACK))
            for t in range(10):
                turn_a[pl.ds(b * 1280 + t, 128, stride=10), :] = jnp.concatenate(
                    [rows[:, t * 40 : t * 40 + 40], blank], axis=1
                )
            for t in range(5):
                energy = (
                    rows[:, 400 + t : 401 + t]
                    + rows[:, 405 + t : 406 + t]
                    + rows[:, 410 + t : 411 + t]
                )
                energy_col[pl.ds(b * 640 + t, 128, stride=5), :] = jnp.broadcast_to(
                    energy, (128, 128)
                )

        def some(group, carry):
            indices = [group * 8 + member for member in range(8)]
            spots = [pl.ds(pl.multiple_of(i * 80, 8), 80) for i in indices]
            turned = [jnp.transpose(turn_a[spot, :])[0:48, :].astype(BF) for spot in spots]
            for i, block in zip(indices, turned, strict=True):
                left_rot[i, :, 0:80] = block
            return carry

        lax.fori_loop(0, 4, some, 0)

    def weights():
        omega = jnp.where(x_lo == 0, phonon_ref[0:1, 0:1], phonon_ref[0:1, 1:2])
        bose = 1.0 / (jnp.exp(omega / thermal) - 1.0)
        scale = (math.pi / 32.0) * (broadening / math.pi) / (2.0 * omega)

        wide = broadening * broadening

        def some(group, carry):
            spots = [pl.ds(pl.multiple_of((group * 8 + i) * 40, 8), 40) for i in range(8)]
            rows = energy_row[pl.ds(pl.multiple_of(group * 8, 8), 8), :]
            gains = scale * length_row[pl.ds(pl.multiple_of(group * 8, 8), 8), :]
            found = []
            for i, spot in enumerate(spots):
                there = energy_col[spot, :]
                filling = 1.0 / (1.0 + jnp.exp(there / thermal))
                spacing = rows[i : i + 1, :] - there
                plus = spacing + omega
                minus = spacing - omega
                found.append(
                    gains[i : i + 1, :]
                    * (
                        (bose + filling) / (plus * plus + wide)
                        + (bose + 1.0 - filling) / (minus * minus + wide)
                    )
                )
            for spot, value in zip(spots, found, strict=True):
                weight[spot, :] = value
            return carry

        lax.fori_loop(0, 4, some, 0)

    def electron_phases():
        lane4 = iota((128, 128), 1)
        place = lane4 >> 4
        ahead = (place + 1) >> 1
        source = (y + 8 + jnp.where(place & 1 == 1, ahead, -ahead)) & 7
        e_of_lane = (source * 2 + ((x_lo + (lane4 >> 3)) & 1)) * 4 + (lane4 & 3)
        row4 = iota((128, 128), 0)
        match = (row4 & 63) == e_of_lane
        sine = row4 >> 6
        imag = (lane4 >> 2) & 1
        to_real = jnp.where(match & (sine == imag), jnp.where(sine == 1, -1.0, 1.0), 0.0)
        to_im = jnp.where(match & (sine != imag), 1.0, 0.0)
        for b in (0, 1):
            table = packs[b, 128:144, 0:128]
            mix[b * 16 : b * 16 + 16, :] = mm(table, to_real.astype(BF)).astype(BF)
            mix[32 + b * 16 : 48 + b * 16, :] = mm(table, to_im.astype(BF)).astype(BF)

    rotations_here()
    electron_phases()

    for copy in u_copies:
        copy.wait_recv()
    u_swap = remote(u_in.at[x_lo], u_in.at[x_lo], swap_s, swap_r, rp, flip_re(1))
    def add_pieces(dl, places, added):
        for dx in (0, 1):
            for place in places:
                if (dl, dx, place) not in pieces:
                    continue
                pieces[dl, dx, place].wait_recv()
                piece = l_piece[dl, dx, place].astype(F32)
                added = piece if added is None else added + piece
        return added

    nearer = [add_pieces(dl, (0, 1, 2), None) for dl in (0, 1)]
    blocks = []
    for dl in (0, 1):
        added = add_pieces(dl, (3, 4), nearer[dl])
        block = jnp.concatenate([added[0:8], added[8:16, 0 : LANES - HALF]], axis=1)
        if dl == 0:
            block = block + part[pl.ds(pl.multiple_of(16 + x_lo * 8, 8), 8), :]
        blocks.append(block)
    waves[0] = jnp.concatenate(blocks, axis=0).astype(BF)

    first = {}
    for place, step in ((4, 2), (3, -2), (2, 1), (1, -1)):
        first[place] = remote(
            waves.at[0], waves.at[place], y1_s.at[place], y1_r.at[place], rp, along_y(step)
        )
    lower = pl.ds(0, HALF)
    upper = pl.ds(HALF, LANES - HALF)
    later = []
    for number, (place, lanes, step) in enumerate(((4, lower, 1), (3, upper, -1))):
        first[place].wait_recv()
        later.append(
            remote(
                waves.at[place, :, lanes],
                waves.at[7, :, lanes],
                y2_s.at[number],
                y2_r.at[number],
                rp,
                along_y(2 * step),
            )
        )
    for number, (place, to, step) in enumerate(((4, 6, 1), (3, 5, -1))):
        later.append(
            remote(
                waves.at[place],
                waves.at[to],
                y2_s.at[2 + number],
                y2_r.at[2 + number],
                rp,
                along_y(step),
            )
        )
    rotations_there()
    weights()
    first[2].wait_recv()
    first[1].wait_recv()
    points_c = mm(mix[:, 0:80], waves[0:5].reshape(80, LANES))
    for copy in later:
        copy.wait_recv()
    points_c = points_c + mm(mix[:, 80:128], waves[5:8].reshape(48, LANES))

    for a in range(40):
        cut = slice(a * 40, a * 40 + 40)
        coupling[pl.ds(a, 32, stride=40), :] = jnp.concatenate(
            [points_c[0:32, cut], points_c[32:64, cut], jnp.zeros((32, 48), F32)], axis=1
        )

    def some_points(group, carry):
        indices = [group * 16 + i for i in range(16)]
        spots = [pl.ds(pl.multiple_of(i * 40, 8), 40) for i in indices]
        turned = [
            mm(coupling[spot, 0:80].astype(BF), right_rot[i])
            for i, spot in zip(indices, spots, strict=True)
        ]
        stacked = [
            jnp.concatenate([t[:, 0:80], t[:, 128:208]], axis=0).astype(BF) for t in turned
        ]
        final = [
            mm(left_rot[i, 0:40, 0:80], s) for i, s in zip(indices, stacked, strict=True)
        ]
        sums = [
            jnp.sum(f * f * weight[spot, 0:80], axis=0, keepdims=True)
            for f, spot in zip(final, spots, strict=True)
        ]
        rates[pl.ds(pl.multiple_of(group * 16, 8), 16), 0:80] = jnp.concatenate(sums, axis=0)
        return carry

    rates[...] = jnp.zeros((32, 128), F32)
    c_copies = []
    for dl in (0, 1):
        b = (x_lo + dl) % 2
        some_points(b, 0)
        rows = rates[pl.ds(pl.multiple_of(b * 16, 16), 16), :]
        rows = rows[:, 0:40] + rows[:, 40:80]
        rates_b[b] = jnp.concatenate([rows[0:8], rows[8:16], jnp.zeros((8, 48), F32)], axis=1)
        for dx in (1, 0):
            for dc in (1, 0):
                spot = dx * 4 + dc * 2 + dl
                if spot == 0:
                    continue
                copy = remote(
                    rates_b.at[b],
                    land_c.at[spot],
                    rc_s.at[spot],
                    rc_r.at[spot],
                    flip_rp(dx, dc),
                    flip_re(dl),
                )
                c_copies.append((spot, copy))
    summed = rates_b[x_lo]
    for spot, copy in reversed(c_copies):
        copy.wait_recv()
        summed = summed + land_c[spot]
    rates_z[...] = summed
    z_copies = []
    for step in (4, 3, 5, 2, 6, 1, 7):
        copy = remote(
            rates_z, land_z.at[step], rz_s.at[step], rz_r.at[step], along_z(step), re
        )
        z_copies.append((step, copy))
    for step, copy in reversed(z_copies):
        copy.wait_recv()
        summed = summed + land_z[step]
    out_ref[0:8, :] = summed[:, 0:40]
    out_ref[8:16, :] = summed[:, 40:80]

    for copy in started:
        copy.wait_send()


def per_device(
    wannier_coupling,
    phonon_lattice,
    phonon_degeneracy,
    electron_lattice,
    electron_degeneracy,
    phonon_wavevectors,
    electron_wavevectors,
    phonon_energies,
    bloch_rotations,
    band_energies,
    shifted_points,
):
    def vm(shape, dtype):
        return pltpu.VMEM(shape, dtype)

    def dma(*shape):
        return pltpu.SemaphoreType.DMA(shape)

    return pl.pallas_call(
        kernel,
        out_shape=pltpu.VMEM((16, 40), F32),
        in_specs=[pl.BlockSpec(memory_space=pl.ANY)] * 11,
        out_specs=pl.BlockSpec(memory_space=pltpu.VMEM),
        scratch_shapes=[
            vm((4, 4, 6400), BF),
            vm((4, 3), jnp.int32),
            vm((1, 4), jnp.int32),
            vm((3, 64), jnp.int32),
            vm((1, 64), jnp.int32),
            vm((3, 32), F32),
            vm((3, 16), F32),
            vm((1, 2), F32),
            vm((16, 3200), F32),
            vm((16, 40), F32),
            vm((1, 256), jnp.int32),
            vm((128, LANES), BF),
            vm((32, 128), BF),
            vm((32, 128), BF),
            vm((256, 128), BF),
            vm((256, 128), BF),
            vm((256, 128), BF),
            vm((16, 16), jnp.int32),
            vm((4, 128, 128), F32),
            vm((144, PACK), BF),
            vm((2, 144, PACK), BF),
            vm((8, 2, 16, PACK), BF),
            vm((2, 8, 2, 16, PACK), BF),
            vm((160, LANES), F32),
            vm((2, 2, 16, LANES), BF),
            vm((2, 2, 16, LANES), BF),
            vm((2, 16, LANES), BF),
            vm((2, 16, LANES), BF),
            vm((2, 2, 5, 16, HALF), BF),
            vm((2, 2, 5, 16, HALF), BF),
            vm((8, 16, LANES), BF),
            vm((64, 128), BF),
            vm((2560, 128), F32),
            vm((2560, 128), F32),
            vm((32, 80, 256), BF),
            vm((32, 48, 128), BF),
            vm((1280, 128), F32),
            vm((32, 128), F32),
            vm((32, 128), F32),
            vm((1280, 128), F32),
            vm((1280, 128), F32),
            vm((32, 128), F32),
            vm((2, 8, 128), F32),
            vm((8, 8, 128), F32),
            vm((8, 128), F32),
            vm((8, 8, 128), F32),
            dma(14),
            dma(2),
            dma(2),
            pltpu.SemaphoreType.DMA,
            pltpu.SemaphoreType.DMA,
            dma(8),
            dma(8),
            dma(2, 2),
            dma(2, 2),
            dma(2),
            dma(2),
            dma(2, 2, 5),
            dma(2, 2, 5),
            pltpu.SemaphoreType.DMA,
            pltpu.SemaphoreType.DMA,
            dma(5),
            dma(5),
            dma(4),
            dma(4),
            dma(8),
            dma(8),
            dma(8),
            dma(8),
        ],
        compiler_params=pltpu.CompilerParams(
            collective_id=0, has_side_effects=True, vmem_limit_bytes=60 * 1024 * 1024
        ),
        cost_estimate=pl.CostEstimate(
            flops=300_000_000, bytes_accessed=2_000_000, transcendentals=200_000
        ),
    )(
        wannier_coupling,
        phonon_lattice,
        phonon_degeneracy.reshape(1, 4),
        electron_lattice.T,
        electron_degeneracy.reshape(1, 64),
        phonon_wavevectors.T,
        electron_wavevectors.T,
        phonon_energies,
        bloch_rotations,
        band_energies,
        shifted_points,
    )


def solution(mesh):
    in_specs = (
        P("re", "rp", None),
        P("rp", None),
        P("rp"),
        P(),
        P(),
        P(),
        P("re", None),
        P("rp", None),
        P("re", None),
        P("re", None),
        P("rp", None),
    )
    return jax.shard_map(
        per_device, mesh=mesh, in_specs=in_specs, out_specs=P("re", None), check_vma=False
    )
```

```python
import math

import jax
import jax.numpy as jnp
from jax import lax
from jax.experimental import pallas as pl
from jax.experimental.pallas import tpu as pltpu
from jax.sharding import PartitionSpec as P

NW = 40
MODES = 2
ROW = 1600
LANES = 1664
PACK = 512
MESH = pl.DeviceIdType.MESH
BF = jnp.bfloat16
F32 = jnp.float32

full_turn = 2.0 * math.pi
thermal = 0.025
broadening = 0.05
highest = lax.Precision.HIGHEST


def three_parts(values):
    high = values.astype(BF).astype(F32)
    rest = values - high
    middle = rest.astype(BF).astype(F32)
    return high, middle, rest - middle


def iota(shape, axis):
    return lax.broadcasted_iota(jnp.int32, shape, axis)


def mm(left, right):
    return jnp.dot(left, right, preferred_element_type=F32)


def outer(left, right):
    return lax.dot_general(
        left, right, (((0,), (0,)), ((), ())), precision=highest, preferred_element_type=F32
    )


LANE_TILES = [(start, min(start + 256, LANES)) for start in range(0, LANES, 256)]
HALF = 896


def kernel(
    w_hbm,
    plat_hbm,
    pdeg_hbm,
    elat_hbm,
    edeg_hbm,
    qvec_hbm,
    kvec_hbm,
    phonon_hbm,
    rot_hbm,
    band_hbm,
    shift_hbm,
    out_ref,
    w_ref,
    plat_ref,
    pdeg_ref,
    elat_ref,
    edeg_ref,
    qvec_ref,
    kvec_ref,
    phonon_ref,
    rot_ref,
    band_ref,
    shift_ref,
    w_both,
    cosw,
    sinw,
    lhs_own,
    lhs_out,
    lhs_sib,
    points_ref,
    pack_f,
    pack,
    packs,
    u_out,
    u_in,
    part,
    s_far,
    l_far,
    s_opp,
    l_opp,
    s_piece,
    l_piece,
    waves,
    mix,
    turn_a,
    turn_b,
    right_rot,
    left_rot,
    energy_col,
    energy_row,
    length_row,
    weight,
    coupling,
    rates,
    rates_b,
    land_c,
    rates_z,
    land_z,
    in_s,
    core_s,
    core_r,
    pack_s,
    pack_r,
    u_s,
    u_r,
    far_s,
    far_r,
    opp_s,
    opp_r,
    piece_s,
    piece_r,
    swap_s,
    swap_r,
    y1_s,
    y1_r,
    y2_s,
    y2_r,
    rc_s,
    rc_r,
    rz_s,
    rz_r,
):
    rp = lax.axis_index("rp")
    re = lax.axis_index("re")
    z = rp // 4
    x_hi = (rp // 2) % 2
    core = rp % 2
    y = re // 2
    x_lo = re % 2

    def flip_rp(dx, dc, step=0):
        hi = (1 - x_hi) if dx else x_hi
        co = (1 - core) if dc else core
        return ((z + 8 + step) % 8) * 4 + hi * 2 + co

    def flip_re(dl):
        return y * 2 + ((1 - x_lo) if dl else x_lo)

    def along_z(step):
        return (rp + 32 + 4 * step) % 32

    def along_y(step):
        return (re + 16 + 2 * step) % 16

    loads = {}

    def load(name, src, dst, number):
        loads[name] = pltpu.make_async_copy(src, dst, in_s.at[number])
        loads[name].start()

    for e in range(4):
        load(f"w{e}", w_hbm.at[e], w_ref.at[e], e)

    def loaded(*names):
        for name in names:
            loads[name].wait()

    started = []

    def remote(src, dst, send, recv, to_rp, to_re):
        copy = pltpu.make_async_remote_copy(
            src_ref=src,
            dst_ref=dst,
            send_sem=send,
            recv_sem=recv,
            device_id={"rp": to_rp, "re": to_re},
            device_id_type=MESH,
        )
        copy.start()
        started.append(copy)
        return copy

    partners = []
    for step in (4, 3, -3, 2, -2, 1, -1):
        partners += [(rp, along_y(step)), (along_z(step), re)]
        if abs(step) < 3:
            partners += [
                (flip_rp(dx, 0, step), flip_re(dl)) for dx, dl in ((1, 1), (1, 0), (0, 1))
            ]
    partners += [
        (flip_rp(dx, dc), flip_re(dl))
        for dc in (0, 1)
        for dx in (1, 0)
        for dl in (1, 0)
        if dx or dc or dl
    ]
    barrier = pltpu.get_barrier_semaphore()
    for to_rp, to_re in partners:
        pl.semaphore_signal(
            barrier, inc=1, device_id={"rp": to_rp, "re": to_re}, device_id_type=MESH
        )

    for number, (name, src, dst) in enumerate(
        (
            ("plat", plat_hbm, plat_ref),
            ("pdeg", pdeg_hbm, pdeg_ref),
            ("qvec", qvec_hbm, qvec_ref),
            ("elat", elat_hbm, elat_ref),
            ("edeg", edeg_hbm, edeg_ref),
            ("kvec", kvec_hbm, kvec_ref),
            ("phonon", phonon_hbm, phonon_ref),
            ("rot", rot_hbm, rot_ref),
            ("band", band_hbm, band_ref),
            ("shift", shift_hbm, shift_ref),
        )
    ):
        load(name, src, dst, 4 + number)

    loaded("w0", "w1", "w2", "w3")
    cells = jnp.concatenate([w_ref[e].astype(F32) for e in range(4)], axis=0)
    for mc in range(4):
        w_both[mc * 16 : mc * 16 + 16, :] = jnp.concatenate(
            [cells[:, mc * ROW : (mc + 1) * ROW], jnp.zeros((16, LANES - ROW), F32)], axis=1
        ).astype(BF)

    loaded("plat", "pdeg", "qvec")
    r_of_lane = jnp.where(iota((4, 128), 0) == (iota((4, 128), 1) & 3), 1.0, 0.0).astype(F32)
    lattice = lax.dot_general(
        plat_ref[...].astype(F32).astype(BF),
        r_of_lane.astype(BF),
        (((0,), (0,)), ((), ())),
        preferred_element_type=F32,
    )
    p_angle = full_turn * outer(qvec_ref[...], lattice)
    p_weight = 1.0 / mm(pdeg_ref[...].astype(F32).astype(BF), r_of_lane.astype(BF))
    cosw[...] = (jnp.cos(p_angle) * p_weight).astype(BF)
    sinw[...] = (jnp.sin(p_angle) * p_weight).astype(BF)
    row = iota((256, 128), 0)
    lane = iota((256, 128), 1)
    same = ((row >> 3) & 1 == (lane >> 5) & 1) & (row & 3 == (lane >> 2) & 3)
    to_imag = (row >> 2) & 1
    of_imag = (lane >> 4) & 1
    pick_cos = same & (to_imag == of_imag)
    pick_sin = same & (to_imag != of_imag)
    sign = jnp.where(to_imag == 1, 1.0, -1.0).astype(F32)
    q_row = iota((256, 32), 0)
    q_lane = iota((256, 32), 1)

    def phases_for(which_core, lanes):
        spread = jnp.where((q_row >> 4) * 2 + which_core == q_lane, 1.0, 0.0).astype(BF)
        cos_part = mm(spread, cosw[...])
        sin_part = mm(spread, sinw[...])
        return jnp.where(
            pick_cos & lanes, cos_part, jnp.where(pick_sin & lanes, sign * sin_part, 0.0)
        ).astype(BF)

    lhs_out[...] = phases_for(1 - core, lane >= 64)

    pl.semaphore_wait(barrier, len(partners))

    sib = flip_rp(0, 1)
    core_copies = [
        remote(
            w_both.at[0:64], w_both.at[64:128], core_s.at[0], core_r.at[0], sib, re
        )
    ]

    core_copies.append(remote(lhs_out, lhs_sib, core_s.at[1], core_r.at[1], sib, re))
    lhs_own[...] = phases_for(core, lane < 64)
    for copy in core_copies:
        copy.wait_recv()
    lhs_own[...] += lhs_sib[...]

    def lhs_of(z_to, sub):
        hi = (1 - x_hi) if sub == 0 else x_hi
        block = ((z_to + 8) % 8) * 2 + hi
        return lhs_own[pl.ds(pl.multiple_of(block * 16, 16), 16), :]

    outer_lhs = jnp.concatenate([lhs_of(z + s, sub) for s in (4, 3, -3) for sub in (0, 1)], axis=0)
    for start, end in LANE_TILES:
        block = mm(outer_lhs, w_both[:, start:end]).astype(BF)
        for sub in (0, 1):
            s_opp[sub, :, start:end] = block[sub * 16 : sub * 16 + 16]
            s_far[0, sub, :, start:end] = block[32 + sub * 16 : 48 + sub * 16]
            s_far[1, sub, :, start:end] = block[64 + sub * 16 : 80 + sub * 16]
    far = {}
    opp = {}
    for sub in (0, 1):
        toward = 2 if sub == 0 else -2
        opp[sub] = remote(
            s_opp.at[sub], l_opp.at[sub], opp_s.at[sub], opp_r.at[sub], along_z(toward), re
        )
        for side, step in ((0, 1), (1, -1)):
            far[side, sub] = remote(
                s_far.at[side, sub],
                l_far.at[side, sub],
                far_s.at[side, sub],
                far_r.at[side, sub],
                along_z(step),
                re,
            )
    inner_lhs = jnp.concatenate(
        [lhs_of(z + s, sub) for s in (0, 1, -1, 2, -2) for sub in (0, 1)], axis=0
    )
    for start, end in LANE_TILES:
        part[:, start:end] = mm(inner_lhs, w_both[:, start:end])

    def piece_of(place, dx, dl):
        first_row = place * 32 + (1 - dx) * 16 + ((x_lo + dl) % 2) * 8
        rows = part[pl.ds(pl.multiple_of(first_row, 8), 8), :]
        end = jnp.concatenate([rows[:, HALF:], jnp.zeros((8, 2 * HALF - LANES), F32)], axis=1)
        return jnp.concatenate([rows[:, 0:HALF], end], axis=0).astype(BF)

    pieces = {}

    def send_piece(place, step, dx, dl):
        s_piece[dl, dx, place] = piece_of(place, dx, dl)
        pieces[dl, dx, place] = remote(
            s_piece.at[dl, dx, place],
            l_piece.at[dl, dx, place],
            piece_s.at[dl, dx, place],
            piece_r.at[dl, dx, place],
            flip_rp(dx, 0, step),
            flip_re(dl),
        )

    for dx, dl in ((1, 1), (1, 0), (0, 1), (0, 0)):
        for place, step in ((1, 1), (2, -1)):
            send_piece(place, step, dx, dl)
    for dx, dl in ((1, 1), (1, 0), (0, 1)):
        send_piece(0, 0, dx, dl)

    loaded("elat", "edeg", "kvec", "phonon", "rot", "band", "shift")
    e_angle = full_turn * outer(kvec_ref[...], elat_ref[...].astype(F32))
    e_weight = 1.0 / edeg_ref[...].astype(F32)
    high, middle, low = three_parts(band_ref[...])
    rest = jnp.zeros((16, PACK - 415), F32)
    for j in range(8):
        five = slice(j * 5, j * 5 + 5)
        eighth = jnp.concatenate(
            [rot_ref[:, j * 400 : j * 400 + 400], high[:, five], middle[:, five], low[:, five], rest],
            axis=1,
        )
        for v in range(4):
            pack_f[v, pl.ds(j, 16, stride=8), :] = eighth[:, v * 128 : v * 128 + 128]
    for v in range(4):
        pack[0:128, v * 128 : v * 128 + 128] = pack_f[v].astype(BF)
    exact = jnp.concatenate([pack_f[v] for v in range(4)], axis=1)
    kept = pack[0:128, :].astype(F32)
    took = (exact - kept) * (exact + kept)
    left = kept * kept
    took = sum(took[:, t * 40 : t * 40 + 40] for t in range(10)).reshape(16, 8, 40)
    left = sum(left[:, t * 40 : t * 40 + 40] for t in range(10)).reshape(16, 8, 40)
    took, left = jnp.sum(took, axis=1), jnp.sum(left, axis=1)
    short = jnp.where(left > 0.0, took / jnp.where(left > 0.0, left, 1.0), 0.0)
    gap = jnp.zeros((16, 48), F32)
    pack[128:144, :] = jnp.concatenate(
        [jnp.cos(e_angle) * e_weight, jnp.sin(e_angle) * e_weight]
        + [high, high, short, gap[:, 0:8], middle, middle, gap, low, low, gap],
        axis=1,
    ).astype(BF)
    pack_copy = remote(pack, packs.at[x_lo], pack_s, pack_r, rp, flip_re(1))

    for d in range(16):
        points_ref[d : d + 1, :] = shift_ref[:, d * 16 : d * 16 + 16]
    points = points_ref[...]
    mine = (points >> 4) == re
    inner = points & 15
    smaller = jnp.min(jnp.where(mine, inner, 99), axis=1, keepdims=True)
    larger = jnp.max(jnp.where(mine, inner, -1), axis=1, keepdims=True)
    both = jnp.where(iota((16, 128), 1) == 0, smaller, larger).astype(F32).astype(BF)
    spread16 = jnp.where((iota((256, 16), 0) >> 4) == iota((256, 16), 1), 1.0, 0.0).astype(BF)
    both_rows = mm(spread16, both)
    slot = (iota((256, 1), 0) >> 3) & 1
    chosen = jnp.where(slot == 0, both_rows[:, 0:1], both_rows[:, 1:2])
    take = ((lane >> 3).astype(F32) == chosen) & ((lane & 7) == (row & 7))
    take = jnp.where(take, 1.0, 0.0).astype(BF)
    u_out[...] = mm(take, pack[0:128, :]).astype(BF).reshape(8, 2, 16, PACK)
    u_copies = []
    for step in (1, 7, 2, 6, 3, 5, 4):
        u_copies.append(
            remote(
                u_out.at[(y + step) % 8],
                u_in.at[x_lo, y],
                u_s.at[step],
                u_r.at[step],
                rp,
                along_y(step),
            )
        )
    packs[x_lo] = pack[...]
    u_in[x_lo, y] = u_out[y]

    for sub in (0, 1):
        for side, step in ((0, 1), (1, -1)):
            far[side, sub].wait_recv()
            more = l_far[side, sub].astype(F32)
            if side == sub:
                opp[sub].wait_recv()
                more = more + l_opp[sub].astype(F32)
            first_row = (3 + side) * 32 + sub * 16
            part[first_row : first_row + 16, :] += more
            for dl in (1, 0):
                send_piece(3 + side, 2 * step, 1 - sub, dl)

    def swap_halves(rows):
        cut = rows.reshape(16, 8, PACK)
        return jnp.concatenate([cut[:, 4:8], cut[:, 0:4]], axis=1).reshape(128, PACK)

    def rotations_here():
        pack_copy.wait_recv()
        blank = jnp.zeros((128, 48), F32)
        for b in (0, 1):
            rows = packs[b, 0:128, :].astype(F32)
            swapped = swap_halves(rows)
            rows = rows * jnp.where((iota((128, 1), 0) >> 2) & 1 == 1, -1.0, 1.0)
            for t in range(10):
                cut = slice(t * 40, t * 40 + 40)
                spot = pl.ds(b * 1280 + t, 128, stride=10)
                turn_a[spot, :] = jnp.concatenate([rows[:, cut], swapped[:, cut], blank], axis=1)
                turn_b[spot, :] = jnp.concatenate([swapped[:, cut], -rows[:, cut], blank], axis=1)
            tail = packs[b, 128:144, :].astype(F32)
            energy_row[b * 16 : b * 16 + 16, :] = (
                tail[:, 128:256] + tail[:, 256:384] + tail[:, 384:512]
            )
            gain = 1.0 + tail[:, 208:248]
            length_row[b * 16 : b * 16 + 16, :] = jnp.concatenate(
                [gain, gain, jnp.zeros((16, 48), F32)], axis=1
            )

        def some(group, carry):
            for i in [group * 8 + member for member in range(8)]:
                spot = pl.ds(pl.multiple_of(i * 80, 8), 80)
                both = [turn_a[spot, :], turn_b[spot, :]]
                right_rot[i] = jnp.concatenate(both, axis=1).astype(BF)
            return carry

        lax.fori_loop(0, 4, some, 0)

    def rotations_there():
        u_swap.wait_recv()
        blank = jnp.zeros((128, 88), F32)
        for b in (0, 1):
            block = points_ref[pl.ds(y * 2 + b, 1), :]
            spot = iota((128, 16), 0) >> 3 == iota((128, 16), 1)
            wide = jnp.broadcast_to(block, (128, 16))
            target = jnp.sum(jnp.where(spot, wide, 0), axis=1, keepdims=True)
            before = ((wide >> 4) == (target >> 4)) & (wide < target)
            second = jnp.max(jnp.where(before, 1, 0), axis=1, keepdims=True)
            source = ((target >> 4) & 1) * 128 + (target >> 5) * 16 + second * 8
            source = source + (iota((128, 1), 0) & 7)
            order = jnp.where(iota((128, 256), 1) == source, 1.0, 0.0).astype(BF)
            rows = mm(order, u_in[:, :, b].reshape(256, PACK))
            for t in range(10):
                turn_a[pl.ds(b * 1280 + t, 128, stride=10), :] = jnp.concatenate(
                    [rows[:, t * 40 : t * 40 + 40], blank], axis=1
                )
            for t in range(5):
                energy = (
                    rows[:, 400 + t : 401 + t]
                    + rows[:, 405 + t : 406 + t]
                    + rows[:, 410 + t : 411 + t]
                )
                energy_col[pl.ds(b * 640 + t, 128, stride=5), :] = jnp.broadcast_to(
                    energy, (128, 128)
                )

        def some(group, carry):
            indices = [group * 8 + member for member in range(8)]
            spots = [pl.ds(pl.multiple_of(i * 80, 8), 80) for i in indices]
            turned = [jnp.transpose(turn_a[spot, :])[0:48, :].astype(BF) for spot in spots]
            for i, block in zip(indices, turned, strict=True):
                left_rot[i, :, 0:80] = block
            return carry

        lax.fori_loop(0, 4, some, 0)

    def weights():
        omega = jnp.where(x_lo == 0, phonon_ref[0:1, 0:1], phonon_ref[0:1, 1:2])
        bose = 1.0 / (jnp.exp(omega / thermal) - 1.0)
        scale = (math.pi / 32.0) * (broadening / math.pi) / (2.0 * omega)

        wide = broadening * broadening

        def some(group, carry):
            spots = [pl.ds(pl.multiple_of((group * 8 + i) * 40, 8), 40) for i in range(8)]
            rows = energy_row[pl.ds(pl.multiple_of(group * 8, 8), 8), :]
            gains = scale * length_row[pl.ds(pl.multiple_of(group * 8, 8), 8), :]
            found = []
            for i, spot in enumerate(spots):
                there = energy_col[spot, :]
                filling = 1.0 / (1.0 + jnp.exp(there / thermal))
                spacing = rows[i : i + 1, :] - there
                plus = spacing + omega
                minus = spacing - omega
                found.append(
                    gains[i : i + 1, :]
                    * (
                        (bose + filling) / (plus * plus + wide)
                        + (bose + 1.0 - filling) / (minus * minus + wide)
                    )
                )
            for spot, value in zip(spots, found, strict=True):
                weight[spot, :] = value
            return carry

        lax.fori_loop(0, 4, some, 0)

    def electron_phases():
        lane4 = iota((128, 128), 1)
        place = lane4 >> 4
        ahead = (place + 1) >> 1
        source = (y + 8 + jnp.where(place & 1 == 1, ahead, -ahead)) & 7
        e_of_lane = (source * 2 + ((x_lo + (lane4 >> 3)) & 1)) * 4 + (lane4 & 3)
        row4 = iota((128, 128), 0)
        match = (row4 & 63) == e_of_lane
        sine = row4 >> 6
        imag = (lane4 >> 2) & 1
        to_real = jnp.where(match & (sine == imag), jnp.where(sine == 1, -1.0, 1.0), 0.0)
        to_im = jnp.where(match & (sine != imag), 1.0, 0.0)
        for b in (0, 1):
            table = packs[b, 128:144, 0:128]
            mix[b * 16 : b * 16 + 16, :] = mm(table, to_real.astype(BF)).astype(BF)
            mix[32 + b * 16 : 48 + b * 16, :] = mm(table, to_im.astype(BF)).astype(BF)

    rotations_here()
    electron_phases()

    for copy in u_copies:
        copy.wait_recv()
    u_swap = remote(u_in.at[x_lo], u_in.at[x_lo], swap_s, swap_r, rp, flip_re(1))
    def add_pieces(dl, places, added):
        for dx in (0, 1):
            for place in places:
                if (dl, dx, place) not in pieces:
                    continue
                pieces[dl, dx, place].wait_recv()
                piece = l_piece[dl, dx, place].astype(F32)
                added = piece if added is None else added + piece
        return added

    nearer = [add_pieces(dl, (0, 1, 2), None) for dl in (0, 1)]
    blocks = []
    for dl in (0, 1):
        added = add_pieces(dl, (3, 4), nearer[dl])
        block = jnp.concatenate([added[0:8], added[8:16, 0 : LANES - HALF]], axis=1)
        if dl == 0:
            block = block + part[pl.ds(pl.multiple_of(16 + x_lo * 8, 8), 8), :]
        blocks.append(block)
    waves[0] = jnp.concatenate(blocks, axis=0).astype(BF)

    first = {}
    for place, step in ((4, 2), (3, -2), (2, 1), (1, -1)):
        first[place] = remote(
            waves.at[0], waves.at[place], y1_s.at[place], y1_r.at[place], rp, along_y(step)
        )
    lower = pl.ds(0, HALF)
    upper = pl.ds(HALF, LANES - HALF)
    later = []
    for number, (place, lanes, step) in enumerate(((4, lower, 1), (3, upper, -1))):
        first[place].wait_recv()
        later.append(
            remote(
                waves.at[place, :, lanes],
                waves.at[7, :, lanes],
                y2_s.at[number],
                y2_r.at[number],
                rp,
                along_y(2 * step),
            )
        )
    for number, (place, to, step) in enumerate(((4, 6, 1), (3, 5, -1))):
        later.append(
            remote(
                waves.at[place],
                waves.at[to],
                y2_s.at[2 + number],
                y2_r.at[2 + number],
                rp,
                along_y(step),
            )
        )
    rotations_there()
    weights()
    first[2].wait_recv()
    first[1].wait_recv()
    points_c = mm(mix[:, 0:80], waves[0:5].reshape(80, LANES))
    for copy in later:
        copy.wait_recv()
    points_c = points_c + mm(mix[:, 80:128], waves[5:8].reshape(48, LANES))

    for a in range(40):
        cut = slice(a * 40, a * 40 + 40)
        coupling[pl.ds(a, 32, stride=40), :] = jnp.concatenate(
            [points_c[0:32, cut], points_c[32:64, cut], jnp.zeros((32, 48), F32)], axis=1
        )

    def some_points(group, carry):
        indices = [group * 16 + i for i in range(16)]
        spots = [pl.ds(pl.multiple_of(i * 40, 8), 40) for i in indices]
        turned = [
            mm(coupling[spot, 0:80].astype(BF), right_rot[i])
            for i, spot in zip(indices, spots, strict=True)
        ]
        stacked = [
            jnp.concatenate([t[:, 0:80], t[:, 128:208]], axis=0).astype(BF) for t in turned
        ]
        final = [
            mm(left_rot[i, 0:40, 0:80], s) for i, s in zip(indices, stacked, strict=True)
        ]
        sums = [
            jnp.sum(f * f * weight[spot, 0:80], axis=0, keepdims=True)
            for f, spot in zip(final, spots, strict=True)
        ]
        rates[pl.ds(pl.multiple_of(group * 16, 8), 16), 0:80] = jnp.concatenate(sums, axis=0)
        return carry

    rates[...] = jnp.zeros((32, 128), F32)
    c_copies = []
    for dl in (0, 1):
        b = (x_lo + dl) % 2
        some_points(b, 0)
        rows = rates[pl.ds(pl.multiple_of(b * 16, 16), 16), :]
        rows = rows[:, 0:40] + rows[:, 40:80]
        rates_b[b] = jnp.concatenate([rows[0:8], rows[8:16], jnp.zeros((8, 48), F32)], axis=1)
        for dx in (1, 0):
            for dc in (1, 0):
                spot = dx * 4 + dc * 2 + dl
                if spot == 0:
                    continue
                copy = remote(
                    rates_b.at[b],
                    land_c.at[spot],
                    rc_s.at[spot],
                    rc_r.at[spot],
                    flip_rp(dx, dc),
                    flip_re(dl),
                )
                c_copies.append((spot, copy))
    summed = rates_b[x_lo]
    for spot, copy in reversed(c_copies):
        copy.wait_recv()
        summed = summed + land_c[spot]
    rates_z[...] = summed
    z_copies = []
    for step in (4, 3, 5, 2, 6, 1, 7):
        copy = remote(
            rates_z, land_z.at[step], rz_s.at[step], rz_r.at[step], along_z(step), re
        )
        z_copies.append((step, copy))
    for step, copy in reversed(z_copies):
        copy.wait_recv()
        summed = summed + land_z[step]
    out_ref[0:8, :] = summed[:, 0:40]
    out_ref[8:16, :] = summed[:, 40:80]

    for copy in started:
        copy.wait_send()


def per_device(
    wannier_coupling,
    phonon_lattice,
    phonon_degeneracy,
    electron_lattice,
    electron_degeneracy,
    phonon_wavevectors,
    electron_wavevectors,
    phonon_energies,
    bloch_rotations,
    band_energies,
    shifted_points,
):
    def vm(shape, dtype):
        return pltpu.VMEM(shape, dtype)

    def dma(*shape):
        return pltpu.SemaphoreType.DMA(shape)

    return pl.pallas_call(
        kernel,
        out_shape=pltpu.VMEM((16, 40), F32),
        in_specs=[pl.BlockSpec(memory_space=pl.ANY)] * 11,
        out_specs=pl.BlockSpec(memory_space=pltpu.VMEM),
        scratch_shapes=[
            vm((4, 4, 6400), BF),
            vm((4, 3), jnp.int32),
            vm((1, 4), jnp.int32),
            vm((3, 64), jnp.int32),
            vm((1, 64), jnp.int32),
            vm((3, 32), F32),
            vm((3, 16), F32),
            vm((1, 2), F32),
            vm((16, 3200), F32),
            vm((16, 40), F32),
            vm((1, 256), jnp.int32),
            vm((128, LANES), BF),
            vm((32, 128), BF),
            vm((32, 128), BF),
            vm((256, 128), BF),
            vm((256, 128), BF),
            vm((256, 128), BF),
            vm((16, 16), jnp.int32),
            vm((4, 128, 128), F32),
            vm((144, PACK), BF),
            vm((2, 144, PACK), BF),
            vm((8, 2, 16, PACK), BF),
            vm((2, 8, 2, 16, PACK), BF),
            vm((160, LANES), F32),
            vm((2, 2, 16, LANES), BF),
            vm((2, 2, 16, LANES), BF),
            vm((2, 16, LANES), BF),
            vm((2, 16, LANES), BF),
            vm((2, 2, 5, 16, HALF), BF),
            vm((2, 2, 5, 16, HALF), BF),
            vm((8, 16, LANES), BF),
            vm((64, 128), BF),
            vm((2560, 128), F32),
            vm((2560, 128), F32),
            vm((32, 80, 256), BF),
            vm((32, 48, 128), BF),
            vm((1280, 128), F32),
            vm((32, 128), F32),
            vm((32, 128), F32),
            vm((1280, 128), F32),
            vm((1280, 128), F32),
            vm((32, 128), F32),
            vm((2, 8, 128), F32),
            vm((8, 8, 128), F32),
            vm((8, 128), F32),
            vm((8, 8, 128), F32),
            dma(14),
            dma(2),
            dma(2),
            pltpu.SemaphoreType.DMA,
            pltpu.SemaphoreType.DMA,
            dma(8),
            dma(8),
            dma(2, 2),
            dma(2, 2),
            dma(2),
            dma(2),
            dma(2, 2, 5),
            dma(2, 2, 5),
            pltpu.SemaphoreType.DMA,
            pltpu.SemaphoreType.DMA,
            dma(5),
            dma(5),
            dma(4),
            dma(4),
            dma(8),
            dma(8),
            dma(8),
            dma(8),
        ],
        compiler_params=pltpu.CompilerParams(
            collective_id=0, has_side_effects=True, vmem_limit_bytes=60 * 1024 * 1024
        ),
        cost_estimate=pl.CostEstimate(
            flops=300_000_000, bytes_accessed=2_000_000, transcendentals=200_000
        ),
    )(
        wannier_coupling,
        phonon_lattice,
        phonon_degeneracy.reshape(1, 4),
        electron_lattice.T,
        electron_degeneracy.reshape(1, 64),
        phonon_wavevectors.T,
        electron_wavevectors.T,
        phonon_energies,
        bloch_rotations,
        band_energies,
        shifted_points,
    )


def solution(mesh):
    in_specs = (
        P("re", "rp", None),
        P("rp", None),
        P("rp"),
        P(),
        P(),
        P(),
        P("re", None),
        P("rp", None),
        P("re", None),
        P("re", None),
        P("rp", None),
    )
    return jax.shard_map(
        per_device, mesh=mesh, in_specs=in_specs, out_specs=P("re", None), check_vma=False
    )
```
